32 devices in a mesh: rows: 16 (over z, y, x), chan: 2 (over core).
Axes of the slice: x: 2, y: 2, z: 4, core: 2. Of those that a mesh axis runs over, the one named last changes fastest.
Arguments:
- tokens: bfloat16 [32768, 768], P('rows', 'chan'), may hold values from -6 to 6
- segments: int32 [32, 1024], P('rows'), may hold values from 0 to 7, never falling along the last dimension, each value on 1 to 512 neighbouring positions
- gain_in: float32 [768], P('chan'), may hold values from 0.5 to 1.5
- shift_in: float32 [768], P('chan'), may hold values from -1 to 1
- query_weight: bfloat16 [768, 768], P(None, 'chan'), may hold values from -0.21875 to 0.21875
- key_weight: bfloat16 [768, 768], P(None, 'chan'), may hold values from -0.21875 to 0.21875
- value_weight: bfloat16 [768, 768], P(None, 'chan'), may hold values from -0.21875 to 0.21875
- out_weight: bfloat16 [768, 768], P('chan'), may hold values from -1.75 to 1.75
- gain_mid: float32 [768], P('chan'), may hold values from 0.5 to 1.5
- shift_mid: float32 [768], P('chan'), may hold values from -1 to 1
- up_weight: bfloat16 [768, 3072], P(None, 'chan'), may hold values from -0.25259074 to 0.25259074
- down_weight: bfloat16 [3072, 768], P('chan'), may hold values from -0.109375 to 0.109375
- pair_bias: float32 [1024, 1024], replicated, may hold values from -4 to 4
- out_grad: bfloat16 [32768, 768], P('rows', 'chan'), may hold values from -6 to 6
Outputs:
- block_out: bfloat16 [32768, 768], P('rows', 'chan')
- tokens_grad: float32 [32768, 768], P('rows', 'chan')
- gain_in_grad: float32 [768], P('chan')
- shift_in_grad: float32 [768], P('chan')
- query_weight_grad: float32 [768, 768], P('rows', 'chan')
- key_weight_grad: float32 [768, 768], P('rows', 'chan')
- value_weight_grad: float32 [768, 768], P('rows', 'chan')
- out_weight_grad: float32 [768, 768], P('chan', 'rows')
- gain_mid_grad: float32 [768], P('chan')
- shift_mid_grad: float32 [768], P('chan')
- up_weight_grad: float32 [768, 3072], P('rows', 'chan')
- down_weight_grad: float32 [3072, 768], P('chan', 'rows')
- pair_bias_grad: float32 [1024, 1024], P('rows', 'chan')
The draws below stay inside these ranges and needn't reach their ends.
Inputs may be any that keep to these rules, and one draw needn't show every extreme that they name: `segments`: segment numbers never fall along a row of 1024 tokens; no document holds more than 512 tokens.
All inputs are finite; a program needn't handle non-finite values.
Results may differ from the reference program's by a relative error of at most 0.017.
Values may be sent and summed in bfloat16 or wider, within the bound.
A program may use at most 192 MiB of HBM per device.

```python
import math
import jax
import jax.numpy as jnp
import numpy as np
from jax import lax

D = 768
FF = 3072
L = 1024
WIN = 256
DOCS = 8
SEQ_DEV = 2
SEQS = 32
TOKENS = 32768
N_CHAN = 2


def draw_up_weight(key, part):
    key = jax.random.fold_in(key, 7)
    entry_key, column_key = jax.random.split(key)
    entries = jax.random.truncated_normal(entry_key, -4.0, 4.0, (D, FF), jnp.float32)
    column_mean = 0.6 * jax.random.truncated_normal(column_key, -4.0, 4.0, (1, FF), jnp.float32)
    return ((entries + column_mean) * D ** (-0.5)).astype(jnp.bfloat16)


def raised(drawn, key, source, target, parts, factor):
    def block_of(position):
        return (jnp.arange(drawn.shape[position]) // (drawn.shape[position] // parts)).reshape((-1,) + (1,) * (drawn.ndim - 1 - position))

    first = jax.random.permutation(key, parts)[block_of(target)]
    second = (block_of(target) + parts // 2) % parts
    return jnp.where((block_of(source) == first) | (block_of(source) == second), factor * drawn, drawn)


def level_of(rng, extent, cuts, low, top_value):
    level, own = 1.0, jax.random.fold_in(rng, 6)
    for position, shards_of in cuts:
        steps = jnp.exp(jax.random.uniform(jax.random.fold_in(own, position), (shards_of,), jnp.float32, low / len(cuts), top_value / len(cuts)))
        level = level * jnp.repeat(steps, extent[position] // shards_of).reshape([-1 if axis == position else 1 for axis in range(len(extent))])
    return level


def length_profile(amount, total, limit, slope):
    portions = [(1 << 20) // math.isqrt(standing ** slope) + 1 for standing in range(2, amount + 1)]
    rest, given = total - limit - (amount - 1), [1] * (amount - 1)
    while rest > 0:
        movable = [i for i in range(amount - 1) if given[i] < limit]
        mass, budget = sum([portions[i] for i in movable]), rest
        for i in movable:
            addition = min(limit - given[i], max(1, budget * portions[i] // mass), rest)
            given[i] = given[i] + addition
            rest = rest - addition
    return np.array([limit] + given)


def uneven(stream_key, count, total, bound, lean):
    if count == 2:
        one = jax.random.randint(stream_key, (), max(1, total - bound), min(bound, total - 1) + 1)
        return jnp.stack([one, total - one])
    lengths = jnp.asarray(length_profile(count, total, bound, lean), jnp.int32)
    twos = (count - 1) // 2
    giver, receiver = lengths[1:1 + 2 * twos:2], lengths[2:2 + 2 * twos:2]
    margin = jnp.minimum(giver - 1, bound - receiver)
    moved = jax.random.randint(jax.random.fold_in(stream_key, 1), (twos,), 0, 1 << 20) % (margin + 1)
    lengths = lengths.at[1:1 + 2 * twos:2].set(giver - moved).at[2:2 + 2 * twos:2].set(receiver + moved)
    return lengths[jax.random.permutation(jax.random.fold_in(stream_key, 2), count)]


def gaussian(key, extent, scale, reach, cuts=(), kind=jnp.bfloat16):
    values = jax.random.normal(key, extent, jnp.float32) * scale
    if len(cuts) > 0:
        values = level_of(key, extent, cuts, -0.22, 0.18) * values
    return jnp.clip(values, min=-reach, max=reach).astype(kind)


def bell_draw_with(own_key, shape, deviation, limit, cuts, heavy, dtype=jnp.bfloat16):
    drawn = deviation * jax.random.normal(own_key, shape, jnp.float32)
    if cuts:
        drawn = drawn * level_of(own_key, shape, cuts, -0.22, 0.18)
    return jnp.clip(raised(drawn, jax.random.fold_in(own_key, 3), *heavy), -limit, limit).astype(dtype)


def setup_inputs(seed: int = 0) -> dict:
    seeds = jax.random.split(jax.random.key(seed), 15)
    return {
        "tokens": gaussian(seeds[0], (TOKENS, D), 1.0, 6.0, ((0, 16), (1, 2))),
        "segments": jax.vmap(lambda own: jnp.searchsorted(jnp.cumsum(uneven(own, DOCS, L, L // 2, 0)), jnp.arange(L), side="right"))(jax.random.split(seeds[1], SEQS)).reshape((SEQS, L)).astype(jnp.int32),
        "gain_in": jnp.clip(1.0 + 0.1 * jax.random.normal(seeds[2], (D,), jnp.float32), 0.5, 1.5),
        "shift_in": gaussian(seeds[3], (D,), 0.3, 1.0, ((0, 2),), jnp.float32),
        "query_weight": gaussian(seeds[4], (D, D), D ** -0.5, 0.21875, ((1, 2),)),
        "key_weight": gaussian(seeds[5], (D, D), D ** -0.5, 0.21875, ((1, 2),)),
        "value_weight": gaussian(seeds[6], (D, D), D ** -0.5, 0.21875, ((1, 2),)),
        "out_weight": gaussian(seeds[7], (D, D), (D // 64) ** -0.5, 1.75, ((0, 2),)),
        "gain_mid": jnp.clip(1.0 + 0.1 * jax.random.normal(seeds[8], (D,), jnp.float32), 0.5, 1.5),
        "shift_mid": gaussian(seeds[9], (D,), 0.3, 1.0, ((0, 2),), jnp.float32),
        "up_weight": draw_up_weight(jax.random.fold_in(seeds[14], 71), 0),
        "down_weight": gaussian(seeds[11], (FF, D), FF ** -0.5, 0.109375, ((0, 2),)),
        "pair_bias": gaussian(seeds[12], (L, L), 1.0, 4.0, (), jnp.float32),
        "out_grad": bell_draw_with(seeds[13], (TOKENS, D), 1.0, 6.0, ((0, 16), (1, 2)), (0, 1, 16, 2.0)),
    }


@jax.custom_vjp
def low(v):
    return lax.optimization_barrier(v.astype(jnp.bfloat16)).astype(jnp.float32)

@jax.custom_vjp
def low_back(v):
    return v

def low_keep(v):
    return (low(v), None)

def low_pass(kept, grad):
    return (grad,)

def back_keep(v):
    return (v, None)

def back_low(kept, grad):
    return (low(grad),)
low.defvjp(low_keep, low_pass)
low_back.defvjp(back_keep, back_low)
epsilon = 1e-05
highest = lax.Precision.HIGHEST

def layer_norm(values, gain, shift):
    row_mean = lax.optimization_barrier(jnp.mean(values, axis=-1, keepdims=True))
    centred = values - row_mean
    spread = lax.optimization_barrier(jnp.mean(centred * centred, axis=-1, keepdims=True))
    return centred * lax.rsqrt(spread + epsilon) * gain + shift

def project(left, right):
    return jnp.einsum('atd,de->ate', left, right, precision=highest)

def block_forward(residual, params, segments):
    gain_in, shift_in, query_w, key_w, value_w, out_w, gain_mid, shift_mid, up_w, down_w, pair_bias = params
    half_width = D // N_CHAN
    hidden_width = FF // N_CHAN
    offset = jnp.arange(L)[:, None] - jnp.arange(L)[None, :]
    inside = jnp.abs(offset) < WIN
    window = low(jnp.where(inside, jnp.exp(pair_bias), 1.0))
    same_doc = segments[:, :, None] == segments[:, None, :]
    mix_weights = jnp.where(same_doc, window[None], 0.0)
    normed_in = low(layer_norm(residual, gain_in, shift_in))
    attn_sum = 0.0
    for chan_part in range(N_CHAN):
        columns = slice(chan_part * half_width, (chan_part + 1) * half_width)
        local_in = low_back(normed_in)
        query_act = low_back(project(local_in, query_w[:, columns]))
        key_act = low_back(project(local_in, key_w[:, columns]))
        value_act = low_back(project(local_in, value_w[:, columns]))
        raised_keys = jnp.exp(key_act)
        carried = jnp.concatenate([low(raised_keys * value_act), low(raised_keys)], -1)
        summed = jnp.einsum('atb,abe->ate', mix_weights, carried, precision=highest)
        numerator = low_back(summed[..., :half_width])
        denominator = low_back(summed[..., half_width:])
        mixed_out = low(jax.nn.sigmoid(query_act) * numerator / denominator)
        attn_sum = attn_sum + low(project(mixed_out, out_w[columns, :]))
    middle = residual + low_back(attn_sum)
    normed_mid = low(layer_norm(middle, gain_mid, shift_mid))
    mlp_sum = 0.0
    for chan_part in range(N_CHAN):
        columns = slice(chan_part * hidden_width, (chan_part + 1) * hidden_width)
        local_mid = low_back(normed_mid)
        pre_act = low_back(project(local_mid, up_w[:, columns]))
        hidden = low(jax.nn.gelu(pre_act, approximate=False))
        mlp_sum = mlp_sum + low(project(hidden, down_w[columns, :]))
    return middle + low_back(mlp_sum)

def reference(tokens, segments, gain_in, shift_in, query_weight, key_weight, value_weight, out_weight, gain_mid, shift_mid, up_weight, down_weight, pair_bias, out_grad):
    params = tuple((item.astype(jnp.float32) for item in (gain_in, shift_in, query_weight, key_weight, value_weight, out_weight, gain_mid, shift_mid, up_weight, down_weight, pair_bias)))
    groups = SEQS // SEQ_DEV
    token_groups = tokens.reshape(groups, SEQ_DEV, L, D)
    seg_groups = segments.reshape(groups, SEQ_DEV, L)
    grad_groups = out_grad.reshape(groups, SEQ_DEV, L, D)

    def visit(totals, batch):
        token_block, seg_block, grad_block = batch

        def run_block(residual, weights):
            return block_forward(residual, weights, seg_block)
        result, pullback = jax.vjp(run_block, token_block.astype(jnp.float32), params)
        token_grad, weight_grads = pullback(grad_block.astype(jnp.float32))
        totals = jax.tree.map(jnp.add, totals, weight_grads)
        return (totals, (result.astype(jnp.bfloat16), token_grad))
    start = tuple((jnp.zeros_like(item) for item in params))
    totals, (outputs, token_grads) = lax.scan(visit, start, (token_groups, seg_groups, grad_groups))
    return (outputs.reshape(SEQS * L, D), token_grads.reshape(SEQS * L, D), totals[0], totals[1], totals[2], totals[3], totals[4], totals[5], totals[6], totals[7], totals[8], totals[9], totals[10])
```

```python
import functools

import jax
import jax.numpy as jnp
from jax import lax
from jax.experimental import pallas as pl
from jax.experimental.pallas import tpu as pltpu
from jax.sharding import PartitionSpec as P

MESH = pl.DeviceIdType.MESH
WIN = 256
EPSILON = 1e-05
TILE = 128
COLS = 256
SLOTS = 4
f32 = jnp.float32
bf16 = jnp.bfloat16


def dot(left, right, cl=1, cr=0):
    return lax.dot_general(left, right, (((cl,), (cr,)), ((), ())), preferred_element_type=f32)


def dot_nt(left, right):
    return dot(left, right, 1, 1)


def dot_tn(left, right):
    return dot(left, right, 0, 0)


def gelu_pair(p):
    phi = 0.5 * (1.0 + lax.erf(p * 0.7071067811865476))
    return p * phi, phi + p * (jnp.exp(-0.5 * p * p) * 0.3989422804014327)


def fold_rows(v):
    return jnp.sum(v.reshape(v.shape[0] // 8, 8, v.shape[1]), axis=0)


def block_kernel(T, D, FH, R, fused, names, *all_refs):
    ref = dict(zip(names, all_refs))
    half = D // 2
    blocks = FH // COLS
    nb = R if fused else 16
    nz = nb // 4
    sh, sp = D // nb, T // nb
    r = lax.axis_index("rows")
    c = lax.axis_index("chan")
    o = 1 - c
    mx, my, mz = lax.rem(r, 2), lax.rem(r // 2, 2), r // 4
    dev_c = (r, o)
    dev_x = (r + 1 - 2 * mx, c)
    dev_y = (r + 2 - 4 * my, c)
    dev_z = [(lax.rem(mz + j, nz) * 4 + lax.rem(r, 4), c) for j in range(1, nz)]
    own_half = pl.ds(pl.multiple_of(c * half, TILE), half)
    other_half = pl.ds(pl.multiple_of(o * half, TILE), half)

    XB, OG, HN, G = ref["XB"], ref["OG"], ref["HN"], ref["G"]
    Y, QQ, RT, RZ, T2 = ref["Y"], ref["QQ"], ref["RT"], ref["RZ"], ref["T2"]
    AB, MM, F1, F3, ST = ref["AB"], ref["MM"], ref["F1"], ref["F3"], ref["ST"]
    WQ, WK, WV, WO, WU, WD = ref["WQ"], ref["WK"], ref["WV"], ref["WO"], ref["WU"], ref["WD"]
    SD, SC, NP, NPS, NPR = ref["SD"], ref["SC"], ref["NP"], ref["NPS"], ref["NPR"]
    PS, PR, S, R1, R2, R3 = ref["PS"], ref["PR"], ref["S"], ref["R1"], ref["R2"], ref["R3"]
    NG, NV, NR, NZS = ref["NG"], ref["NV"], ref["NR"], ref["NZS"]
    local_sem, entry_s, entry_r = ref["local_sem"], ref["entry_s"], ref["entry_r"]
    pair_s, pair_r, ring_s, ring_r = ref["pair_s"], ref["pair_r"], ref["ring_s"], ref["ring_r"]
    end_s, end_r, norm_s, norm_r = ref["end_s"], ref["end_r"], ref["norm_s"], ref["norm_r"]

    def remote(src, dst, send, recv, device):
        return pltpu.make_async_remote_copy(
            src_ref=src, dst_ref=dst, send_sem=send, recv_sem=recv, device_id=device, device_id_type=MESH
        )

    my_rows, other_rows = pl.ds(c * T, T), pl.ds(o * T, T)
    up_rows = pl.ds(pl.multiple_of(c * D, TILE), D)
    down_rows = pl.ds(pl.multiple_of(c * FH, TILE), FH)
    wo_rows = pl.ds(pl.multiple_of(c * half, TILE), half)
    h2 = T // 2
    plan = [
        ("pair_bias", ref["pair_bias"].at[0:h2, 0:D], F3.at[0:h2, :], None),
        ("pair_bias2", ref["pair_bias"].at[h2:T, T - D : T], F3.at[h2:T, :], None),
        ("tokens", ref["tokens"].at[my_rows, :], XB.at[:, own_half], ref["tokens"].at[other_rows, :]),
        ("wq", ref["wq"], WQ.at[:, own_half], ref["wq"]),
        ("wk", ref["wk"], WK.at[:, own_half], ref["wk"]),
        ("wv", ref["wv"], WV.at[:, own_half], ref["wv"]),
        ("wo", ref["wo"], WO.at[wo_rows, :], ref["wo"]),
        ("og", ref["out_grad"].at[my_rows, :], OG.at[:, own_half], ref["out_grad"].at[other_rows, :]),
        ("wu", ref["wu"], WU.at[up_rows, :], ref["wu"]),
        ("wd", ref["wd"], WD.at[down_rows, :], ref["wd"]),
    ]
    if fused:
        pair_rows = pl.ds(pl.multiple_of(r * sp, 8), sp)
        pair_cols = pl.ds(pl.multiple_of(c * (T // 2), TILE), T // 2)
        plan.append(("pbo", ref["pair_bias"].at[pair_rows, pair_cols], ref["PBO"], None))
    local, cross = {}, {}
    for i, (name, src, dst, away) in enumerate(plan):
        local[name] = pltpu.make_async_copy(src, dst, local_sem.at[i])
        local[name].start()
        if away is not None:
            cross[name] = remote(away, dst, entry_s.at[i], entry_r.at[i], dev_c)
    cross["norms"] = remote(NPS, NPR, entry_s.at[len(plan)], entry_r.at[len(plan)], dev_c)

    NPS[...] = jnp.zeros(NPS.shape, f32)
    for i, name in enumerate(("gi", "si", "gm", "sm")):
        NPS[i : i + 1, :] = ref[name][...]
    barrier = pltpu.get_barrier_semaphore()
    greeted = [dev_c] + ([dev_x, dev_y] + dev_z if fused else [])
    for device in greeted:
        pl.semaphore_signal(barrier, inc=1, device_id=device, device_id_type=MESH)
    pl.semaphore_wait(barrier, len(greeted))
    for name in ("norms", "tokens", "wq", "wk", "wv"):
        cross[name].start()

    def ready(*chosen):
        for name in chosen:
            if name in local:
                local[name].wait()
            if name in cross:
                cross[name].wait()

    seg = ref["segments"][pl.ds(c, 1), :].astype(f32)
    SC[...] = jnp.broadcast_to(seg, (TILE, T)).T
    ready("pair_bias", "pair_bias2")
    row_id = lax.broadcasted_iota(jnp.int32, (TILE, TILE), 0)
    col_id = lax.broadcasted_iota(jnp.int32, (TILE, TILE), 1)
    for a in range(T // TILE):
        rows = slice(a * TILE, (a + 1) * TILE)
        shift = 0 if a * TILE < h2 else T - D
        for b in range(T // TILE):
            cols = slice(b * TILE, (b + 1) * TILE)
            far = abs(a - b) * TILE
            if far - TILE + 1 >= T // 2:
                MM[rows, cols] = jnp.zeros((TILE, TILE), bf16)
                continue
            same = SC[rows, :] == seg[:, cols]
            if far - TILE + 1 >= WIN:
                weight = jnp.ones((TILE, TILE), f32)
            else:
                weight = jnp.exp(F3[rows, b * TILE - shift : (b + 1) * TILE - shift])
                if far + TILE - 1 >= WIN:
                    inside = jnp.abs(row_id - col_id + (a - b) * TILE) < WIN
                    weight = jnp.where(inside, weight, 1.0)
            MM[rows, cols] = jnp.where(same, weight, 0.0).astype(bf16)

    ready("norms")
    for i in range(4):
        NP[i : i + 1, own_half] = NPS[i : i + 1, :]
        NP[i : i + 1, other_half] = NPR[i : i + 1, :]
    step_rows = 256
    ready("tokens")

    def norm_in(i, carry):
        rows = pl.ds(i * step_rows, step_rows)
        x = XB[rows, :].astype(f32)
        centred = x - jnp.mean(x, axis=1, keepdims=True)
        inv = lax.rsqrt(jnp.mean(centred * centred, axis=1, keepdims=True) + EPSILON)
        t = centred * inv
        F1[rows, :] = x
        XB[rows, :] = t.astype(bf16)
        HN[rows, :] = (t * NP[0:1, :] + NP[1:2, :]).astype(bf16)
        ST[rows, 0:1] = inv
        return carry

    lax.fori_loop(0, T // step_rows, norm_in, 0)
    for name in ("wo", "og", "wu", "wd"):
        cross[name].start()
    ready("wq", "wk", "wv")

    for j in range(D // COLS):
        cols = slice(j * COLS, (j + 1) * COLS)
        late = slice(D + j * COLS, D + (j + 1) * COLS)
        e = jnp.exp(dot(HN[...], WK[:, cols]))
        a = (e * dot(HN[...], WV[:, cols])).astype(bf16)
        AB[:, cols] = a
        AB[:, late] = e.astype(bf16)
        gate = jax.nn.sigmoid(dot(HN[...], WQ[:, cols]))
        inv = 1.0 / dot(MM[...], AB[:, late])
        ratio = dot(MM[...], AB[:, cols]) * inv
        y = gate * ratio
        Y[:, cols] = y.astype(bf16)
        QQ[:, cols] = (y * (1.0 - gate)).astype(bf16)
        RT[:, cols] = ratio.astype(bf16)
        RZ[:, cols] = (gate * inv).astype(bf16)

    ready("wo")
    F1[...] += dot(Y[...], WO[...])

    def norm_mid(i, carry):
        rows = pl.ds(i * step_rows, step_rows)
        x = F1[rows, :]
        centred = x - jnp.mean(x, axis=1, keepdims=True)
        inv = lax.rsqrt(jnp.mean(centred * centred, axis=1, keepdims=True) + EPSILON)
        t = centred * inv
        T2[rows, :] = t.astype(bf16)
        G[rows, :] = (t * NP[2:3, :] + NP[3:4, :]).astype(bf16)
        ST[rows, 1:2] = inv
        F3[rows, :] = jnp.zeros((step_rows, D), f32)
        return carry

    lax.fori_loop(0, T // step_rows, norm_mid, 0)
    ready("og", "wu", "wd", "pbo")

    order = {
        0: lambda b: b if not fused else ((b % 2) * 2 + (b // 2) % 2) * nz + b // 4,
        1: lambda b: b if not fused else (((b // 2) % 2) * 2 + b % 2) * nz + b // 4,
    }
    route = {0: (mx, dev_x, my, dev_y), 1: (my, dev_y, mx, dev_x)}

    def form(k, part, height, own, at=0):
        slot, pslot = k % SLOTS, k % 2
        width = own.shape[1]
        for b in range(nb):
            rows = slice(b * height, (b + 1) * height)
            total = own[rows, :].astype(f32) + PR[pslot, part, rows, at : at + width].astype(f32)
            S[slot, part, order[part](b), 0:height, at : at + width] = total.astype(bf16)

    def first(k, part, height):
        slot = k % SLOTS
        b1, d1, _, _ = route[part]
        return remote(
            S.at[slot, part, pl.ds((1 - b1) * 2 * nz, 2 * nz), pl.ds(0, height), :],
            R1.at[slot, part, :, pl.ds(0, height), :],
            ring_s.at[slot, part], ring_r.at[slot, part], d1,
        )

    def second(k, part, height):
        slot = k % SLOTS
        b1, _, b2, d2 = route[part]
        return remote(
            S.at[slot, part, pl.ds(b1 * 2 * nz + (1 - b2) * nz, nz), pl.ds(0, height), :],
            R2.at[slot, part, :, pl.ds(0, height), :],
            ring_s.at[slot, 2 + part], ring_r.at[slot, 2 + part], d2,
        )

    def third(k, part, height):
        slot = k % SLOTS
        b1, _, b2, _ = route[part]
        copies = []
        for j in range(1, nz):
            sem = 4 + part * (nz - 1) + j - 1
            copies.append(remote(
                S.at[slot, part, b1 * 2 * nz + b2 * nz + lax.rem(mz + j, nz), pl.ds(0, height), :],
                R3.at[slot, part, j - 1, pl.ds(0, height), :],
                ring_s.at[slot, sem], ring_r.at[slot, sem], dev_z[j - 1],
            ))
        return copies

    def whole(k):
        return pltpu.make_async_copy(S.at[k % SLOTS], ref["GO"].at[k], ring_s.at[k % SLOTS, 0])

    def start_sum(k, height):
        if not fused:
            whole(k).start()
            return
        for part in range(2):
            first(k, part, height).start()

    def after_first(k, height):
        if not fused:
            whole(k).wait()
            return
        slot = k % SLOTS
        for part in range(2):
            b1, _, _, _ = route[part]
            first(k, part, height).wait()
            keep = pl.ds(b1 * 2 * nz, 2 * nz)
            total = S[slot, part, keep, 0:height, :].astype(f32) + R1[slot, part, :, 0:height, :].astype(f32)
            S[slot, part, keep, 0:height, :] = total.astype(bf16)
            second(k, part, height).start()

    def after_second(k, height):
        if not fused:
            return
        slot = k % SLOTS
        for part in range(2):
            b1, _, b2, _ = route[part]
            second(k, part, height).wait()
            keep = pl.ds(b1 * 2 * nz + b2 * nz, nz)
            total = S[slot, part, keep, 0:height, :].astype(f32) + R2[slot, part, :, 0:height, :].astype(f32)
            S[slot, part, keep, 0:height, :] = total.astype(bf16)
            for copy in third(k, part, height):
                copy.start()

    def after_third(k, height, put):
        if not fused:
            return
        slot = k % SLOTS
        for part in range(2):
            b1, _, b2, _ = route[part]
            for copy in third(k, part, height):
                copy.wait()
            total = S[slot, part, b1 * 2 * nz + b2 * nz + mz, 0:height, :].astype(f32)
            for j in range(nz - 1):
                total = total + R3[slot, part, j, 0:height, :].astype(f32)
            put(k, part, total)

    def upright(v):
        filled = jnp.concatenate([v, jnp.zeros((TILE - v.shape[0], v.shape[1]), f32)], 0)
        return filled.T[:, : v.shape[0]]

    def put_hidden(k, part, total):
        at = pl.ds(pl.multiple_of(k * COLS, COLS), COLS)
        if part == 0:
            ref["o_up"][:, at] = total
        else:
            ref["o_dn"][at, :] = upright(total)

    def hidden_step(owner, i):
        cols = pl.ds(pl.multiple_of(i * COLS, COLS), COLS)
        up_at = pl.ds(pl.multiple_of(owner * D, TILE), D)
        down_at = pl.ds(pl.multiple_of(owner * FH + i * COLS, COLS), COLS)
        s, slope = gelu_pair(dot(G[...], WU[up_at, cols]))
        SD[:, 0:COLS] = s.astype(bf16)
        SD[:, COLS:] = (dot_nt(OG[...], WD[down_at, :]) * slope).astype(bf16)
        F1[...] += dot(SD[:, 0:COLS], WD[down_at, :])
        F3[...] += dot_nt(SD[:, COLS:], WU[up_at, cols])
        return dot_tn(G[...], SD[:, COLS:]), dot_tn(OG[...], SD[:, 0:COLS])

    def pair_copy(k, height):
        slot = k % 2
        return remote(
            PS.at[slot, :, pl.ds(0, height), :], PR.at[slot, :, pl.ds(0, height), :],
            pair_s.at[slot, 0], pair_r.at[slot, 0], dev_c,
        )

    def hidden_block(i, carry):
        slot = lax.rem(i, 2)
        up, down = hidden_step(o, i)
        PS[slot, 0, 0:D, :] = up.astype(bf16)
        PS[slot, 1, 0:D, :] = down.astype(bf16)
        pair_copy(i, D).start()
        up, down = hidden_step(c, i)
        pair_copy(i, D).wait()
        form(i, 0, sh, up)
        form(i, 1, sh, down)
        start_sum(i, sh)
        pl.when(i >= 1)(lambda: after_first(i - 1, sh))
        pl.when(i >= 2)(lambda: after_second(i - 2, sh))
        pl.when(i >= 3)(lambda: after_third(i - 3, sh, put_hidden))
        return carry

    lax.fori_loop(0, blocks, hidden_block, 0)

    def finish_out(i, carry):
        rows = pl.ds(i * step_rows, step_rows)
        G[rows, :] = F1[rows, :].astype(bf16)
        return carry

    lax.fori_loop(0, T // step_rows, finish_out, 0)
    blk_local = pltpu.make_async_copy(G.at[:, own_half], ref["o_blk"].at[my_rows, :], local_sem.at[12])
    blk_cross = remote(G.at[:, other_half], ref["o_blk"].at[my_rows, :], end_s.at[0], end_r.at[0], dev_c)
    blk_local.start()
    blk_cross.start()

    NG[...] = jnp.zeros(NG.shape, f32)

    def norm_mid_back(i, carry):
        rows = pl.ds(i * step_rows, step_rows)
        grad, t = F3[rows, :], T2[rows, :].astype(f32)
        w = grad * NP[2:3, :]
        mean_w = jnp.mean(w, axis=1, keepdims=True)
        mean_wt = jnp.mean(w * t, axis=1, keepdims=True)
        dx = OG[rows, :].astype(f32) + ST[rows, 1:2] * (w - mean_w - t * mean_wt)
        F3[rows, :] = dx
        T2[rows, :] = dx.astype(bf16)
        NG[2] += fold_rows(grad * t)
        NG[3] += fold_rows(grad)
        return carry

    lax.fori_loop(0, T // step_rows, norm_mid_back, 0)
    last = blocks - 1
    after_first(last, sh)
    after_second(last - 1, sh)
    after_third(last - 2, sh, put_hidden)

    NZ = WU
    for j in range(D // COLS):
        cols = slice(j * COLS, (j + 1) * COLS)
        late = slice(D + j * COLS, D + (j + 1) * COLS)
        dm = dot_nt(T2[...], WO[cols, :])
        WD[0:T, cols] = (dm * QQ[:, cols].astype(f32)).astype(bf16)
        dn = dm * RZ[:, cols].astype(f32)
        NZ[0:T, cols] = dn.astype(bf16)
        NZ[0:T, late] = (-dn * RT[:, cols].astype(f32)).astype(bf16)
    OG[0:D, :] = dot_tn(T2[...], Y[...]).astype(bf16)
    QQ[0:D, :] = dot_tn(HN[...], WD[0:T, :]).astype(bf16)

    sources = (OG, QQ, RZ, RT)

    def pieces(part_no):
        found, at = [], part_no * COLS
        while at < (part_no + 1) * COLS:
            source, off = at // half, at % half
            width = min(half - off, (part_no + 1) * COLS - at)
            found.append((source, off, width, at - part_no * COLS))
            at += width
        return found

    def late_copies(k, first_part):
        slot, copies = k % 2, []
        for part in range(2):
            for source, off, width, at in pieces(first_part + part):
                cols = pl.ds(pl.multiple_of(o * half + off, TILE), width)
                copies.append(remote(
                    sources[source].at[pl.ds(0, D), cols], PR.at[slot, part, pl.ds(0, D), pl.ds(at, width)],
                    pair_s.at[slot, 1 + len(copies)], pair_r.at[slot, 1 + len(copies)], dev_c,
                ))
        return copies

    def late_form(k, first_part, copies):
        for copy in copies:
            copy.wait()
        for part in range(2):
            for source, off, width, at in pieces(first_part + part):
                cols = pl.ds(pl.multiple_of(c * half + off, TILE), width)
                form(k, part, sh, sources[source][0:D, cols], at)

    def put_late(first_part):
        def put(k, part, total):
            for source, off, width, at in pieces(first_part + part):
                value = total[:, at : at + width]
                if source == 0:
                    ref["o_wo"][off : off + width, :] = upright(value)
                else:
                    ref[("o_q", "o_k", "o_v")[source - 1]][:, off : off + width] = value
        return put

    k0, k1, k2, k3 = blocks, blocks + 1, blocks + 2, blocks + 3
    sent = late_copies(k0, 0)
    for copy in sent:
        copy.start()

    for j in range(T // COLS):
        cols = slice(j * COLS, (j + 1) * COLS)
        low, high = max(0, (j - 1) * COLS), min(T, (j + 2) * COLS)
        target = PS.at[j // 2, j % 2]
        for start, stop in ((0, low), (high, T)):
            if stop > start:
                target[start:stop, :] = jnp.zeros((stop - start, COLS), bf16)
        grad = dot_nt(NZ[low:high, :], AB[cols, :])
        for t in range(COLS // TILE):
            at = j * COLS + t * TILE
            same = SC[low:high, :] == seg[:, at : at + TILE]
            gap = (
                lax.broadcasted_iota(jnp.int32, (high - low, TILE), 0)
                - lax.broadcasted_iota(jnp.int32, (high - low, TILE), 1)
                + (low - at)
            )
            kept = jnp.where(same & (jnp.abs(gap) < WIN), grad[:, t * TILE : (t + 1) * TILE], 0.0)
            target[low:high, t * TILE : (t + 1) * TILE] = kept.astype(bf16)

    late_form(k0, 0, sent)
    start_sum(k0, sh)
    after_second(last, sh)
    after_third(last - 1, sh, put_hidden)

    def mixer_copy():
        return remote(PS.at[o], PR.at[k1 % 2], pair_s.at[k1 % 2, 0], pair_r.at[k1 % 2, 0], dev_c)

    mixer_copy().start()

    for j in range(D // COLS):
        cols = slice(j * COLS, (j + 1) * COLS)
        late = slice(D + j * COLS, D + (j + 1) * COLS)
        da = dot_tn(MM[...], NZ[0:T, cols])
        db = dot_tn(MM[...], NZ[0:T, late])
        e = AB[:, late].astype(f32)
        WD[T : 2 * T, cols] = (db * e + da * AB[:, cols].astype(f32)).astype(bf16)
        WD[2 * T : 3 * T, cols] = (da * e).astype(bf16)
    RZ[0:D, :] = dot_tn(HN[...], WD[T : 2 * T, :]).astype(bf16)

    mixer_copy().wait()
    for part in range(2):
        form(k1, part, sp, PS.at[c, part][...])
    start_sum(k1, sp)
    after_first(k0, sh)
    after_third(last, sh, put_hidden)

    sent = late_copies(k2, 2)
    for copy in sent:
        copy.start()
    RT[0:D, :] = dot_tn(HN[...], WD[2 * T : 3 * T, :]).astype(bf16)
    late_form(k2, 2, sent)
    start_sum(k2, sh)
    after_first(k1, sp)
    after_second(k0, sh)
    sent = late_copies(k3, 4)
    for copy in sent:
        copy.start()

    for j in range(D // COLS):
        cols = slice(j * COLS, (j + 1) * COLS)
        F1[:, cols] = (
            dot_nt(WD[0:T, :], WQ[cols, :])
            + dot_nt(WD[T : 2 * T, :], WK[cols, :])
            + dot_nt(WD[2 * T : 3 * T, :], WV[cols, :])
        )
    late_form(k3, 4, sent)
    start_sum(k3, sh)

    def norm_in_back(i, carry):
        rows = pl.ds(i * step_rows, step_rows)
        grad, t = F1[rows, :], XB[rows, :].astype(f32)
        w = grad * NP[0:1, :]
        mean_w = jnp.mean(w, axis=1, keepdims=True)
        mean_wt = jnp.mean(w * t, axis=1, keepdims=True)
        F3[rows, :] = F3[rows, :] + ST[rows, 0:1] * (w - mean_w - t * mean_wt)
        NG[0] += fold_rows(grad * t)
        NG[1] += fold_rows(grad)
        return carry

    lax.fori_loop(0, T // step_rows, norm_in_back, 0)
    tok_local = pltpu.make_async_copy(F3.at[:, own_half], ref["o_tok"].at[my_rows, :], local_sem.at[13])
    tok_cross = remote(F3.at[:, other_half], ref["o_tok"].at[my_rows, :], end_s.at[1], end_r.at[1], dev_c)
    tok_local.start()
    tok_cross.start()

    NV[...] = jnp.zeros(NV.shape, f32)
    for i in range(4):
        NV[i : i + 1, :] = jnp.sum(NG[i], axis=0, keepdims=True)
    copy = remote(NV.at[:, other_half], NR.at[0], norm_s.at[0], norm_r.at[0], dev_c)
    copy.start()
    copy.wait()
    NR[1] = NV[:, own_half] + NR[0]
    if fused:
        def put_pair(k, part, total):
            cols = slice(part * COLS, (part + 1) * COLS)
            ref["o_pair"][:, cols] = total * jnp.exp(ref["PBO"][:, cols])

        copy = remote(NR.at[1], NR.at[2], norm_s.at[1], norm_r.at[1], dev_x)
        copy.start()
        after_first(k2, sh)
        after_second(k1, sp)
        after_third(k0, sh, put_late(0))
        copy.wait()
        NR[3] = NR[1] + NR[2]
        copy = remote(NR.at[3], NR.at[4], norm_s.at[2], norm_r.at[2], dev_y)
        copy.start()
        after_first(k3, sh)
        after_second(k2, sh)
        after_third(k1, sp, put_pair)
        copy.wait()
        total = NR[3] + NR[4]
        NZS[mz] = total
        copies = [
            remote(NZS.at[mz], NZS.at[mz], norm_s.at[2 + j], norm_r.at[2 + j], dev_z[j - 1])
            for j in range(1, nz)
        ]
        for copy in copies:
            copy.start()
        after_second(k3, sh)
        after_third(k2, sh, put_late(2))
        for copy in copies:
            copy.wait()
        total = NZS[0]
        for j in range(1, nz):
            total = total + NZS[j]
        for i, name in enumerate(("o_gi", "o_si", "o_gm", "o_sm")):
            ref[name][...] = total[i : i + 1, :]
        after_third(k3, sh, put_late(4))
    else:
        ref["o_norm"][...] = NR[1]
        for k in (k2, k3):
            after_first(k, sh)
    blk_local.wait()
    blk_cross.wait()
    tok_local.wait()
    tok_cross.wait()


def run_block(T, D, FH, R, args):
    half = D // 2
    blocks = FH // COLS
    fused = R % 4 == 0 and (D // R) % 16 == 0 and D % R == 0 and (T // R) % 16 == 0 and T % R == 0
    nb = R if fused else 16
    nz = nb // 4
    sh, sp = D // nb, T // nb
    any_spec, vmem = pl.BlockSpec(memory_space=pl.ANY), pl.BlockSpec(memory_space=pltpu.VMEM)
    inputs = {
        "tokens": any_spec, "segments": vmem, "gi": vmem, "si": vmem, "wq": any_spec, "wk": any_spec,
        "wv": any_spec, "wo": any_spec, "gm": vmem, "sm": vmem, "wu": any_spec, "wd": any_spec,
        "pair_bias": any_spec, "out_grad": any_spec,
    }
    outputs = {"o_blk": (any_spec, (2 * T, half), bf16), "o_tok": (any_spec, (2 * T, half), f32)}
    if fused:
        for name in ("o_gi", "o_si", "o_gm", "o_sm"):
            outputs[name] = (vmem, (1, half), f32)
        for name in ("o_q", "o_k", "o_v"):
            outputs[name] = (vmem, (sh, half), f32)
        outputs["o_wo"] = (vmem, (half, sh), f32)
        outputs["o_up"] = (vmem, (sh, FH), f32)
        outputs["o_dn"] = (vmem, (FH, sh), f32)
        outputs["o_pair"] = (vmem, (sp, T // 2), f32)
    else:
        outputs["o_norm"] = (vmem, (8, half), f32)
        outputs["GO"] = (any_spec, (blocks + 4, 2, nb, sp, COLS), bf16)
    wide = (T, D)
    scratch = {name: pltpu.VMEM(wide, bf16) for name in ("XB", "OG", "HN", "G", "Y", "QQ", "RT", "RZ", "T2")}
    scratch |= {
        "AB": pltpu.VMEM((T, 2 * D), bf16), "MM": pltpu.VMEM((T, T), bf16),
        "F1": pltpu.VMEM(wide, f32), "F3": pltpu.VMEM(wide, f32), "ST": pltpu.VMEM((T, TILE), f32),
        "WQ": pltpu.VMEM((D, D), bf16), "WK": pltpu.VMEM((D, D), bf16), "WV": pltpu.VMEM((D, D), bf16),
        "WO": pltpu.VMEM((D, D), bf16), "WU": pltpu.VMEM((2 * D, FH), bf16), "WD": pltpu.VMEM((2 * FH, D), bf16),
        "SD": pltpu.VMEM((T, 2 * COLS), bf16), "SC": pltpu.VMEM((T, TILE), f32),
        "NP": pltpu.VMEM((8, D), f32), "NPS": pltpu.VMEM((8, half), f32), "NPR": pltpu.VMEM((8, half), f32),
        "PS": pltpu.VMEM((2, 2, T, COLS), bf16), "PR": pltpu.VMEM((2, 2, T, COLS), bf16),
        "S": pltpu.VMEM((SLOTS, 2, nb, sp, COLS), bf16),
        "R1": pltpu.VMEM((SLOTS, 2, 2 * nz, sp, COLS), bf16) if fused else pltpu.VMEM((8, TILE), f32),
        "R2": pltpu.VMEM((SLOTS, 2, nz, sp, COLS), bf16) if fused else pltpu.VMEM((8, TILE), f32),
        "R3": pltpu.VMEM((SLOTS, 2, nz - 1, sp, COLS), bf16) if fused else pltpu.VMEM((8, TILE), f32),
        "NG": pltpu.VMEM((4, 8, D), f32), "NV": pltpu.VMEM((8, D), f32), "NR": pltpu.VMEM((5, 8, half), f32),
        "NZS": pltpu.VMEM((nz, 8, half), f32), "PBO": pltpu.VMEM((sp, T // 2), f32),
        "local_sem": pltpu.SemaphoreType.DMA((16,)),
        "entry_s": pltpu.SemaphoreType.DMA((16,)), "entry_r": pltpu.SemaphoreType.DMA((16,)),
        "pair_s": pltpu.SemaphoreType.DMA((2, 5)), "pair_r": pltpu.SemaphoreType.DMA((2, 5)),
        "ring_s": pltpu.SemaphoreType.DMA((SLOTS, 4 + 2 * nz)), "ring_r": pltpu.SemaphoreType.DMA((SLOTS, 4 + 2 * nz)),
        "end_s": pltpu.SemaphoreType.DMA((2,)), "end_r": pltpu.SemaphoreType.DMA((2,)),
        "norm_s": pltpu.SemaphoreType.DMA((2 + nz,)), "norm_r": pltpu.SemaphoreType.DMA((2 + nz,)),
    }
    names = tuple(inputs) + tuple(outputs) + tuple(scratch)
    results = pl.pallas_call(
        functools.partial(block_kernel, T, D, FH, R, fused, names),
        out_shape=tuple(jax.ShapeDtypeStruct(shape, kind) for _, shape, kind in outputs.values()),
        in_specs=list(inputs.values()),
        out_specs=tuple(spec for spec, _, _ in outputs.values()),
        scratch_shapes=list(scratch.values()),
        compiler_params=pltpu.CompilerParams(
            collective_id=0, has_side_effects=True, vmem_limit_bytes=63 << 20
        ),
    )(*args)
    out = dict(zip(outputs, results))
    if fused:
        return out
    parts = out.pop("GO")
    height = lambda v, rows: v.reshape(nb, sp, v.shape[-1])[:, : rows // nb].reshape(rows, v.shape[-1])
    join = lambda chosen: jnp.concatenate(chosen, 1).astype(f32)
    scatter = lambda v: lax.psum_scatter(v, "rows", scatter_dimension=0, tiled=True)
    out["o_up"] = scatter(join([height(parts[k, 0], D) for k in range(blocks)]))
    out["o_dn"] = scatter(join([height(parts[k, 1], D) for k in range(blocks)])).T
    late = join([height(parts[k, p], D) for k in (blocks, blocks + 2, blocks + 3) for p in range(2)])
    cut = [scatter(late[:, i * half : (i + 1) * half]) for i in range(4)]
    out["o_wo"], out["o_q"], out["o_k"], out["o_v"] = cut[0].T, cut[1], cut[2], cut[3]
    pair = scatter(join([height(parts[blocks + 1, p], T) for p in range(2)]))
    bias = lax.dynamic_slice(
        args[12], (lax.axis_index("rows") * pair.shape[0], lax.axis_index("chan") * (T // 2)), pair.shape
    )
    out["o_pair"] = pair * jnp.exp(bias)
    norms = lax.psum(out["o_norm"], "rows")
    for i, name in enumerate(("o_gi", "o_si", "o_gm", "o_sm")):
        out[name] = norms[i : i + 1]
    return out


def on_device(
    tokens, segments, gain_in, shift_in, query_weight, key_weight, value_weight, out_weight,
    gain_mid, shift_mid, up_weight, down_weight, pair_bias, out_grad,
):
    T = segments.shape[1]
    D, FH = up_weight.shape
    R = lax.axis_size("rows")
    row = lambda v: v.reshape(1, v.shape[0])
    out = run_block(T, D, FH, R, (
        tokens, segments, row(gain_in), row(shift_in), query_weight, key_weight, value_weight, out_weight,
        row(gain_mid), row(shift_mid), up_weight, down_weight, pair_bias, out_grad,
    ))
    flat = lambda name: out[name].reshape(out[name].shape[1])
    return (
        out["o_blk"], out["o_tok"], flat("o_gi"), flat("o_si"), out["o_q"], out["o_k"], out["o_v"], out["o_wo"],
        flat("o_gm"), flat("o_sm"), out["o_up"], out["o_dn"], out["o_pair"],
    )


def solution(mesh):
    split, first, second = P("rows", "chan"), P("chan", None), P(None, "chan")
    return jax.shard_map(
        on_device,
        mesh=mesh,
        in_specs=(
            split, P("rows", None), P("chan"), P("chan"), second, second, second, first,
            P("chan"), P("chan"), second, first, P(), split,
        ),
        out_specs=(
            split, split, P("chan"), P("chan"), split, split, split, P("chan", "rows"),
            P("chan"), P("chan"), split, P("chan", "rows"), split,
        ),
        check_vma=False,
    )
```

```python
import functools

import jax
import jax.numpy as jnp
from jax import lax
from jax.experimental import pallas as pl
from jax.experimental.pallas import tpu as pltpu
from jax.sharding import PartitionSpec as P

MESH = pl.DeviceIdType.MESH
WIN = 256
EPSILON = 1e-05
TILE = 128
COLS = 256
SLOTS = 4
f32 = jnp.float32
bf16 = jnp.bfloat16


def dot(left, right, cl=1, cr=0):
    return lax.dot_general(left, right, (((cl,), (cr,)), ((), ())), preferred_element_type=f32)


def dot_nt(left, right):
    return dot(left, right, 1, 1)


def dot_tn(left, right):
    return dot(left, right, 0, 0)


def gelu_pair(p):
    phi = 0.5 * (1.0 + lax.erf(p * 0.7071067811865476))
    return p * phi, phi + p * (jnp.exp(-0.5 * p * p) * 0.3989422804014327)


def fold_rows(v):
    return jnp.sum(v.reshape(v.shape[0] // 8, 8, v.shape[1]), axis=0)


def block_kernel(T, D, FH, R, fused, names, *all_refs):
    ref = dict(zip(names, all_refs))
    half = D // 2
    blocks = FH // COLS
    nb = R if fused else 16
    nz = nb // 4
    sh, sp = D // nb, T // nb
    r = lax.axis_index("rows")
    c = lax.axis_index("chan")
    o = 1 - c
    mx, my, mz = lax.rem(r, 2), lax.rem(r // 2, 2), r // 4
    dev_c = (r, o)
    dev_x = (r + 1 - 2 * mx, c)
    dev_y = (r + 2 - 4 * my, c)
    dev_z = [(lax.rem(mz + j, nz) * 4 + lax.rem(r, 4), c) for j in range(1, nz)]
    own_half = pl.ds(pl.multiple_of(c * half, TILE), half)
    other_half = pl.ds(pl.multiple_of(o * half, TILE), half)

    XB, OG, HN, G = ref["XB"], ref["OG"], ref["HN"], ref["G"]
    Y, QQ, RT, RZ, T2 = ref["Y"], ref["QQ"], ref["RT"], ref["RZ"], ref["T2"]
    AB, MM, F1, F3, ST = ref["AB"], ref["MM"], ref["F1"], ref["F3"], ref["ST"]
    WQ, WK, WV, WO, WU, WD = ref["WQ"], ref["WK"], ref["WV"], ref["WO"], ref["WU"], ref["WD"]
    SD, SC, NP, NPS, NPR = ref["SD"], ref["SC"], ref["NP"], ref["NPS"], ref["NPR"]
    PS, PR, S, R1, R2, R3 = ref["PS"], ref["PR"], ref["S"], ref["R1"], ref["R2"], ref["R3"]
    NG, NV, NR, NZS = ref["NG"], ref["NV"], ref["NR"], ref["NZS"]
    FIN, fin_sem = ref["FIN"], ref["fin_sem"]
    local_sem, entry_s, entry_r = ref["local_sem"], ref["entry_s"], ref["entry_r"]
    pair_s, pair_r, ring_s, ring_r = ref["pair_s"], ref["pair_r"], ref["ring_s"], ref["ring_r"]
    end_s, end_r, norm_s, norm_r = ref["end_s"], ref["end_r"], ref["norm_s"], ref["norm_r"]

    def remote(src, dst, send, recv, device):
        return pltpu.make_async_remote_copy(
            src_ref=src, dst_ref=dst, send_sem=send, recv_sem=recv, device_id=device, device_id_type=MESH
        )

    my_rows, other_rows = pl.ds(c * T, T), pl.ds(o * T, T)
    up_rows = pl.ds(pl.multiple_of(c * D, TILE), D)
    down_rows = pl.ds(pl.multiple_of(c * FH, TILE), FH)
    wo_rows = pl.ds(pl.multiple_of(c * half, TILE), half)
    h2 = T // 2
    plan = [
        ("pair_bias", ref["pair_bias"].at[0:h2, 0:D], F3.at[0:h2, :], None),
        ("pair_bias2", ref["pair_bias"].at[h2:T, T - D : T], F3.at[h2:T, :], None),
        ("tokens", ref["tokens"].at[my_rows, :], XB.at[:, own_half], ref["tokens"].at[other_rows, :]),
        ("wq", ref["wq"], WQ.at[:, own_half], ref["wq"]),
        ("wk", ref["wk"], WK.at[:, own_half], ref["wk"]),
        ("wv", ref["wv"], WV.at[:, own_half], ref["wv"]),
        ("wo", ref["wo"], WO.at[wo_rows, :], ref["wo"]),
        ("og", ref["out_grad"].at[my_rows, :], OG.at[:, own_half], ref["out_grad"].at[other_rows, :]),
        ("wu", ref["wu"], WU.at[up_rows, :], ref["wu"]),
        ("wd", ref["wd"], WD.at[down_rows, :], ref["wd"]),
    ]
    if fused:
        pair_rows = pl.ds(pl.multiple_of(r * sp, 8), sp)
        pair_cols = pl.ds(pl.multiple_of(c * (T // 2), TILE), T // 2)
        plan.append(("pbo", ref["pair_bias"].at[pair_rows, pair_cols], ref["PBO"], None))
    local, cross = {}, {}
    for i, (name, src, dst, away) in enumerate(plan):
        local[name] = pltpu.make_async_copy(src, dst, local_sem.at[i])
        local[name].start()
        if away is not None:
            cross[name] = remote(away, dst, entry_s.at[i], entry_r.at[i], dev_c)
    cross["norms"] = remote(NPS, NPR, entry_s.at[len(plan)], entry_r.at[len(plan)], dev_c)

    NPS[...] = jnp.zeros(NPS.shape, f32)
    for i, name in enumerate(("gi", "si", "gm", "sm")):
        NPS[i : i + 1, :] = ref[name][...].reshape(1, half)
    barrier = pltpu.get_barrier_semaphore()
    greeted = [dev_c] + ([dev_x, dev_y] + dev_z if fused else [])
    for device in greeted:
        pl.semaphore_signal(barrier, inc=1, device_id=device, device_id_type=MESH)
    pl.semaphore_wait(barrier, len(greeted))
    for name in ("norms", "tokens", "wq", "wk", "wv"):
        cross[name].start()

    def ready(*chosen):
        for name in chosen:
            if name in local:
                local[name].wait()
            if name in cross:
                cross[name].wait()

    seg = ref["segments"][pl.ds(c, 1), :].astype(f32)
    SC[...] = jnp.broadcast_to(seg, (TILE, T)).T
    ready("pair_bias", "pair_bias2")
    row_id = lax.broadcasted_iota(jnp.int32, (TILE, TILE), 0)
    col_id = lax.broadcasted_iota(jnp.int32, (TILE, TILE), 1)
    for a in range(T // TILE):
        rows = slice(a * TILE, (a + 1) * TILE)
        shift = 0 if a * TILE < h2 else T - D
        for b in range(T // TILE):
            cols = slice(b * TILE, (b + 1) * TILE)
            far = abs(a - b) * TILE
            if far - TILE + 1 >= T // 2:
                MM[rows, cols] = jnp.zeros((TILE, TILE), bf16)
                continue
            same = SC[rows, :] == seg[:, cols]
            if far - TILE + 1 >= WIN:
                weight = jnp.ones((TILE, TILE), f32)
            else:
                weight = jnp.exp(F3[rows, b * TILE - shift : (b + 1) * TILE - shift])
                if far + TILE - 1 >= WIN:
                    inside = jnp.abs(row_id - col_id + (a - b) * TILE) < WIN
                    weight = jnp.where(inside, weight, 1.0)
            MM[rows, cols] = jnp.where(same, weight, 0.0).astype(bf16)

    ready("norms")
    for i in range(4):
        NP[i : i + 1, own_half] = NPS[i : i + 1, :]
        NP[i : i + 1, other_half] = NPR[i : i + 1, :]
    step_rows = 256
    ready("tokens")

    def norm_in(i, carry):
        rows = pl.ds(i * step_rows, step_rows)
        x = XB[rows, :].astype(f32)
        centred = x - jnp.mean(x, axis=1, keepdims=True)
        inv = lax.rsqrt(jnp.mean(centred * centred, axis=1, keepdims=True) + EPSILON)
        t = centred * inv
        F1[rows, :] = x
        XB[rows, :] = t.astype(bf16)
        HN[rows, :] = (t * NP[0:1, :] + NP[1:2, :]).astype(bf16)
        ST[rows, 0:1] = inv
        return carry

    lax.fori_loop(0, T // step_rows, norm_in, 0)
    for name in ("wo", "og", "wu", "wd"):
        cross[name].start()
    ready("wq", "wk", "wv")

    for j in range(D // COLS):
        cols = slice(j * COLS, (j + 1) * COLS)
        late = slice(D + j * COLS, D + (j + 1) * COLS)
        e = jnp.exp(dot(HN[...], WK[:, cols]))
        a = (e * dot(HN[...], WV[:, cols])).astype(bf16)
        AB[:, cols] = a
        AB[:, late] = e.astype(bf16)
        gate = jax.nn.sigmoid(dot(HN[...], WQ[:, cols]))
        inv = 1.0 / dot(MM[...], AB[:, late])
        ratio = dot(MM[...], AB[:, cols]) * inv
        y = gate * ratio
        Y[:, cols] = y.astype(bf16)
        QQ[:, cols] = (y * (1.0 - gate)).astype(bf16)
        RT[:, cols] = ratio.astype(bf16)
        RZ[:, cols] = (gate * inv).astype(bf16)

    ready("wo")
    F1[...] += dot(Y[...], WO[...])

    def norm_mid(i, carry):
        rows = pl.ds(i * step_rows, step_rows)
        x = F1[rows, :]
        centred = x - jnp.mean(x, axis=1, keepdims=True)
        inv = lax.rsqrt(jnp.mean(centred * centred, axis=1, keepdims=True) + EPSILON)
        t = centred * inv
        T2[rows, :] = t.astype(bf16)
        G[rows, :] = (t * NP[2:3, :] + NP[3:4, :]).astype(bf16)
        ST[rows, 1:2] = inv
        F3[rows, :] = jnp.zeros((step_rows, D), f32)
        return carry

    lax.fori_loop(0, T // step_rows, norm_mid, 0)
    ready("og", "wu", "wd", "pbo")

    order = {
        0: lambda b: b if not fused else ((b % 2) * 2 + (b // 2) % 2) * nz + b // 4,
        1: lambda b: b if not fused else (((b // 2) % 2) * 2 + b % 2) * nz + b // 4,
    }
    route = {0: (mx, dev_x, my, dev_y), 1: (my, dev_y, mx, dev_x)}

    def form(k, part, height, own, at=0):
        slot, pslot = k % SLOTS, k % 2
        width = own.shape[1]
        for b in range(nb):
            rows = slice(b * height, (b + 1) * height)
            total = own[rows, :].astype(f32) + PR[pslot, part, rows, at : at + width].astype(f32)
            S[slot, part, order[part](b), 0:height, at : at + width] = total.astype(bf16)

    def first(k, part, height):
        slot = k % SLOTS
        b1, d1, _, _ = route[part]
        return remote(
            S.at[slot, part, pl.ds((1 - b1) * 2 * nz, 2 * nz), pl.ds(0, height), :],
            R1.at[slot, part, :, pl.ds(0, height), :],
            ring_s.at[slot, part], ring_r.at[slot, part], d1,
        )

    def second(k, part, height):
        slot = k % SLOTS
        b1, _, b2, d2 = route[part]
        return remote(
            S.at[slot, part, pl.ds(b1 * 2 * nz + (1 - b2) * nz, nz), pl.ds(0, height), :],
            R2.at[slot, part, :, pl.ds(0, height), :],
            ring_s.at[slot, 2 + part], ring_r.at[slot, 2 + part], d2,
        )

    def third(k, part, height):
        slot = k % SLOTS
        b1, _, b2, _ = route[part]
        copies = []
        for j in range(1, nz):
            sem = 4 + part * (nz - 1) + j - 1
            copies.append(remote(
                S.at[slot, part, b1 * 2 * nz + b2 * nz + lax.rem(mz + j, nz), pl.ds(0, height), :],
                R3.at[slot, part, j - 1, pl.ds(0, height), :],
                ring_s.at[slot, sem], ring_r.at[slot, sem], dev_z[j - 1],
            ))
        return copies

    def whole(k):
        return pltpu.make_async_copy(S.at[k % SLOTS], ref["GO"].at[k], ring_s.at[k % SLOTS, 0])

    def start_sum(k, height):
        if not fused:
            whole(k).start()
            return
        for part in range(2):
            first(k, part, height).start()

    def after_first(k, height):
        if not fused:
            whole(k).wait()
            return
        slot = k % SLOTS
        for part in range(2):
            b1, _, _, _ = route[part]
            first(k, part, height).wait()
            keep = pl.ds(b1 * 2 * nz, 2 * nz)
            total = S[slot, part, keep, 0:height, :].astype(f32) + R1[slot, part, :, 0:height, :].astype(f32)
            S[slot, part, keep, 0:height, :] = total.astype(bf16)
            second(k, part, height).start()

    def after_second(k, height):
        if not fused:
            return
        slot = k % SLOTS
        for part in range(2):
            b1, _, b2, _ = route[part]
            second(k, part, height).wait()
            keep = pl.ds(b1 * 2 * nz + b2 * nz, nz)
            total = S[slot, part, keep, 0:height, :].astype(f32) + R2[slot, part, :, 0:height, :].astype(f32)
            S[slot, part, keep, 0:height, :] = total.astype(bf16)
            for copy in third(k, part, height):
                copy.start()

    def after_third(k, height):
        if not fused:
            return
        slot = k % SLOTS
        for part in range(2):
            b1, _, b2, _ = route[part]
            for copy in third(k, part, height):
                copy.wait()
            total = S[slot, part, b1 * 2 * nz + b2 * nz + mz, 0:height, :].astype(f32)
            for j in range(nz - 1):
                total = total + R3[slot, part, j, 0:height, :].astype(f32)
            if height != sh:
                total = total * jnp.exp(ref["PBO"][:, part * COLS : (part + 1) * COLS])
            FIN[k, part, 0:height, :] = total
            fin_copy(k, part, height).start()

    def fin_copy(k, part, height):
        return pltpu.make_async_copy(
            FIN.at[k, part, pl.ds(0, height), :], ref["o_fin"].at[k, part, pl.ds(0, height), :], fin_sem.at[k, part]
        )

    def hidden_step(owner, i):
        cols = pl.ds(pl.multiple_of(i * COLS, COLS), COLS)
        up_at = pl.ds(pl.multiple_of(owner * D, TILE), D)
        down_at = pl.ds(pl.multiple_of(owner * FH + i * COLS, COLS), COLS)
        s, slope = gelu_pair(dot(G[...], WU[up_at, cols]))
        SD[:, 0:COLS] = s.astype(bf16)
        SD[:, COLS:] = (dot_nt(OG[...], WD[down_at, :]) * slope).astype(bf16)
        F1[...] += dot(SD[:, 0:COLS], WD[down_at, :])
        F3[...] += dot_nt(SD[:, COLS:], WU[up_at, cols])
        return dot_tn(G[...], SD[:, COLS:]), dot_tn(OG[...], SD[:, 0:COLS])

    def pair_copy(k, height):
        slot = k % 2
        return remote(
            PS.at[slot, :, pl.ds(0, height), :], PR.at[slot, :, pl.ds(0, height), :],
            pair_s.at[slot, 0], pair_r.at[slot, 0], dev_c,
        )

    def hidden_block(i, carry):
        slot = lax.rem(i, 2)
        up, down = hidden_step(o, i)
        PS[slot, 0, 0:D, :] = up.astype(bf16)
        PS[slot, 1, 0:D, :] = down.astype(bf16)
        pair_copy(i, D).start()
        up, down = hidden_step(c, i)
        pair_copy(i, D).wait()
        form(i, 0, sh, up)
        form(i, 1, sh, down)
        start_sum(i, sh)
        pl.when(i >= 1)(lambda: after_first(i - 1, sh))
        pl.when(i >= 2)(lambda: after_second(i - 2, sh))
        pl.when(i >= 3)(lambda: after_third(i - 3, sh))
        return carry

    lax.fori_loop(0, blocks, hidden_block, 0)

    def finish_out(i, carry):
        rows = pl.ds(i * step_rows, step_rows)
        G[rows, :] = F1[rows, :].astype(bf16)
        return carry

    lax.fori_loop(0, T // step_rows, finish_out, 0)
    blk_local = pltpu.make_async_copy(G.at[:, own_half], ref["o_blk"].at[my_rows, :], local_sem.at[12])
    blk_cross = remote(G.at[:, other_half], ref["o_blk"].at[my_rows, :], end_s.at[0], end_r.at[0], dev_c)
    blk_local.start()
    blk_cross.start()

    NG[...] = jnp.zeros(NG.shape, f32)

    def norm_mid_back(i, carry):
        rows = pl.ds(i * step_rows, step_rows)
        grad, t = F3[rows, :], T2[rows, :].astype(f32)
        w = grad * NP[2:3, :]
        mean_w = jnp.mean(w, axis=1, keepdims=True)
        mean_wt = jnp.mean(w * t, axis=1, keepdims=True)
        dx = OG[rows, :].astype(f32) + ST[rows, 1:2] * (w - mean_w - t * mean_wt)
        F3[rows, :] = dx
        T2[rows, :] = dx.astype(bf16)
        NG[2] += fold_rows(grad * t)
        NG[3] += fold_rows(grad)
        return carry

    lax.fori_loop(0, T // step_rows, norm_mid_back, 0)
    last = blocks - 1
    after_first(last, sh)
    after_second(last - 1, sh)
    after_third(last - 2, sh)

    NZ = WU
    for j in range(D // COLS):
        cols = slice(j * COLS, (j + 1) * COLS)
        late = slice(D + j * COLS, D + (j + 1) * COLS)
        dm = dot_nt(T2[...], WO[cols, :])
        WD[0:T, cols] = (dm * QQ[:, cols].astype(f32)).astype(bf16)
        dn = dm * RZ[:, cols].astype(f32)
        NZ[0:T, cols] = dn.astype(bf16)
        NZ[0:T, late] = (-dn * RT[:, cols].astype(f32)).astype(bf16)
    OG[0:D, :] = dot_tn(T2[...], Y[...]).astype(bf16)
    QQ[0:D, :] = dot_tn(HN[...], WD[0:T, :]).astype(bf16)

    sources = (OG, QQ, RZ, RT)

    pieces = functools.partial(late_pieces, half)

    def late_copies(k, first_part):
        slot, copies = k % 2, []
        for part in range(2):
            for source, off, width, at in pieces(first_part + part):
                cols = pl.ds(pl.multiple_of(o * half + off, TILE), width)
                copies.append(remote(
                    sources[source].at[pl.ds(0, D), cols], PR.at[slot, part, pl.ds(0, D), pl.ds(at, width)],
                    pair_s.at[slot, 1 + len(copies)], pair_r.at[slot, 1 + len(copies)], dev_c,
                ))
        return copies

    def late_form(k, first_part, copies):
        for copy in copies:
            copy.wait()
        for part in range(2):
            for source, off, width, at in pieces(first_part + part):
                cols = pl.ds(pl.multiple_of(c * half + off, TILE), width)
                form(k, part, sh, sources[source][0:D, cols], at)

    k0, k1, k2, k3 = blocks, blocks + 1, blocks + 2, blocks + 3
    sent = late_copies(k0, 0)
    for copy in sent:
        copy.start()

    for j in range(T // COLS):
        cols = slice(j * COLS, (j + 1) * COLS)
        low, high = max(0, (j - 1) * COLS), min(T, (j + 2) * COLS)
        target = PS.at[j // 2, j % 2]
        for start, stop in ((0, low), (high, T)):
            if stop > start:
                target[start:stop, :] = jnp.zeros((stop - start, COLS), bf16)
        grad = dot_nt(NZ[low:high, :], AB[cols, :])
        for t in range(COLS // TILE):
            at = j * COLS + t * TILE
            same = SC[low:high, :] == seg[:, at : at + TILE]
            gap = (
                lax.broadcasted_iota(jnp.int32, (high - low, TILE), 0)
                - lax.broadcasted_iota(jnp.int32, (high - low, TILE), 1)
                + (low - at)
            )
            kept = jnp.where(same & (jnp.abs(gap) < WIN), grad[:, t * TILE : (t + 1) * TILE], 0.0)
            target[low:high, t * TILE : (t + 1) * TILE] = kept.astype(bf16)

    late_form(k0, 0, sent)
    start_sum(k0, sh)
    after_second(last, sh)
    after_third(last - 1, sh)

    def mixer_copy():
        return remote(PS.at[o], PR.at[k1 % 2], pair_s.at[k1 % 2, 0], pair_r.at[k1 % 2, 0], dev_c)

    mixer_copy().start()

    for j in range(D // COLS):
        cols = slice(j * COLS, (j + 1) * COLS)
        late = slice(D + j * COLS, D + (j + 1) * COLS)
        da = dot_tn(MM[...], NZ[0:T, cols])
        db = dot_tn(MM[...], NZ[0:T, late])
        e = AB[:, late].astype(f32)
        WD[T : 2 * T, cols] = (db * e + da * AB[:, cols].astype(f32)).astype(bf16)
        WD[2 * T : 3 * T, cols] = (da * e).astype(bf16)
    RZ[0:D, :] = dot_tn(HN[...], WD[T : 2 * T, :]).astype(bf16)

    mixer_copy().wait()
    for part in range(2):
        form(k1, part, sp, PS.at[c, part][...])
    start_sum(k1, sp)
    after_first(k0, sh)
    after_third(last, sh)

    sent = late_copies(k2, 2)
    for copy in sent:
        copy.start()
    RT[0:D, :] = dot_tn(HN[...], WD[2 * T : 3 * T, :]).astype(bf16)
    late_form(k2, 2, sent)
    start_sum(k2, sh)
    after_first(k1, sp)
    after_second(k0, sh)
    sent = late_copies(k3, 4)
    for copy in sent:
        copy.start()

    for j in range(D // COLS):
        cols = slice(j * COLS, (j + 1) * COLS)
        F1[:, cols] = (
            dot_nt(WD[0:T, :], WQ[cols, :])
            + dot_nt(WD[T : 2 * T, :], WK[cols, :])
            + dot_nt(WD[2 * T : 3 * T, :], WV[cols, :])
        )
    late_form(k3, 4, sent)
    start_sum(k3, sh)

    def norm_in_back(i, carry):
        rows = pl.ds(i * step_rows, step_rows)
        grad, t = F1[rows, :], XB[rows, :].astype(f32)
        w = grad * NP[0:1, :]
        mean_w = jnp.mean(w, axis=1, keepdims=True)
        mean_wt = jnp.mean(w * t, axis=1, keepdims=True)
        Y[rows, :] = (F3[rows, :] + ST[rows, 0:1] * (w - mean_w - t * mean_wt)).astype(bf16)
        NG[0] += fold_rows(grad * t)
        NG[1] += fold_rows(grad)
        return carry

    lax.fori_loop(0, T // step_rows, norm_in_back, 0)
    tok_local = pltpu.make_async_copy(Y.at[:, own_half], ref["o_tok"].at[my_rows, :], local_sem.at[13])
    tok_cross = remote(Y.at[:, other_half], ref["o_tok"].at[my_rows, :], end_s.at[1], end_r.at[1], dev_c)
    tok_local.start()
    tok_cross.start()

    NV[...] = jnp.zeros(NV.shape, f32)
    for i in range(4):
        NV[i : i + 1, :] = jnp.sum(NG[i], axis=0, keepdims=True)
    copy = remote(NV.at[:, other_half], NR.at[0], norm_s.at[0], norm_r.at[0], dev_c)
    copy.start()
    copy.wait()
    NR[1] = NV[:, own_half] + NR[0]
    if fused:
        copy = remote(NR.at[1], NR.at[2], norm_s.at[1], norm_r.at[1], dev_x)
        copy.start()
        after_first(k2, sh)
        after_second(k1, sp)
        after_third(k0, sh)
        copy.wait()
        NR[3] = NR[1] + NR[2]
        copy = remote(NR.at[3], NR.at[4], norm_s.at[2], norm_r.at[2], dev_y)
        copy.start()
        after_first(k3, sh)
        after_second(k2, sh)
        after_third(k1, sp)
        copy.wait()
        total = NR[3] + NR[4]
        NZS[mz] = total
        copies = [
            remote(NZS.at[mz], NZS.at[mz], norm_s.at[2 + j], norm_r.at[2 + j], dev_z[j - 1])
            for j in range(1, nz)
        ]
        for copy in copies:
            copy.start()
        after_second(k3, sh)
        after_third(k2, sh)
        for copy in copies:
            copy.wait()
        total = NZS[0]
        for j in range(1, nz):
            total = total + NZS[j]
        ref["o_norm"][...] = total
        after_third(k3, sh)
        for k in range(blocks + 4):
            for part in range(2):
                fin_copy(k, part, sp if k == k1 else sh).wait()
    else:
        ref["o_norm"][...] = NR[1]
        for k in (k2, k3):
            after_first(k, sh)
    blk_local.wait()
    blk_cross.wait()
    tok_local.wait()
    tok_cross.wait()


def late_pieces(half, part_no):
    found, at = [], part_no * COLS
    while at < (part_no + 1) * COLS:
        width = min(half - at % half, (part_no + 1) * COLS - at)
        found.append((at // half, at % half, width, at - part_no * COLS))
        at += width
    return found


def unpack_kernel(sh, blocks, half, pieces_in, names, *all_refs):
    ref = dict(zip(names, all_refs))
    step = ref["tok_in"].shape[0] // pieces_in
    load_b = pltpu.make_async_copy(ref["o_blk"], ref["blk"], ref["sem"].at[0, 0])
    save_b = pltpu.make_async_copy(ref["blk"], ref["r_blk"], ref["sem"].at[1, 0])
    loads, saves = [], []
    for i in range(pieces_in):
        rows = slice(i * step, (i + 1) * step)
        loads.append(pltpu.make_async_copy(ref["o_tok"].at[rows, :], ref["tok_in"].at[rows, :], ref["sem"].at[0, 1 + i]))
        saves.append(pltpu.make_async_copy(ref["tok_out"].at[rows, :], ref["r_tok"].at[rows, :], ref["sem"].at[1, 1 + i]))
    load_f = pltpu.make_async_copy(ref["o_fin"], ref["fin"], ref["sem"].at[0, 1 + pieces_in])
    load_n = pltpu.make_async_copy(ref["o_norm"], ref["norm"], ref["sem"].at[1, 1 + pieces_in])
    loads[0].start()
    load_b.start()
    for load in loads[1:]:
        load.start()
    load_f.start()
    load_n.start()
    fin, norm = ref["fin"], ref["norm"]
    for i in range(pieces_in):
        loads[i].wait()
        rows = slice(i * step, (i + 1) * step)
        ref["tok_out"][rows, :] = ref["tok_in"][rows, :].astype(f32)
        saves[i].start()
        if i == 0:
            load_b.wait()
            save_b.start()
    load_n.wait()
    for i, name in enumerate(("r_gi", "r_si", "r_gm", "r_sm")):
        ref[name][...] = norm[i, :]
    load_f.wait()
    for k in range(blocks):
        cols = slice(k * COLS, (k + 1) * COLS)
        ref["r_up"][:, cols] = fin[k, 0, 0:sh, :]
        ref["r_dn"][:, cols] = fin[k, 1, 0:sh, :]
    for part in range(2):
        ref["r_pair"][:, part * COLS : (part + 1) * COLS] = fin[blocks + 1, part]
    for k, first_part in ((blocks, 0), (blocks + 2, 2), (blocks + 3, 4)):
        for part in range(2):
            for source, off, width, at in late_pieces(half, first_part + part):
                value = fin[k, part, 0:sh, at : at + width]
                ref[("r_wo", "r_q", "r_k", "r_v")[source]][:, off : off + width] = value
    for save in saves:
        save.wait()
    save_b.wait()


def unpack(T, D, FH, sh, sp, out):
    half = D // 2
    blocks = FH // COLS
    pieces_in = 4
    any_spec, vmem = pl.BlockSpec(memory_space=pl.ANY), pl.BlockSpec(memory_space=pltpu.VMEM)
    inputs = {"o_blk": any_spec, "o_tok": any_spec, "o_norm": any_spec, "o_fin": any_spec}
    results = {"r_blk": (any_spec, (2 * T, half), bf16), "r_tok": (any_spec, (2 * T, half), f32)}
    results |= {name: (vmem, (half,), f32) for name in ("r_gi", "r_si", "r_gm", "r_sm")}
    results |= {name: (vmem, (sh, half), f32) for name in ("r_q", "r_k", "r_v", "r_wo")}
    results |= {
        "r_up": (vmem, (sh, FH), f32), "r_dn": (vmem, (sh, FH), f32),
        "r_pair": (vmem, (sp, T // 2), f32),
    }
    scratch = {
        "blk": pltpu.VMEM((2 * T, half), bf16), "tok_in": pltpu.VMEM((2 * T, half), bf16),
        "tok_out": pltpu.VMEM((2 * T, half), f32), "sem": pltpu.SemaphoreType.DMA((2, 2 + pieces_in)),
        "fin": pltpu.VMEM(out["o_fin"].shape, f32), "norm": pltpu.VMEM((8, half), f32),
    }
    names = tuple(inputs) + tuple(results) + tuple(scratch)
    values = pl.pallas_call(
        functools.partial(unpack_kernel, sh, blocks, half, pieces_in, names),
        out_shape=tuple(jax.ShapeDtypeStruct(shape, kind) for _, shape, kind in results.values()),
        in_specs=list(inputs.values()),
        out_specs=tuple(spec for spec, _, _ in results.values()),
        scratch_shapes=list(scratch.values()),
        compiler_params=pltpu.CompilerParams(vmem_limit_bytes=63 << 20),
    )(*(out[name] for name in inputs))
    done = {"o_" + name[2:]: value for name, value in zip(results, values)}
    done["o_wo"], done["o_dn"] = done["o_wo"].T, done["o_dn"].T
    return done


def run_block(T, D, FH, R, args):
    half = D // 2
    blocks = FH // COLS
    fused = R % 4 == 0 and (D // R) % 16 == 0 and D % R == 0 and (T // R) % 16 == 0 and T % R == 0
    nb = R if fused else 16
    nz = nb // 4
    sh, sp = D // nb, T // nb
    any_spec, vmem = pl.BlockSpec(memory_space=pl.ANY), pl.BlockSpec(memory_space=pltpu.VMEM)
    inputs = {
        "tokens": any_spec, "segments": vmem, "gi": vmem, "si": vmem, "wq": any_spec, "wk": any_spec,
        "wv": any_spec, "wo": any_spec, "gm": vmem, "sm": vmem, "wu": any_spec, "wd": any_spec,
        "pair_bias": any_spec, "out_grad": any_spec,
    }
    outputs = {
        "o_blk": (any_spec, (2 * T, half), bf16), "o_tok": (any_spec, (2 * T, half), bf16),
        "o_norm": (vmem, (8, half), f32),
    }
    if fused:
        outputs["o_fin"] = (any_spec, (blocks + 4, 2, sp, COLS), f32)
    else:
        outputs["GO"] = (any_spec, (blocks + 4, 2, nb, sp, COLS), bf16)
    wide = (T, D)
    scratch = {name: pltpu.VMEM(wide, bf16) for name in ("XB", "OG", "HN", "G", "Y", "QQ", "RT", "RZ", "T2")}
    scratch |= {
        "AB": pltpu.VMEM((T, 2 * D), bf16), "MM": pltpu.VMEM((T, T), bf16),
        "F1": pltpu.VMEM(wide, f32), "F3": pltpu.VMEM(wide, f32), "ST": pltpu.VMEM((T, TILE), f32),
        "WQ": pltpu.VMEM((D, D), bf16), "WK": pltpu.VMEM((D, D), bf16), "WV": pltpu.VMEM((D, D), bf16),
        "WO": pltpu.VMEM((D, D), bf16), "WU": pltpu.VMEM((2 * D, FH), bf16), "WD": pltpu.VMEM((2 * FH, D), bf16),
        "SD": pltpu.VMEM((T, 2 * COLS), bf16), "SC": pltpu.VMEM((T, TILE), f32),
        "NP": pltpu.VMEM((8, D), f32), "NPS": pltpu.VMEM((8, half), f32), "NPR": pltpu.VMEM((8, half), f32),
        "PS": pltpu.VMEM((2, 2, T, COLS), bf16), "PR": pltpu.VMEM((2, 2, T, COLS), bf16),
        "S": pltpu.VMEM((SLOTS, 2, nb, sp, COLS), bf16),
        "R1": pltpu.VMEM((SLOTS, 2, 2 * nz, sp, COLS), bf16) if fused else pltpu.VMEM((8, TILE), f32),
        "R2": pltpu.VMEM((SLOTS, 2, nz, sp, COLS), bf16) if fused else pltpu.VMEM((8, TILE), f32),
        "R3": pltpu.VMEM((SLOTS, 2, nz - 1, sp, COLS), bf16) if fused else pltpu.VMEM((8, TILE), f32),
        "NG": pltpu.VMEM((4, 8, D), f32), "NV": pltpu.VMEM((8, D), f32), "NR": pltpu.VMEM((5, 8, half), f32),
        "NZS": pltpu.VMEM((nz, 8, half), f32), "PBO": pltpu.VMEM((sp, T // 2), f32),
        "FIN": pltpu.VMEM((blocks + 4, 2, sp, COLS), f32) if fused else pltpu.VMEM((8, TILE), f32),
        "fin_sem": pltpu.SemaphoreType.DMA((blocks + 4, 2)),
        "local_sem": pltpu.SemaphoreType.DMA((16,)),
        "entry_s": pltpu.SemaphoreType.DMA((16,)), "entry_r": pltpu.SemaphoreType.DMA((16,)),
        "pair_s": pltpu.SemaphoreType.DMA((2, 5)), "pair_r": pltpu.SemaphoreType.DMA((2, 5)),
        "ring_s": pltpu.SemaphoreType.DMA((SLOTS, 4 + 2 * nz)), "ring_r": pltpu.SemaphoreType.DMA((SLOTS, 4 + 2 * nz)),
        "end_s": pltpu.SemaphoreType.DMA((2,)), "end_r": pltpu.SemaphoreType.DMA((2,)),
        "norm_s": pltpu.SemaphoreType.DMA((2 + nz,)), "norm_r": pltpu.SemaphoreType.DMA((2 + nz,)),
    }
    names = tuple(inputs) + tuple(outputs) + tuple(scratch)
    results = pl.pallas_call(
        functools.partial(block_kernel, T, D, FH, R, fused, names),
        out_shape=tuple(jax.ShapeDtypeStruct(shape, kind) for _, shape, kind in outputs.values()),
        in_specs=list(inputs.values()),
        out_specs=tuple(spec for spec, _, _ in outputs.values()),
        scratch_shapes=list(scratch.values()),
        compiler_params=pltpu.CompilerParams(
            collective_id=0, has_side_effects=True, vmem_limit_bytes=63 << 20
        ),
    )(*args)
    out = dict(zip(outputs, results))
    if fused:
        return unpack(T, D, FH, sh, sp, out)
    out["o_tok"] = out["o_tok"].astype(f32)
    parts = out.pop("GO")
    height = lambda v, rows: v.reshape(nb, sp, v.shape[-1])[:, : rows // nb].reshape(rows, v.shape[-1])
    join = lambda chosen: jnp.concatenate(chosen, 1).astype(f32)
    scatter = lambda v: lax.psum_scatter(v, "rows", scatter_dimension=0, tiled=True)
    out["o_up"] = scatter(join([height(parts[k, 0], D) for k in range(blocks)]))
    out["o_dn"] = scatter(join([height(parts[k, 1], D) for k in range(blocks)])).T
    late = join([height(parts[k, p], D) for k in (blocks, blocks + 2, blocks + 3) for p in range(2)])
    cut = [scatter(late[:, i * half : (i + 1) * half]) for i in range(4)]
    out["o_wo"], out["o_q"], out["o_k"], out["o_v"] = cut[0].T, cut[1], cut[2], cut[3]
    pair = scatter(join([height(parts[blocks + 1, p], T) for p in range(2)]))
    bias = lax.dynamic_slice(
        args[12], (lax.axis_index("rows") * pair.shape[0], lax.axis_index("chan") * (T // 2)), pair.shape
    )
    out["o_pair"] = pair * jnp.exp(bias)
    norms = lax.psum(out["o_norm"], "rows")
    for i, name in enumerate(("o_gi", "o_si", "o_gm", "o_sm")):
        out[name] = norms[i]
    return out


def on_device(
    tokens, segments, gain_in, shift_in, query_weight, key_weight, value_weight, out_weight,
    gain_mid, shift_mid, up_weight, down_weight, pair_bias, out_grad,
):
    T = segments.shape[1]
    D, FH = up_weight.shape
    R = lax.axis_size("rows")
    out = run_block(T, D, FH, R, (
        tokens, segments, gain_in, shift_in, query_weight, key_weight, value_weight, out_weight,
        gain_mid, shift_mid, up_weight, down_weight, pair_bias, out_grad,
    ))
    return tuple(out[name] for name in (
        "o_blk", "o_tok", "o_gi", "o_si", "o_q", "o_k", "o_v", "o_wo", "o_gm", "o_sm", "o_up", "o_dn", "o_pair",
    ))


def solution(mesh):
    split, first, second = P("rows", "chan"), P("chan", None), P(None, "chan")
    return jax.shard_map(
        on_device,
        mesh=mesh,
        in_specs=(
            split, P("rows", None), P("chan"), P("chan"), second, second, second, first,
            P("chan"), P("chan"), second, first, P(), split,
        ),
        out_specs=(
            split, split, P("chan"), P("chan"), split, split, split, P("chan", "rows"),
            P("chan"), P("chan"), split, P("chan", "rows"), split,
        ),
        check_vma=False,
    )
```

```python
import functools
from types import SimpleNamespace

import jax
import jax.numpy as jnp
from jax import lax
from jax.experimental import pallas as pl
from jax.experimental.pallas import tpu as pltpu
from jax.sharding import PartitionSpec as P

MESH = pl.DeviceIdType.MESH
ANY, VMEM = pl.BlockSpec(memory_space=pl.ANY), pl.BlockSpec(memory_space=pltpu.VMEM)
WIN = 256
EPSILON = 1e-05
TILE = 128
COLS = 256
SLOTS = 4
STEP = 256
f32 = jnp.float32
bf16 = jnp.bfloat16


def dot(left, right, cl=1, cr=0):
    return lax.dot_general(left, right, (((cl,), (cr,)), ((), ())), preferred_element_type=f32)


def dot_nt(left, right):
    return dot(left, right, 1, 1)


def dot_tn(left, right):
    return dot(left, right, 0, 0)


def gelu_pair(p):
    phi = 0.5 * (1.0 + lax.erf(p * 0.7071067811865476))
    return p * phi, phi + p * (jnp.exp(-0.5 * p * p) * 0.3989422804014327)


def fold_rows(v):
    return jnp.sum(v.reshape(v.shape[0] // 8, 8, v.shape[1]), axis=0)


def late_pieces(half, part_no):
    found, at = [], part_no * COLS
    while at < (part_no + 1) * COLS:
        width = min(half - at % half, (part_no + 1) * COLS - at)
        found.append((at // half, at % half, width, at - part_no * COLS))
        at += width
    return found


def block_kernel(T, D, FH, R, fused, names, *all_refs):
    ref = SimpleNamespace(**dict(zip(names, all_refs)))
    half = D // 2
    blocks = FH // COLS
    nb = R if fused else 16
    nz = nb // 4
    sh, sp = D // nb, T // nb
    r = lax.axis_index("rows")
    c = lax.axis_index("chan")
    o = 1 - c
    mx, my, mz = lax.rem(r, 2), lax.rem(r // 2, 2), r // 4
    z0, z1 = lax.rem(mz, 2), mz // 2
    dev_c = (r, o)
    dev_x = (r + 1 - 2 * mx, c)
    dev_y = (r + 2 - 4 * my, c)
    dev_z = [(lax.rem(mz + j, nz) * 4 + lax.rem(r, 4), c) for j in range(1, nz)]
    dev_z0 = (r + 4 - 8 * z0, c)
    dev_z1 = (r + 8 - 16 * z1, c)
    own_half = pl.ds(pl.multiple_of(c * half, TILE), half)
    other_half = pl.ds(pl.multiple_of(o * half, TILE), half)

    XB, OG, HN, G = ref.XB, ref.OG, ref.HN, ref.G
    Y, QQ, RT, RZ, T2 = ref.Y, ref.QQ, ref.RT, ref.RZ, ref.T2
    AB, MM, F1, F3, ST = ref.AB, ref.MM, ref.F1, ref.F3, ref.ST
    WQ, WK, WV, WO, WU, WD = ref.WQ, ref.WK, ref.WV, ref.WO, ref.WU, ref.WD
    SD, SC, NP, NPS, NPR = ref.SD, ref.SC, ref.NP, ref.NPS, ref.NPR
    PS, PR, S, RX, FIN = ref.PS, ref.PR, ref.S, ref.RX, ref.FIN
    NG, NV, NR, NZS = ref.NG, ref.NV, ref.NR, ref.NZS

    def remote(src, dst, send, recv, device):
        return pltpu.make_async_remote_copy(
            src_ref=src, dst_ref=dst, send_sem=send, recv_sem=recv, device_id=device, device_id_type=MESH
        )

    my_rows, other_rows = pl.ds(c * T, T), pl.ds(o * T, T)
    h2 = T // 2
    local, cross = [], []

    def load(src, dst, away=None, there=None):
        at = len(local)
        local.append(pltpu.make_async_copy(src, dst, ref.local_sem.at[at]))
        cross.append(None if away is None else remote(away, there, ref.entry_s.at[at], ref.entry_r.at[at], dev_c))
        local[at].start()
        return at

    bias_at = [
        load(ref.pair_bias.at[0:h2, 0:D], F3.at[0:h2, :]),
        load(ref.pair_bias.at[h2:T, T - D : T], F3.at[h2:T, :]),
    ]
    tokens_at = load(
        ref.tokens.at[my_rows, :], XB.at[:, own_half], ref.tokens.at[other_rows, :], XB.at[:, own_half]
    )
    qkv_at = [
        load(src, dst.at[:, 0:half], src, dst.at[:, half:D]) for src, dst in ((ref.wk, WK), (ref.wv, WV), (ref.wq, WQ))
    ]
    wo_at = load(ref.wo, WO.at[0:half, :], ref.wo, WO.at[half:D, :])
    og_at = load(
        ref.out_grad.at[my_rows, :], OG.at[:, own_half], ref.out_grad.at[other_rows, :], OG.at[:, own_half]
    )
    wide = 2 * COLS

    def up_piece(i, away):
        cols = pl.ds(pl.multiple_of(i * wide, wide), wide)
        if away:
            return remote(ref.wu.at[:, cols], WU.at[D : 2 * D, cols], ref.up_s.at[i], ref.up_r.at[i], dev_c)
        return pltpu.make_async_copy(ref.wu.at[:, cols], WU.at[0:D, cols], ref.up_l.at[i])

    def down_piece(i, away):
        src = ref.wd.at[pl.ds(pl.multiple_of(i * wide, wide), wide), :]
        if away:
            dst = WD.at[pl.ds(pl.multiple_of(FH + i * wide, wide), wide), :]
            return remote(src, dst, ref.down_s.at[i], ref.down_r.at[i], dev_c)
        return pltpu.make_async_copy(src, WD.at[pl.ds(pl.multiple_of(i * wide, wide), wide), :], ref.down_l.at[i])

    pbo_at = None
    if fused:
        pair_rows = pl.ds(pl.multiple_of(r * sp, 8), sp)
        pair_cols = pl.ds(pl.multiple_of(c * (T // 2), TILE), T // 2)
        pbo_at = load(ref.pair_bias.at[pair_rows, pair_cols], ref.PBO)
    for i in range(blocks // 2):
        up_piece(i, False).start()
        down_piece(i, False).start()

    NPS[...] = jnp.zeros(NPS.shape, f32)
    for i, vector in enumerate((ref.gi, ref.si, ref.gm, ref.sm)):
        NPS[i : i + 1, :] = vector[...].reshape(1, half)
    norms_cross = remote(NPS, NPR, ref.entry_s.at[15], ref.entry_r.at[15], dev_c)
    barrier = pltpu.get_barrier_semaphore()
    greeted = [dev_c] + ([dev_x, dev_y] + dev_z if fused else [])
    for device in greeted:
        pl.semaphore_signal(barrier, inc=1, device_id=device, device_id_type=MESH)
    pl.semaphore_wait(barrier, len(greeted))
    norms_cross.start()
    for at in [tokens_at] + qkv_at:
        cross[at].start()

    def ready(*chosen):
        for at in chosen:
            local[at].wait()
            if cross[at] is not None:
                cross[at].wait()

    seg = ref.segments[pl.ds(c, 1), :].astype(f32)
    SC[...] = jnp.broadcast_to(seg, (TILE, T)).T
    ready(*bias_at)
    row_id = lax.broadcasted_iota(jnp.int32, (TILE, TILE), 0)
    col_id = lax.broadcasted_iota(jnp.int32, (TILE, TILE), 1)
    for a in range(T // TILE):
        rows = slice(a * TILE, (a + 1) * TILE)
        shift = 0 if a * TILE < h2 else T - D
        for b in range(T // TILE):
            cols = slice(b * TILE, (b + 1) * TILE)
            far = abs(a - b) * TILE
            if far - TILE + 1 >= T // 2:
                MM[rows, cols] = jnp.zeros((TILE, TILE), bf16)
                continue
            same = SC[rows, :] == seg[:, cols]
            if far - TILE + 1 >= WIN:
                weight = jnp.ones((TILE, TILE), f32)
            else:
                weight = jnp.exp(F3[rows, b * TILE - shift : (b + 1) * TILE - shift])
                if far + TILE - 1 >= WIN:
                    inside = jnp.abs(row_id - col_id + (a - b) * TILE) < WIN
                    weight = jnp.where(inside, weight, 1.0)
            MM[rows, cols] = jnp.where(same, weight, 0.0).astype(bf16)

    norms_cross.wait()
    for i in range(4):
        NP[i : i + 1, own_half] = NPS[i : i + 1, :]
        NP[i : i + 1, other_half] = NPR[i : i + 1, :]
    ready(tokens_at)

    def norm_in(i, carry):
        rows = pl.ds(i * STEP, STEP)
        x = XB[rows, :].astype(f32)
        centred = x - jnp.mean(x, axis=1, keepdims=True)
        inv = lax.rsqrt(jnp.mean(centred * centred, axis=1, keepdims=True) + EPSILON)
        t = centred * inv
        F1[rows, :] = x
        XB[rows, :] = t.astype(bf16)
        HN[rows, :] = (t * NP[0:1, :] + NP[1:2, :]).astype(bf16)
        ST[rows, 0:1] = inv
        return carry

    lax.fori_loop(0, T // STEP, norm_in, 0)
    cross[wo_at].start()
    cross[og_at].start()
    for i in range(blocks // 2):
        up_piece(i, True).start()
        down_piece(i, True).start()
    for at in qkv_at:
        local[at].wait()

    for j in range(D // COLS):
        if j * COLS <= half < (j + 1) * COLS:
            for at in qkv_at:
                cross[at].wait()
        cols = slice(j * COLS, (j + 1) * COLS)
        late = slice(D + j * COLS, D + (j + 1) * COLS)
        e = jnp.exp(dot(HN[...], WK[:, cols]))
        a = (e * dot(HN[...], WV[:, cols])).astype(bf16)
        AB[:, cols] = a
        AB[:, late] = e.astype(bf16)
        gate = jax.nn.sigmoid(dot(HN[...], WQ[:, cols]))
        inv = 1.0 / dot(MM[...], AB[:, late])
        ratio = dot(MM[...], AB[:, cols]) * inv
        y = gate * ratio
        Y[:, cols] = y.astype(bf16)
        QQ[:, cols] = (y * (1.0 - gate)).astype(bf16)
        RT[:, cols] = ratio.astype(bf16)
        RZ[:, cols] = (gate * inv).astype(bf16)

    ready(wo_at)
    F1[...] += dot(Y[...], WO[...])

    def norm_mid(i, carry):
        rows = pl.ds(i * STEP, STEP)
        x = F1[rows, :]
        centred = x - jnp.mean(x, axis=1, keepdims=True)
        inv = lax.rsqrt(jnp.mean(centred * centred, axis=1, keepdims=True) + EPSILON)
        t = centred * inv
        T2[rows, :] = t.astype(bf16)
        G[rows, :] = (t * NP[2:3, :] + NP[3:4, :]).astype(bf16)
        ST[rows, 1:2] = inv
        F3[rows, :] = jnp.zeros((STEP, D), f32)
        return carry

    lax.fori_loop(0, T // STEP, norm_mid, 0)
    ready(og_at)
    if fused:
        ready(pbo_at)

    axes = (((mx, dev_x), (my, dev_y)), ((my, dev_y), (mx, dev_x)))
    room = (0, nb // 2, nb // 2 + nb // 4)

    def place(b, part):
        if not fused:
            return b
        bx, by, bz = b % 2, (b // 2) % 2, b // 4
        outer, inner = (bx, by) if part == 0 else (by, bx)
        return (outer * 2 + inner) * nz + bz

    def chunk(k, height=sh, reach=None):
        return SimpleNamespace(k=k, height=height, reach=reach, slot=k % SLOTS)

    def form(ch, part, own, at=0):
        width, height = own.shape[1], ch.height
        for b in range(nb):
            rows = slice(b * height, (b + 1) * height)
            total = own[rows, :].astype(bf16) + PR[ch.k % 2, part, rows, at : at + width]
            S[ch.slot, part, place(b, part), 0:height, at : at + width] = total

    def span(part, n):
        base, size = 0, nb
        for bit, _ in axes[part][: n - 1]:
            size //= 2
            base = base + bit * size
        return base, size

    def runs(ch, part, base, size):
        if ch.reach is None:
            return [(base, 0, size)]
        low, count = ch.reach[part]
        return [(base + i * nz + low, i * count, count) for i in range(size // nz)]

    def stage(ch, part, n):
        rows, copies = pl.ds(0, ch.height), []
        base, size = span(part, n)
        if n < 3:
            bit, device = axes[part][n - 1]
            for i, (start, at, count) in enumerate(runs(ch, part, base + (1 - bit) * (size // 2), size // 2)):
                sem = 2 * (n - 1) + i
                copies.append(remote(
                    S.at[ch.slot, part, pl.ds(start, count), rows, :],
                    RX.at[ch.slot, part, pl.ds(room[n - 1] + at, count), rows, :],
                    ref.ring_s.at[ch.slot, part, sem], ref.ring_r.at[ch.slot, part, sem], device,
                ))
        else:
            for j in range(1, nz):
                sem = 2 + j
                copies.append(remote(
                    S.at[ch.slot, part, base + lax.rem(mz + j, nz), rows, :],
                    RX.at[ch.slot, part, room[n - 1] + j - 1, rows, :],
                    ref.ring_s.at[ch.slot, part, sem], ref.ring_r.at[ch.slot, part, sem], dev_z[j - 1],
                ))
        return copies

    def whole(ch):
        return pltpu.make_async_copy(S.at[ch.slot], ref.GO.at[ch.k], ref.ring_s.at[ch.slot, 0, 0])

    def fin_copy(ch, part):
        rows = pl.ds(0, ch.height)
        return pltpu.make_async_copy(
            FIN.at[ch.k, part, rows, :], ref.o_fin.at[ch.k, part, rows, :], ref.fin_sem.at[ch.k, part]
        )

    def launch(ch):
        if not fused:
            whole(ch).start()
            return
        for part in range(2):
            for copy in stage(ch, part, 1):
                copy.start()

    def advance(ch, n):
        if not fused:
            if n == 1:
                whole(ch).wait()
            return
        rows = slice(0, ch.height)
        for part in range(2):
            for copy in stage(ch, part, n):
                copy.wait()
            if n < 3:
                for start, at, count in runs(ch, part, *span(part, n + 1)):
                    S[ch.slot, part, pl.ds(start, count), rows, :] += RX[
                        ch.slot, part, pl.ds(room[n - 1] + at, count), rows, :
                    ]
                for copy in stage(ch, part, n + 1):
                    copy.start()
                continue
            total = S[ch.slot, part, span(part, 3)[0] + mz, rows, :].astype(f32)
            for j in range(nz - 1):
                total = total + RX[ch.slot, part, room[2] + j, rows, :].astype(f32)
            if ch.height != sh:
                total = total * jnp.exp(ref.PBO[:, pl.ds(pl.multiple_of(pair_part[part] * COLS, COLS), COLS)])
            FIN[ch.k, part, rows, :] = total
            fin_copy(ch, part).start()

    def hidden_step(owner, i):
        cols = pl.ds(pl.multiple_of(i * COLS, COLS), COLS)
        up_at = slice(owner * D, (owner + 1) * D)
        down_at = pl.ds(pl.multiple_of(owner * FH + i * COLS, COLS), COLS)
        s, slope = gelu_pair(dot(G[...], WU[up_at, cols]))
        SD[:, 0:COLS] = s.astype(bf16)
        SD[:, COLS:] = (dot_nt(OG[...], WD[down_at, :]) * slope).astype(bf16)
        F1[...] += dot(SD[:, 0:COLS], WD[down_at, :])
        F3[...] += dot_nt(SD[:, COLS:], WU[up_at, cols])
        return dot_tn(G[...], SD[:, COLS:]), dot_tn(OG[...], SD[:, 0:COLS])

    def pair_copy(slot, height):
        return remote(
            PS.at[slot, :, pl.ds(0, height), :], PR.at[slot, :, pl.ds(0, height), :],
            ref.pair_s.at[slot, 0], ref.pair_r.at[slot, 0], dev_c,
        )

    def hidden_pair(i, carry):
        for copies in (up_piece, down_piece):
            copies(i, False).wait()
            copies(i, True).wait()
        for q in range(2):
            ch = chunk(2 * i + q)
            up, down = hidden_step(1, ch.k)
            PS[q, 0, 0:D, :] = up.astype(bf16)
            PS[q, 1, 0:D, :] = down.astype(bf16)
            pair_copy(q, D).start()
            for n in (1, 2, 3):
                before = chunk(2 * i + q - 1 - n)
                pl.when(2 * i + q >= 1 + n)(functools.partial(advance, before, n))
            up, down = hidden_step(0, ch.k)
            pair_copy(q, D).wait()
            form(ch, 0, up)
            form(ch, 1, down)
            launch(ch)
        return carry

    lax.fori_loop(0, blocks // 2, hidden_pair, 0)
    h2, h3, h4, h5 = (chunk(blocks - i) for i in (4, 3, 2, 1))
    k0, k2, k3 = chunk(blocks), chunk(blocks + 2), chunk(blocks + 3)
    pair_part = (c, 1 - c)
    k1 = chunk(blocks + 1, sp, ((2 * c, 2), (c, 3)) if fused else None)

    def finish_out(i, carry):
        rows = pl.ds(i * STEP, STEP)
        G[rows, :] = F1[rows, :].astype(bf16)
        return carry

    lax.fori_loop(0, T // STEP, finish_out, 0)
    blk_local = pltpu.make_async_copy(G.at[:, own_half], ref.o_blk.at[my_rows, :], ref.end_l.at[0])
    blk_cross = remote(G.at[:, other_half], ref.o_blk.at[my_rows, :], ref.end_s.at[0], ref.end_r.at[0], dev_c)
    blk_local.start()
    blk_cross.start()
    advance(h2, 3)
    advance(h3, 2)
    advance(h4, 1)

    NG[...] = jnp.zeros(NG.shape, f32)

    def norm_mid_back(i, carry):
        rows = pl.ds(i * STEP, STEP)
        grad, t = F3[rows, :], T2[rows, :].astype(f32)
        w = grad * NP[2:3, :]
        mean_w = jnp.mean(w, axis=1, keepdims=True)
        mean_wt = jnp.mean(w * t, axis=1, keepdims=True)
        dx = OG[rows, :].astype(f32) + ST[rows, 1:2] * (w - mean_w - t * mean_wt)
        F3[rows, :] = dx
        T2[rows, :] = dx.astype(bf16)
        NG[2] += fold_rows(grad * t)
        NG[3] += fold_rows(grad)
        return carry

    lax.fori_loop(0, T // STEP, norm_mid_back, 0)

    NZ = WU
    for j in range(D // COLS):
        cols = slice(j * COLS, (j + 1) * COLS)
        late = slice(D + j * COLS, D + (j + 1) * COLS)
        dm = dot_nt(T2[...], WO[cols, :])
        WD[0:T, cols] = (dm * QQ[:, cols].astype(f32)).astype(bf16)
        dn = dm * RZ[:, cols].astype(f32)
        NZ[0:T, cols] = dn.astype(bf16)
        NZ[0:T, late] = (-dn * RT[:, cols].astype(f32)).astype(bf16)
    OG[0:D, :] = dot_tn(T2[...], Y[...]).astype(bf16)
    advance(h3, 3)
    advance(h4, 2)
    advance(h5, 1)
    QQ[0:D, :] = dot_tn(HN[...], WD[0:T, :]).astype(bf16)

    sources = (OG, QQ, RZ, RT)
    pieces = functools.partial(late_pieces, half)

    def late_copies(ch, first_part):
        slot, copies = ch.k % 2, []
        for part in range(2):
            for source, off, width, at in pieces(first_part + part):
                cols = slice(half + off, half + off + width)
                copies.append(remote(
                    sources[source].at[pl.ds(0, D), cols], PR.at[slot, part, pl.ds(0, D), pl.ds(at, width)],
                    ref.pair_s.at[slot, 1 + len(copies)], ref.pair_r.at[slot, 1 + len(copies)], dev_c,
                ))
        for copy in copies:
            copy.start()
        return copies

    def late_form(ch, first_part, copies):
        for copy in copies:
            copy.wait()
        for part in range(2):
            for source, off, width, at in pieces(first_part + part):
                form(ch, part, sources[source][0:D, off : off + width], at)

    sent = late_copies(k0, 0)

    def mixer_grad(j):
        cols = slice(j * COLS, (j + 1) * COLS)
        low, high = max(0, (j - 1) * COLS), min(T, (j + 2) * COLS)
        target = PS.at[j // 2, (j % 2) if j < 2 else 1 - j % 2]
        for start, stop in ((0, low), (high, T)):
            if stop > start:
                target[start:stop, :] = jnp.zeros((stop - start, COLS), bf16)
        grad = dot_nt(NZ[low:high, :], AB[cols, :])
        for t in range(COLS // TILE):
            at = j * COLS + t * TILE
            same = SC[low:high, :] == seg[:, at : at + TILE]
            gap = (
                lax.broadcasted_iota(jnp.int32, (high - low, TILE), 0)
                - lax.broadcasted_iota(jnp.int32, (high - low, TILE), 1)
                + (low - at)
            )
            kept = jnp.where(same & (jnp.abs(gap) < WIN), grad[:, t * TILE : (t + 1) * TILE], 0.0)
            target[low:high, t * TILE : (t + 1) * TILE] = kept.astype(bf16)

    mixer_grad(0)
    mixer_grad(1)
    late_form(k0, 0, sent)
    launch(k0)
    mixer_grad(2)
    mixer_grad(3)
    mixer_copy = remote(PS.at[o], PR.at[k1.k % 2], ref.pair_s.at[k1.k % 2, 0], ref.pair_r.at[k1.k % 2, 0], dev_c)
    mixer_copy.start()

    def mixing_back(j):
        cols = slice(j * COLS, (j + 1) * COLS)
        late = slice(D + j * COLS, D + (j + 1) * COLS)
        da = dot_tn(MM[...], NZ[0:T, cols])
        db = dot_tn(MM[...], NZ[0:T, late])
        e = AB[:, late].astype(f32)
        WD[T : 2 * T, cols] = (db * e + da * AB[:, cols].astype(f32)).astype(bf16)
        WD[2 * T : 3 * T, cols] = (da * e).astype(bf16)

    advance(h5, 2)
    mixing_back(0)
    mixer_copy.wait()
    for part in range(2):
        form(k1, part, PS.at[c, part][...])
    launch(k1)
    advance(h4, 3)
    mixing_back(1)
    advance(k0, 1)
    mixing_back(2)
    RZ[0:D, :] = dot_tn(HN[...], WD[T : 2 * T, :]).astype(bf16)
    sent = late_copies(k2, 2)
    advance(h5, 3)
    RT[0:D, :] = dot_tn(HN[...], WD[2 * T : 3 * T, :]).astype(bf16)
    late_form(k2, 2, sent)
    launch(k2)
    sent = late_copies(k3, 4)

    for j in range(D // COLS):
        cols = slice(j * COLS, (j + 1) * COLS)
        F1[:, cols] = (
            dot_nt(WD[0:T, :], WQ[cols, :])
            + dot_nt(WD[T : 2 * T, :], WK[cols, :])
            + dot_nt(WD[2 * T : 3 * T, :], WV[cols, :])
        )
        if j == 0:
            advance(k1, 1)
            late_form(k3, 4, sent)
            launch(k3)
            advance(k0, 2)
    advance(k2, 1)
    advance(k1, 2)
    advance(k0, 3)

    def norm_in_back(i, carry):
        rows = pl.ds(i * STEP, STEP)
        grad, t = F1[rows, :], XB[rows, :].astype(f32)
        w = grad * NP[0:1, :]
        mean_w = jnp.mean(w, axis=1, keepdims=True)
        mean_wt = jnp.mean(w * t, axis=1, keepdims=True)
        Y[rows, :] = (F3[rows, :] + ST[rows, 0:1] * (w - mean_w - t * mean_wt)).astype(bf16)
        NG[0] += fold_rows(grad * t)
        NG[1] += fold_rows(grad)
        return carry

    lax.fori_loop(0, T // STEP, norm_in_back, 0)
    tok_local = pltpu.make_async_copy(Y.at[:, own_half], ref.o_tok.at[my_rows, :], ref.end_l.at[1])
    tok_cross = remote(Y.at[:, other_half], ref.o_tok.at[my_rows, :], ref.end_s.at[1], ref.end_r.at[1], dev_c)
    tok_local.start()
    tok_cross.start()

    NV[...] = jnp.zeros(NV.shape, f32)
    for i in range(4):
        NV[i : i + 1, :] = jnp.sum(NG[i], axis=0, keepdims=True)
    copy = remote(NV.at[:, other_half], NR.at[0], ref.norm_s.at[0], ref.norm_r.at[0], dev_c)
    copy.start()
    copy.wait()
    NR[1] = NV[:, own_half] + NR[0]
    if fused:
        copy = remote(NR.at[1], NR.at[2], ref.norm_s.at[1], ref.norm_r.at[1], dev_x)
        copy.start()
        advance(k3, 1)
        advance(k2, 2)
        copy.wait()
        NR[3] = NR[1] + NR[2]
        copy = remote(NR.at[3], NR.at[4], ref.norm_s.at[2], ref.norm_r.at[2], dev_y)
        copy.start()
        advance(k1, 3)
        advance(k3, 2)
        copy.wait()
        NZS[mz] = NR[3] + NR[4]
        copies = [
            remote(NZS.at[mz], NZS.at[mz], ref.norm_s.at[2 + j], ref.norm_r.at[2 + j], dev_z[j - 1])
            for j in range(1, nz)
        ]
        for copy in copies:
            copy.start()
        advance(k2, 3)
        advance(k3, 3)
        for copy in copies:
            copy.wait()
        total = NZS[0]
        for j in range(1, nz):
            total = total + NZS[j]
        ref.o_norm[...] = total
        for k in range(blocks + 4):
            for part in range(2):
                fin_copy(k1 if k == k1.k else chunk(k), part).wait()
    else:
        ref.o_norm[...] = NR[1]
        advance(k3, 1)
    blk_local.wait()
    blk_cross.wait()
    tok_local.wait()
    tok_cross.wait()


def unpack_kernel(sh, blocks, half, count, names, *all_refs):
    ref = SimpleNamespace(**dict(zip(names, all_refs)))
    step = ref.tok_in.shape[0] // count
    load_b = pltpu.make_async_copy(ref.o_blk, ref.blk, ref.sem.at[0, 0])
    save_b = pltpu.make_async_copy(ref.blk, ref.r_blk, ref.sem.at[1, 0])
    loads, saves = [], []
    for i in range(count):
        rows = slice(i * step, (i + 1) * step)
        loads.append(pltpu.make_async_copy(ref.o_tok.at[rows, :], ref.tok_in.at[rows, :], ref.sem.at[0, 1 + i]))
        saves.append(pltpu.make_async_copy(ref.tok_out.at[rows, :], ref.r_tok.at[rows, :], ref.sem.at[1, 1 + i]))
    load_f = pltpu.make_async_copy(ref.o_fin, ref.fin, ref.sem.at[0, 1 + count])
    load_n = pltpu.make_async_copy(ref.o_norm, ref.norm, ref.sem.at[1, 1 + count])
    loads[0].start()
    load_b.start()
    for load in loads[1:]:
        load.start()
    load_f.start()
    load_n.start()
    fin, norm = ref.fin, ref.norm
    for i in range(count):
        loads[i].wait()
        rows = slice(i * step, (i + 1) * step)
        ref.tok_out[rows, :] = ref.tok_in[rows, :].astype(f32)
        saves[i].start()
        if i == 0:
            load_b.wait()
            save_b.start()
    load_n.wait()
    for i, vector in enumerate((ref.r_gi, ref.r_si, ref.r_gm, ref.r_sm)):
        vector[...] = norm[i, :]
    load_f.wait()
    for k in range(blocks):
        cols = slice(k * COLS, (k + 1) * COLS)
        ref.r_up[:, cols] = fin[k, 0, 0:sh, :]
        ref.r_dn[:, cols] = fin[k, 1, 0:sh, :]
    low, high = fin[blocks + 1, 0], fin[blocks + 1, 1]
    first = lax.axis_index("chan") == 0
    ref.r_pair[:, 0:COLS] = jnp.where(first, low, high)
    ref.r_pair[:, COLS : 2 * COLS] = jnp.where(first, high, low)
    targets = (ref.r_wo, ref.r_q, ref.r_k, ref.r_v)
    for k, first_part in ((blocks, 0), (blocks + 2, 2), (blocks + 3, 4)):
        for part in range(2):
            for source, off, width, at in late_pieces(half, first_part + part):
                targets[source][:, off : off + width] = fin[k, part, 0:sh, at : at + width]
    for save in saves:
        save.wait()
    save_b.wait()


def unpack(T, D, FH, sh, sp, out):
    half = D // 2
    blocks = FH // COLS
    count = 4
    inputs = dict(o_blk=out.o_blk, o_tok=out.o_tok, o_norm=out.o_norm, o_fin=out.o_fin)
    vector, square, wide = (VMEM, (half,), f32), (VMEM, (sh, half), f32), (VMEM, (sh, FH), f32)
    results = dict(
        r_blk=(ANY, (2 * T, half), bf16), r_tok=(ANY, (2 * T, half), f32), r_gi=vector, r_si=vector, r_q=square,
        r_k=square, r_v=square, r_wo=square, r_gm=vector, r_sm=vector, r_up=wide, r_dn=wide,
        r_pair=(VMEM, (sp, T // 2), f32),
    )
    scratch = dict(
        blk=pltpu.VMEM((2 * T, half), bf16), tok_in=pltpu.VMEM((2 * T, half), bf16),
        tok_out=pltpu.VMEM((2 * T, half), f32), sem=pltpu.SemaphoreType.DMA((2, 2 + count)),
        fin=pltpu.VMEM(out.o_fin.shape, f32), norm=pltpu.VMEM((8, half), f32),
    )
    values = pl.pallas_call(
        functools.partial(unpack_kernel, sh, blocks, half, count, tuple(inputs) + tuple(results) + tuple(scratch)),
        out_shape=tuple(jax.ShapeDtypeStruct(shape, kind) for _, shape, kind in results.values()),
        in_specs=[ANY] * len(inputs),
        out_specs=tuple(spec for spec, _, _ in results.values()),
        scratch_shapes=list(scratch.values()),
        compiler_params=pltpu.CompilerParams(vmem_limit_bytes=63 << 20),
    )(*inputs.values())
    blk, tok, gi, si, q, k, v, wo, gm, sm, up, dn, pair = values
    return blk, tok, gi, si, q, k, v, wo.T, gm, sm, up, dn.T, pair


def gather_parts(T, D, R, nb, sp, out, pair_bias):
    half = D // 2
    parts = out.GO
    blocks = parts.shape[0] - 4
    height = lambda v, rows: v.reshape(nb, sp, v.shape[-1])[:, : rows // nb].reshape(rows, v.shape[-1])
    join = lambda chosen: jnp.concatenate(chosen, 1).astype(f32)
    scatter = lambda v: lax.psum_scatter(v, "rows", scatter_dimension=0, tiled=True)
    up = scatter(join([height(parts[k, 0], D) for k in range(blocks)]))
    down = scatter(join([height(parts[k, 1], D) for k in range(blocks)])).T
    late = join([height(parts[k, p], D) for k in (blocks, blocks + 2, blocks + 3) for p in range(2)])
    wo, q, k, v = (scatter(late[:, i * half : (i + 1) * half]) for i in range(4))
    first = lax.axis_index("chan") == 0
    low, high = (height(parts[blocks + 1, p], T) for p in range(2))
    pair = scatter(join([jnp.where(first, low, high), jnp.where(first, high, low)]))
    bias = lax.dynamic_slice(
        pair_bias, (lax.axis_index("rows") * pair.shape[0], lax.axis_index("chan") * (T // 2)), pair.shape
    )
    norms = lax.psum(out.o_norm, "rows")
    return (
        out.o_blk, out.o_tok.astype(f32), norms[0], norms[1], q, k, v, wo.T, norms[2], norms[3], up, down,
        pair * jnp.exp(bias),
    )


def on_device(
    tokens, segments, gain_in, shift_in, query_weight, key_weight, value_weight, out_weight,
    gain_mid, shift_mid, up_weight, down_weight, pair_bias, out_grad,
):
    T = segments.shape[1]
    D, FH = up_weight.shape
    R = lax.axis_size("rows")
    half = D // 2
    blocks = FH // COLS
    fused = R == 16 and D % (16 * R) == 0 and T % (16 * R) == 0
    nb = R if fused else 16
    nz = nb // 4
    sh, sp = D // nb, T // nb
    inputs = dict(
        tokens=tokens, segments=segments, gi=gain_in, si=shift_in, wq=query_weight, wk=key_weight, wv=value_weight,
        wo=out_weight, gm=gain_mid, sm=shift_mid, wu=up_weight, wd=down_weight, pair_bias=pair_bias,
        out_grad=out_grad,
    )
    near = ("segments", "gi", "si", "gm", "sm")
    outputs = dict(
        o_blk=(ANY, (2 * T, half), bf16), o_tok=(ANY, (2 * T, half), bf16), o_norm=(VMEM, (8, half), f32)
    )
    if fused:
        outputs |= dict(o_fin=(ANY, (blocks + 4, 2, sp, COLS), f32))
    else:
        outputs |= dict(GO=(ANY, (blocks + 4, 2, nb, sp, COLS), bf16))
    square, act, total = pltpu.VMEM((D, D), bf16), pltpu.VMEM((T, D), bf16), pltpu.VMEM((T, D), f32)
    small, halves = pltpu.VMEM((8, TILE), f32), pltpu.VMEM((8, half), f32)
    sems = pltpu.SemaphoreType.DMA
    scratch = dict(
        XB=act, OG=act, HN=act, G=act, Y=act, QQ=act, RT=act, RZ=act, T2=act,
        AB=pltpu.VMEM((T, 2 * D), bf16), MM=pltpu.VMEM((T, T), bf16), F1=total, F3=total,
        ST=pltpu.VMEM((T, TILE), f32), WQ=square, WK=square, WV=square, WO=square,
        WU=pltpu.VMEM((2 * D, FH), bf16), WD=pltpu.VMEM((2 * FH, D), bf16),
        SD=pltpu.VMEM((T, 2 * COLS), bf16), SC=pltpu.VMEM((T, TILE), f32),
        NP=pltpu.VMEM((8, D), f32), NPS=halves, NPR=halves,
        PS=pltpu.VMEM((2, 2, T, COLS), bf16), PR=pltpu.VMEM((2, 2, T, COLS), bf16),
        S=pltpu.VMEM((SLOTS, 2, nb, sp, COLS), bf16),
        RX=pltpu.VMEM((SLOTS, 2, nb - 1, sp, COLS), bf16) if fused else small,
        FIN=pltpu.VMEM((blocks + 4, 2, sp, COLS), f32) if fused else small,
        NG=pltpu.VMEM((4, 8, D), f32), NV=pltpu.VMEM((8, D), f32), NR=pltpu.VMEM((5, 8, half), f32),
        NZS=pltpu.VMEM((nz, 8, half), f32), PBO=pltpu.VMEM((sp, T // 2), f32),
        local_sem=sems((16,)), entry_s=sems((16,)), entry_r=sems((16,)), end_l=sems((2,)), end_s=sems((2,)),
        end_r=sems((2,)), up_l=sems((blocks // 2,)), up_s=sems((blocks // 2,)), up_r=sems((blocks // 2,)),
        down_l=sems((blocks // 2,)), down_s=sems((blocks // 2,)), down_r=sems((blocks // 2,)),
        pair_s=sems((2, 5)), pair_r=sems((2, 5)), ring_s=sems((SLOTS, 2, 6)), ring_r=sems((SLOTS, 2, 6)),
        norm_s=sems((2 + nz,)), norm_r=sems((2 + nz,)), fin_sem=sems((blocks + 4, 2)),
    )
    results = pl.pallas_call(
        functools.partial(
            block_kernel, T, D, FH, R, fused, tuple(inputs) + tuple(outputs) + tuple(scratch)
        ),
        out_shape=tuple(jax.ShapeDtypeStruct(shape, kind) for _, shape, kind in outputs.values()),
        in_specs=[VMEM if name in near else ANY for name in inputs],
        out_specs=tuple(spec for spec, _, _ in outputs.values()),
        scratch_shapes=list(scratch.values()),
        compiler_params=pltpu.CompilerParams(
            collective_id=0, has_side_effects=True, vmem_limit_bytes=63 << 20
        ),
    )(*inputs.values())
    out = SimpleNamespace(**dict(zip(outputs, results)))
    if fused:
        return unpack(T, D, FH, sh, sp, out)
    return gather_parts(T, D, R, nb, sp, out, pair_bias)


def solution(mesh):
    split, first, second, vector = P("rows", "chan"), P("chan", None), P(None, "chan"), P("chan")
    return jax.shard_map(
        on_device,
        mesh=mesh,
        in_specs=(
            split, P("rows", None), vector, vector, second, second, second, first, vector, vector, second, first,
            P(), split,
        ),
        out_specs=(
            split, split, vector, vector, split, split, split, P("chan", "rows"), vector, vector, split,
            P("chan", "rows"), split,
        ),
        check_vma=False,
    )
```

```python
import functools
from types import SimpleNamespace

import jax
import jax.numpy as jnp
from jax import lax
from jax.experimental import pallas as pl
from jax.experimental.pallas import tpu as pltpu
from jax.sharding import PartitionSpec as P

MESH = pl.DeviceIdType.MESH
ANY, VMEM = pl.BlockSpec(memory_space=pl.ANY), pl.BlockSpec(memory_space=pltpu.VMEM)
WIN = 256
EPSILON = 1e-05
TILE = 128
COLS = 256
SLOTS = 6
STEP = 256
LAGS = (2, 3, 4)
LATE = (
    ((-3, 2), (-2, 1)), (), ((-4, 3), (-2, 2), (-1, 1)), (), ((0, 1),), ((-1, 2),), ((-3, 3), (-2, 3)), ((0, 2), (1, 1)),
    ((2, 1),), ((1, 2),), ((0, 3), (2, 2)), ((3, 1),), ((-1, 3), (4, 1)), ((3, 2),), ((1, 3), (4, 2)),
    ((2, 3), (3, 3), (4, 3)),
)
f32 = jnp.float32
bf16 = jnp.bfloat16


def dot(left, right, cl=1, cr=0):
    return lax.dot_general(left, right, (((cl,), (cr,)), ((), ())), preferred_element_type=f32)


def dot_nt(left, right):
    return dot(left, right, 1, 1)


def dot_tn(left, right):
    return dot(left, right, 0, 0)


def gelu_pair(p):
    phi = 0.5 * (1.0 + lax.erf(p * 0.7071067811865476))
    return p * phi, phi + p * (jnp.exp(-0.5 * p * p) * 0.3989422804014327)


def fold_rows(v):
    return jnp.sum(v.reshape(v.shape[0] // 8, 8, v.shape[1]), axis=0)


def widths_of(half, late):
    return (COLS, half - COLS) if late % 2 == 0 else (half - COLS, COLS)


def block_kernel(T, D, FH, R, fused, names, *all_refs):
    ref = SimpleNamespace(**dict(zip(names, all_refs)))
    half = D // 2
    blocks = FH // COLS
    nb = R if fused else 16
    nz = nb // 4
    sh, sp = D // nb, T // nb
    r = lax.axis_index("rows")
    c = lax.axis_index("chan")
    o = 1 - c
    mx, my, mz = lax.rem(r, 2), lax.rem(r // 2, 2), r // 4
    z0, z1 = lax.rem(mz, 2), mz // 2
    dev_c = (r, o)
    dev_x = (r + 1 - 2 * mx, c)
    dev_y = (r + 2 - 4 * my, c)
    z0, z1 = lax.rem(mz, 2), mz // 2
    dev_z = [(lax.rem(mz + j, nz) * 4 + lax.rem(r, 4), c) for j in range(1, nz)]
    dev_z0, dev_z1 = (r + 4 - 8 * z0, c), (r + 8 - 16 * z1, c)
    dev_z0 = (r + 4 - 8 * z0, c)
    dev_z1 = (r + 8 - 16 * z1, c)
    own_half = pl.ds(pl.multiple_of(c * half, TILE), half)
    other_half = pl.ds(pl.multiple_of(o * half, TILE), half)

    XB, OG, HN, G = ref.XB, ref.OG, ref.HN, ref.G
    Y, QQ, RT, RZ, T2 = ref.Y, ref.QQ, ref.RT, ref.RZ, ref.T2
    AB, MM, F1, F3, ST = ref.AB, ref.MM, ref.F1, ref.F3, ref.ST
    WQ, WK, WV, WO, WU, WD = ref.WQ, ref.WK, ref.WV, ref.WO, ref.WU, ref.WD
    SD, SC, NP, NPS, NPR = ref.SD, ref.SC, ref.NP, ref.NPS, ref.NPR
    PS, PR, S, RX, FIN = ref.PS, ref.PR, ref.S, ref.RX, ref.FIN
    NG, NV, NR, NZS = ref.NG, ref.NV, ref.NR, ref.NZS

    def remote(src, dst, send, recv, device):
        return pltpu.make_async_remote_copy(
            src_ref=src, dst_ref=dst, send_sem=send, recv_sem=recv, device_id=device, device_id_type=MESH
        )

    my_rows, other_rows = pl.ds(c * T, T), pl.ds(o * T, T)
    h2 = T // 2
    local, cross = [], []

    def load(src, dst, away=None, there=None):
        at = len(local)
        local.append(pltpu.make_async_copy(src, dst, ref.local_sem.at[at]))
        cross.append(None if away is None else remote(away, there, ref.entry_s.at[at], ref.entry_r.at[at], dev_c))
        local[at].start()
        return at

    bias_at = [
        load(ref.pair_bias.at[0:h2, 0:D], F3.at[0:h2, :]),
        load(ref.pair_bias.at[h2:T, T - D : T], F3.at[h2:T, :]),
    ]
    tokens_at = load(
        ref.tokens.at[my_rows, :], XB.at[:, own_half], ref.tokens.at[other_rows, :], XB.at[:, own_half]
    )
    qkv_at = [
        load(src, dst.at[:, 0:half], src, dst.at[:, half:D]) for src, dst in ((ref.wk, WK), (ref.wv, WV), (ref.wq, WQ))
    ]
    wo_at = load(ref.wo, WO.at[0:half, :], ref.wo, WO.at[half:D, :])
    og_at = load(
        ref.out_grad.at[my_rows, :], OG.at[:, own_half], ref.out_grad.at[other_rows, :], OG.at[:, own_half]
    )
    wide, per_row = 2 * COLS, blocks // 2

    def up_block(i, at=0, width=wide):
        rows = pl.ds(pl.multiple_of(i // per_row * D, TILE), D)
        return rows, pl.ds(pl.multiple_of(lax.rem(i, per_row) * wide + at, COLS), width)

    def down_block(i, at=0, width=wide):
        return pl.ds(pl.multiple_of(i * wide + at, COLS), width)

    def hidden_copies(i):
        part = pl.ds(pl.multiple_of(i * COLS, COLS), COLS)
        up, down = ref.wu.at[:, part], ref.wd.at[part, :]
        return (
            pltpu.make_async_copy(up, WU.at[up_block(i, 0, COLS)], ref.up_l.at[i]),
            pltpu.make_async_copy(down, WD.at[down_block(i, 0, COLS), :], ref.down_l.at[i]),
            remote(up, WU.at[up_block(i, COLS, COLS)], ref.up_s.at[i], ref.up_r.at[i], dev_c),
            remote(down, WD.at[down_block(i, COLS, COLS), :], ref.down_s.at[i], ref.down_r.at[i], dev_c),
        )

    pbo_at = None
    if fused:
        pair_rows = pl.ds(pl.multiple_of(r * sp, 8), sp)
        pair_cols = pl.ds(pl.multiple_of(c * (T // 2), TILE), T // 2)
        pbo_at = load(ref.pair_bias.at[pair_rows, pair_cols], ref.PBO)
    hidden_weights = [hidden_copies(jnp.int32(i)) for i in range(blocks)]
    for copies in hidden_weights:
        copies[0].start()
        copies[1].start()

    NPS[...] = jnp.zeros(NPS.shape, f32)
    for i, vector in enumerate((ref.gi, ref.si, ref.gm, ref.sm)):
        NPS[i : i + 1, :] = vector[...].reshape(1, half)
    norms_cross = remote(NPS, NPR, ref.entry_s.at[15], ref.entry_r.at[15], dev_c)
    barrier = pltpu.get_barrier_semaphore()
    greeted = [dev_c] + ([dev_x, dev_y] + dev_z if fused else [])
    for device in greeted:
        pl.semaphore_signal(barrier, inc=1, device_id=device, device_id_type=MESH)
    pl.semaphore_wait(barrier, len(greeted))
    norms_cross.start()
    for at in [tokens_at] + qkv_at:
        cross[at].start()

    def ready(*chosen):
        for at in chosen:
            local[at].wait()
            if cross[at] is not None:
                cross[at].wait()

    seg = ref.segments[pl.ds(c, 1), :].astype(f32)
    SC[...] = jnp.broadcast_to(seg, (TILE, T)).T.astype(bf16)
    ready(*bias_at)
    row_id = lax.broadcasted_iota(jnp.int32, (TILE, TILE), 0)
    col_id = lax.broadcasted_iota(jnp.int32, (TILE, TILE), 1)
    for a in range(T // TILE):
        rows = slice(a * TILE, (a + 1) * TILE)
        shift = 0 if a * TILE < h2 else T - D
        for b in range(T // TILE):
            cols = slice(b * TILE, (b + 1) * TILE)
            far = abs(a - b) * TILE
            if far - TILE + 1 >= T // 2:
                MM[rows, cols] = jnp.zeros((TILE, TILE), bf16)
                continue
            same = SC[rows, :].astype(f32) == seg[:, cols]
            if far - TILE + 1 >= WIN:
                weight = jnp.ones((TILE, TILE), f32)
            else:
                weight = jnp.exp(F3[rows, b * TILE - shift : (b + 1) * TILE - shift])
                if far + TILE - 1 >= WIN:
                    inside = jnp.abs(row_id - col_id + (a - b) * TILE) < WIN
                    weight = jnp.where(inside, weight, 1.0)
            MM[rows, cols] = jnp.where(same, weight, 0.0).astype(bf16)

    norms_cross.wait()
    for i in range(4):
        NP[i : i + 1, own_half] = NPS[i : i + 1, :]
        NP[i : i + 1, other_half] = NPR[i : i + 1, :]
    ready(tokens_at)

    def norm_in(i, carry):
        rows = pl.ds(i * STEP, STEP)
        x = XB[rows, :].astype(f32)
        centred = x - jnp.mean(x, axis=1, keepdims=True)
        inv = lax.rsqrt(jnp.mean(centred * centred, axis=1, keepdims=True) + EPSILON)
        t = centred * inv
        F1[rows, :] = x
        XB[rows, :] = t.astype(bf16)
        HN[rows, :] = (t * NP[0:1, :] + NP[1:2, :]).astype(bf16)
        ST[rows, 0:1] = inv
        return carry

    lax.fori_loop(0, T // STEP, norm_in, 0)
    cross[wo_at].start()
    cross[og_at].start()
    for copies in hidden_weights:
        copies[2].start()
        copies[3].start()
    for at in qkv_at:
        local[at].wait()

    for j in range(D // COLS):
        if j * COLS <= half < (j + 1) * COLS:
            for at in qkv_at:
                cross[at].wait()
        cols = slice(j * COLS, (j + 1) * COLS)
        late = slice(D + j * COLS, D + (j + 1) * COLS)
        e = jnp.exp(dot(HN[...], WK[:, cols]))
        a = (e * dot(HN[...], WV[:, cols])).astype(bf16)
        AB[:, cols] = a
        AB[:, late] = e.astype(bf16)
        gate = jax.nn.sigmoid(dot(HN[...], WQ[:, cols]))
        inv = 1.0 / dot(MM[...], AB[:, late])
        ratio = dot(MM[...], AB[:, cols]) * inv
        y = gate * ratio
        Y[:, cols] = y.astype(bf16)
        QQ[:, cols] = (y * (1.0 - gate)).astype(bf16)
        RT[:, cols] = ratio.astype(bf16)
        RZ[:, cols] = (gate * inv).astype(bf16)

    ready(wo_at)
    for i in range(T // STEP):
        rows = slice(i * STEP, (i + 1) * STEP)
        x = F1[rows, :] + dot(Y[rows, :], WO[...])
        F1[rows, :] = x
        centred = x - jnp.mean(x, axis=1, keepdims=True)
        inv = lax.rsqrt(jnp.mean(centred * centred, axis=1, keepdims=True) + EPSILON)
        t = centred * inv
        T2[rows, :] = t.astype(bf16)
        G[rows, :] = (t * NP[2:3, :] + NP[3:4, :]).astype(bf16)
        ST[rows, 1:2] = inv
        F3[rows, :] = jnp.zeros((STEP, D), f32)
    ready(og_at)
    if fused:
        ready(pbo_at)

    ex, ey, ez0, ez1 = (mx, dev_x), (my, dev_y), (z0, dev_z0), (z1, dev_z1)
    halvings = (((ex, ey), (ey, ex)), ((ex, ez0, ez1, ey), (ey, ez0, ez1, ex)))

    def chunk(k, wind=(0, 0), widths=(COLS, COLS)):
        return SimpleNamespace(
            k=k, slot=lax.rem(k, SLOTS), wind=wind, widths=widths, height=sh, counts=(nz, nz),
            index=(lambda z: z, lambda z: z), valid=(None, None), late=False,
        )

    def late_chunk(late):
        widths = (COLS, COLS) if late == 2 else widths_of(half, late if late < 2 else late - 1)
        ch = chunk(jnp.int32(blocks + late), widths=widths)
        ch.late = True
        if late == 2:
            ch.height = sp
        if late == 2 and fused:
            ch.counts = (2, 3)
            ch.index = (lambda z: lax.rem(z, 2), lambda z: lax.rem(z + 3 - c, 3))
            ch.valid = (mz // 2 == c, mz != 3 * o)
        return ch

    def place(ch, b, part):
        if not fused:
            return b
        bx, by, bz = b % 2, (b // 2) % 2, b // 4
        outer, inner = (bx, by) if part == 0 else (by, bx)
        if ch.wind[part]:
            return ((outer * 2 + bz % 2) * 2 + bz // 2) * 2 + inner
        return (outer * 2 + inner) * ch.counts[part] + bz

    def form(ch, part, own, total_rows):
        width, height = ch.widths[part], ch.height
        for b in range(total_rows // height):
            rows = slice(b * height, (b + 1) * height)
            at = place(ch, b, part) * height
            S[ch.slot, part, at : at + height, 0:width] = (
                own[rows, :].astype(bf16) + PR[lax.rem(ch.k, 2), part, rows, 0:width]
            )

    def block_rows(ch, first, count):
        return pl.ds(pl.multiple_of(first * ch.height, 16), count * ch.height)

    def stages(ch, part):
        return 4 if ch.wind[part] else 3

    def span(ch, part, n):
        base, size = 0, nb if ch.wind[part] else 4 * ch.counts[part]
        for bit, _ in halvings[ch.wind[part]][part][: n - 1]:
            size //= 2
            base = base + bit * size
        return base, size

    def landing(ch, part, n):
        if ch.wind[part]:
            return (0, nb // 2, 3 * nb // 4, nb - 2)[n - 1]
        return (0, 2, 3)[n - 1] * ch.counts[part]

    def stage(ch, part, n):
        cols, copies = pl.ds(0, ch.widths[part]), []
        base, size = span(ch, part, n)
        plan = halvings[ch.wind[part]][part]
        if n <= len(plan):
            bit, device = plan[n - 1]
            moves = [(base + (1 - bit) * (size // 2), landing(ch, part, n), size // 2, device)]
        else:
            moves = [
                (base + ch.index[part](lax.rem(mz + j, nz)), landing(ch, part, n) + j - 1, 1, dev_z[j - 1])
                for j in range(1, nz)
            ]
        for i, (first, at, count, device) in enumerate(moves):
            copies.append(remote(
                S.at[ch.slot, part, block_rows(ch, first, count), cols],
                RX.at[ch.slot, part, block_rows(ch, at, count), cols],
                ref.ring_s.at[ch.slot, part, n - 1 + i], ref.ring_r.at[ch.slot, part, n - 1 + i], device,
            ))
        return copies

    def whole(ch):
        return pltpu.make_async_copy(S.at[ch.slot], ref.GO.at[ch.k], ref.ring_s.at[ch.slot, 0, 0])

    def fin_copy(ch, part):
        rows, cols = pl.ds(0, ch.height), pl.ds(0, ch.widths[part])
        return pltpu.make_async_copy(
            FIN.at[lax.rem(ch.k, SLOTS), part, rows, cols], ref.o_fin.at[ch.k, part, rows, cols], ref.fin_sem.at[ch.k, part]
        )

    def launch(ch):
        if not fused:
            whole(ch).start()
            return
        for part in range(2):
            for copy in stage(ch, part, 1):
                copy.start()

    def advance(ch, n):
        if not fused:
            if n == 1:
                whole(ch).wait()
            return
        for part in range(2):
            last = stages(ch, part)
            if n > last:
                continue
            for copy in stage(ch, part, n):
                copy.wait()
            cols, at = slice(0, ch.widths[part]), landing(ch, part, n)
            base, size = span(ch, part, n + 1)
            if n < last:
                S[ch.slot, part, block_rows(ch, base, size), cols] += RX[ch.slot, part, block_rows(ch, at, size), cols]
                for copy in stage(ch, part, n + 1):
                    copy.start()
                continue
            mine = base if ch.wind[part] else base + ch.index[part](mz)
            total = S[ch.slot, part, block_rows(ch, mine, 1), cols].astype(f32)
            for j in range(1 if ch.wind[part] else nz - 1):
                total = total + RX[ch.slot, part, block_rows(ch, at + j, 1), cols].astype(f32)
            if ch.valid[part] is not None:
                bias = ref.PBO[:, pl.ds(pl.multiple_of(pair_part[part] * COLS, COLS), COLS)]
                total = jnp.where(ch.valid[part], total * jnp.exp(bias), 0.0)
            if ch.late:
                fin_copy(chunk(ch.k - SLOTS), part).wait()
            FIN[lax.rem(ch.k, SLOTS), part, 0 : ch.height, cols] = total
            fin_copy(ch, part).start()

    def pair_copy(slot):
        return remote(PS.at[slot], PR.at[slot], ref.pair_s.at[slot, 0], ref.pair_r.at[slot, 0], dev_c)

    def hidden_round(i, carry):
        for copy in hidden_copies(i):
            copy.wait()
        up_at, down_at = up_block(i), down_block(i)
        s, slope = gelu_pair(dot(G[...], WU[up_at]))
        SD[:, 0:wide] = s.astype(bf16)
        SD[:, wide:] = (dot_nt(OG[...], WD[down_at, :]) * slope).astype(bf16)
        for n, lag in enumerate(LAGS):
            pl.when(i >= lag)(functools.partial(advance, chunk(i - lag), n + 1))
        slot = lax.rem(i, 2)
        PS[slot, 0] = dot_tn(G[...], SD[:, wide + COLS :]).astype(bf16)
        PS[slot, 1] = dot_tn(OG[...], SD[:, COLS:wide]).astype(bf16)
        pair_copy(slot).start()
        F1[...] += dot(SD[:, 0:wide], WD[down_at, :])
        F3[...] += dot_nt(SD[:, wide:], WU[up_at])
        up = dot_tn(G[...], SD[:, wide : wide + COLS])
        down = dot_tn(OG[...], SD[:, 0:COLS])
        pair_copy(slot).wait()
        ch = chunk(i)
        form(ch, 0, up, D)
        form(ch, 1, down, D)
        launch(ch)
        return carry

    lax.fori_loop(0, blocks, hidden_round, 0)
    pair_part = (c, 1 - c)

    def pump(*steps):
        for late, n in steps:
            if late >= 0:
                advance(late_chunk(late), n)
            else:
                advance(chunk(jnp.int32(blocks + late)), n)

    NG[...] = jnp.zeros(NG.shape, f32)

    def norm_mid_back(i, carry):
        rows = pl.ds(i * STEP, STEP)
        G[rows, :] = F1[rows, :].astype(bf16)
        grad, t = F3[rows, :], T2[rows, :].astype(f32)
        w = grad * NP[2:3, :]
        mean_w = jnp.mean(w, axis=1, keepdims=True)
        mean_wt = jnp.mean(w * t, axis=1, keepdims=True)
        dx = OG[rows, :].astype(f32) + ST[rows, 1:2] * (w - mean_w - t * mean_wt)
        F3[rows, :] = dx
        T2[rows, :] = dx.astype(bf16)
        NG[2] += fold_rows(grad * t)
        NG[3] += fold_rows(grad)
        return carry

    lax.fori_loop(0, T // STEP, norm_mid_back, 0)
    blk_local = pltpu.make_async_copy(G.at[:, own_half], ref.o_blk.at[my_rows, :], ref.end_l.at[0])
    blk_cross = remote(G.at[:, other_half], ref.o_blk.at[my_rows, :], ref.end_s.at[0], ref.end_r.at[0], dev_c)
    blk_local.start()
    blk_cross.start()
    pump(*LATE[0])

    half_cols = (slice(0, half), slice(half, D))

    def late_copies(late, source):
        ch, copies, at = late_chunk(late), [], half
        for part, width in enumerate(ch.widths):
            copies.append(remote(
                source.at[pl.ds(0, D), pl.ds(at, width)], PR.at[late % 2, part, :, pl.ds(0, width)],
                ref.pair_s.at[late % 2, 1 + part], ref.pair_r.at[late % 2, 1 + part], dev_c,
            ))
            at += width
        for copy in copies:
            copy.start()
        return copies

    def late_form(late, source, copies):
        for copy in copies:
            copy.wait()
        ch, at = late_chunk(late), 0
        for part, width in enumerate(ch.widths):
            form(ch, part, source.at[pl.ds(0, D), pl.ds(at, width)], D)
            at += width
        launch(ch)

    NZ = WU

    def gate_back(j):
        cols = slice(j * COLS, (j + 1) * COLS)
        late = slice(D + j * COLS, D + (j + 1) * COLS)
        dm = dot_nt(T2[...], WO[cols, :])
        QQ[:, cols] = (dm * QQ[:, cols].astype(f32)).astype(bf16)
        dn = dm * RZ[:, cols].astype(f32)
        NZ[0:T, cols] = dn.astype(bf16)
        NZ[0:T, late] = (-dn * RT[:, cols].astype(f32)).astype(bf16)

    OG[0:D, :] = dot_tn(T2[...], Y[...]).astype(bf16)
    sent = late_copies(0, OG)
    gate_back(0)
    gate_back(1)
    pump(*LATE[1])
    late_form(0, OG, sent)
    gate_back(2)
    RZ[0:D, :] = dot_tn(HN[...], QQ[...]).astype(bf16)
    sent = late_copies(1, RZ)
    pump(*LATE[2])

    def mixer_grad(j):
        cols = slice(j * COLS, (j + 1) * COLS)
        low, high = max(0, (j - 1) * COLS), min(T, (j + 2) * COLS)
        target = PS.at[j // 2, j if j < 2 else 3 - j]
        grad = dot_nt(NZ[low:high, :], AB[cols, :])
        for t in range(COLS // TILE):
            at = j * COLS + t * TILE
            same = SC[low:high, :].astype(f32) == seg[:, at : at + TILE]
            gap = (
                lax.broadcasted_iota(jnp.int32, (high - low, TILE), 0)
                - lax.broadcasted_iota(jnp.int32, (high - low, TILE), 1)
                + (low - at)
            )
            kept = jnp.where(same & (jnp.abs(gap) < WIN), grad[:, t * TILE : (t + 1) * TILE], 0.0)
            target[0 : high - low, t * TILE : (t + 1) * TILE] = kept.astype(bf16)

    mixer_rows = (2 * COLS, 3 * COLS)
    mixer_grad(0)
    mixer_grad(1)
    pump(*LATE[3])
    late_form(1, RZ, sent)
    mixer_grad(2)
    mixer_grad(3)
    mixer_copies = [
        remote(
            PS.at[o, part, pl.ds(0, mixer_rows[part]), :], PR.at[0, part, pl.ds(0, mixer_rows[part]), :],
            ref.pair_s.at[0, 3 + part], ref.pair_r.at[0, 3 + part], dev_c,
        )
        for part in range(2)
    ]
    for copy in mixer_copies:
        copy.start()
    pump(*LATE[4])

    def mixing_back(j):
        cols = slice(j * COLS, (j + 1) * COLS)
        late = slice(D + j * COLS, D + (j + 1) * COLS)
        da = dot_tn(MM[...], NZ[0:T, cols])
        db = dot_tn(MM[...], NZ[0:T, late])
        e = AB[:, late].astype(f32)
        T2[:, cols] = (db * e + da * AB[:, cols].astype(f32)).astype(bf16)
        Y[:, cols] = (da * e).astype(bf16)

    mixing_back(0)
    pump(*LATE[5])
    for copy in mixer_copies:
        copy.wait()
    for part in range(2):
        form(late_chunk(2), part, PS.at[c, part], mixer_rows[part])
    launch(late_chunk(2))
    mixing_back(1)
    mixing_back(2)
    pump(*LATE[6])
    RT[0:D, :] = dot_tn(HN[...], T2[...]).astype(bf16)
    sent = late_copies(3, RT)
    pump(*LATE[7])
    AB[0:D, 0:D] = dot_tn(HN[...], Y[...]).astype(bf16)
    pump(*LATE[8])
    late_form(3, RT, sent)
    sent = late_copies(4, AB)

    def norm_in_grad(j):
        cols = slice(j * COLS, (j + 1) * COLS)
        F1[:, cols] = dot_nt(QQ[...], WQ[cols, :]) + dot_nt(T2[...], WK[cols, :]) + dot_nt(Y[...], WV[cols, :])

    norm_in_grad(0)
    pump(*LATE[9])
    late_form(4, AB, sent)
    norm_in_grad(1)
    pump(*LATE[10])
    norm_in_grad(2)
    pump(*LATE[11])

    def norm_in_back(i, carry):
        rows = pl.ds(i * STEP, STEP)
        grad, t = F1[rows, :], XB[rows, :].astype(f32)
        w = grad * NP[0:1, :]
        mean_w = jnp.mean(w, axis=1, keepdims=True)
        mean_wt = jnp.mean(w * t, axis=1, keepdims=True)
        HN[rows, :] = (F3[rows, :] + ST[rows, 0:1] * (w - mean_w - t * mean_wt)).astype(bf16)
        NG[0] += fold_rows(grad * t)
        NG[1] += fold_rows(grad)
        return carry

    lax.fori_loop(0, T // STEP, norm_in_back, 0)
    tok_local = pltpu.make_async_copy(HN.at[:, own_half], ref.o_tok.at[my_rows, :], ref.end_l.at[1])
    tok_cross = remote(HN.at[:, other_half], ref.o_tok.at[my_rows, :], ref.end_s.at[1], ref.end_r.at[1], dev_c)
    tok_local.start()
    tok_cross.start()

    NV[...] = jnp.zeros(NV.shape, f32)
    for i in range(4):
        NV[i : i + 1, :] = jnp.sum(NG[i], axis=0, keepdims=True)
    copy = remote(NV.at[:, other_half], NR.at[0], ref.norm_s.at[0], ref.norm_r.at[0], dev_c)
    copy.start()
    pump(*LATE[12])
    copy.wait()
    NR[1] = NV[:, own_half] + NR[0]
    if fused:
        copy = remote(NR.at[1], NR.at[2], ref.norm_s.at[1], ref.norm_r.at[1], dev_x)
        copy.start()
        pump(*LATE[13])
        copy.wait()
        NR[3] = NR[1] + NR[2]
        copy = remote(NR.at[3], NR.at[4], ref.norm_s.at[2], ref.norm_r.at[2], dev_y)
        copy.start()
        pump(*LATE[14])
        copy.wait()
        NZS[mz] = NR[3] + NR[4]
        copies = [
            remote(NZS.at[mz], NZS.at[mz], ref.norm_s.at[2 + j], ref.norm_r.at[2 + j], dev_z[j - 1])
            for j in range(1, nz)
        ]
        for copy in copies:
            copy.start()
    pump(*LATE[15])
    if fused:
        for copy in copies:
            copy.wait()
        total = NZS[0]
        for j in range(1, nz):
            total = total + NZS[j]
        ref.o_norm[...] = total
        for k in range(blocks + 5 - SLOTS, blocks + 5):
            for part in range(2):
                fin_copy(late_chunk(k - blocks) if k >= blocks else chunk(jnp.int32(k)), part).wait()
    else:
        pump((4, 1))
        ref.o_norm[...] = NR[1]
    blk_local.wait()
    blk_cross.wait()
    tok_local.wait()
    tok_cross.wait()


def unpack_kernel(sh, blocks, half, count, names, *all_refs):
    ref = SimpleNamespace(**dict(zip(names, all_refs)))
    step = ref.tok_in.shape[0] // count
    load_b = pltpu.make_async_copy(ref.o_blk, ref.blk, ref.sem.at[0, 0])
    save_b = pltpu.make_async_copy(ref.blk, ref.r_blk, ref.sem.at[1, 0])
    loads, saves = [], []
    for i in range(count):
        rows = slice(i * step, (i + 1) * step)
        loads.append(pltpu.make_async_copy(ref.o_tok.at[rows, :], ref.tok_in.at[rows, :], ref.sem.at[0, 1 + i]))
        saves.append(pltpu.make_async_copy(ref.tok_out.at[rows, :], ref.r_tok.at[rows, :], ref.sem.at[1, 1 + i]))
    load_f = pltpu.make_async_copy(ref.o_fin, ref.fin, ref.sem.at[0, 1 + count])
    load_n = pltpu.make_async_copy(ref.o_norm, ref.norm, ref.sem.at[1, 1 + count])
    loads[0].start()
    load_b.start()
    for load in loads[1:]:
        load.start()
    load_f.start()
    load_n.start()
    fin, norm = ref.fin, ref.norm
    for i in range(count):
        loads[i].wait()
        rows = slice(i * step, (i + 1) * step)
        ref.tok_out[rows, :] = ref.tok_in[rows, :].astype(f32)
        saves[i].start()
        if i == 0:
            load_b.wait()
            save_b.start()
    load_n.wait()
    for i, vector in enumerate((ref.r_gi, ref.r_si, ref.r_gm, ref.r_sm)):
        vector[...] = norm[i, :]
    load_f.wait()
    for k in range(blocks):
        cols = slice(k * COLS, (k + 1) * COLS)
        ref.r_up[:, cols] = fin[k, 0, 0:sh, :]
        ref.r_dn[:, cols] = fin[k, 1, 0:sh, :]
    low, high = fin[blocks + 2, 0], fin[blocks + 2, 1]
    first = lax.axis_index("chan") == 0
    ref.r_pair[:, 0:COLS] = jnp.where(first, low, high)
    ref.r_pair[:, COLS : 2 * COLS] = jnp.where(first, high, low)
    for late, target in ((0, ref.r_wo), (1, ref.r_q), (3, ref.r_k), (4, ref.r_v)):
        at = 0
        for part, width in enumerate(widths_of(half, late if late < 2 else late - 1)):
            target[:, at : at + width] = fin[blocks + late, part, 0:sh, 0:width]
            at += width
    for save in saves:
        save.wait()
    save_b.wait()


def unpack(T, D, FH, sh, sp, out):
    half = D // 2
    blocks = FH // COLS
    count = 4
    inputs = dict(o_blk=out.o_blk, o_tok=out.o_tok, o_norm=out.o_norm, o_fin=out.o_fin)
    vector, square, wide = (VMEM, (half,), f32), (VMEM, (sh, half), f32), (VMEM, (sh, FH), f32)
    results = dict(
        r_blk=(ANY, (2 * T, half), bf16), r_tok=(ANY, (2 * T, half), f32), r_gi=vector, r_si=vector, r_q=square,
        r_k=square, r_v=square, r_wo=square, r_gm=vector, r_sm=vector, r_up=wide, r_dn=wide,
        r_pair=(VMEM, (sp, T // 2), f32),
    )
    scratch = dict(
        blk=pltpu.VMEM((2 * T, half), bf16), tok_in=pltpu.VMEM((2 * T, half), bf16),
        tok_out=pltpu.VMEM((2 * T, half), f32), sem=pltpu.SemaphoreType.DMA((2, 2 + count)),
        fin=pltpu.VMEM(out.o_fin.shape, f32), norm=pltpu.VMEM((8, half), f32),
    )
    values = pl.pallas_call(
        functools.partial(unpack_kernel, sh, blocks, half, count, tuple(inputs) + tuple(results) + tuple(scratch)),
        out_shape=tuple(jax.ShapeDtypeStruct(shape, kind) for _, shape, kind in results.values()),
        in_specs=[ANY] * len(inputs),
        out_specs=tuple(spec for spec, _, _ in results.values()),
        scratch_shapes=list(scratch.values()),
        compiler_params=pltpu.CompilerParams(vmem_limit_bytes=63 << 20),
    )(*inputs.values())
    blk, tok, gi, si, q, k, v, wo, gm, sm, up, dn, pair = values
    return blk, tok, gi, si, q, k, v, wo.T, gm, sm, up, dn.T, pair


def gather_parts(T, D, out, pair_bias):
    half = D // 2
    parts = out.GO
    blocks = parts.shape[0] - 5
    join = lambda chosen: jnp.concatenate(chosen, 1).astype(f32)
    scatter = lambda v: lax.psum_scatter(v, "rows", scatter_dimension=0, tiled=True)
    up = scatter(join([parts[k, 0] for k in range(blocks)]))
    down = scatter(join([parts[k, 1] for k in range(blocks)])).T
    late = []
    for i in (0, 1, 3, 4):
        widths = widths_of(half, i if i < 2 else i - 1)
        late.append(scatter(join([parts[blocks + i, p, :, 0:width] for p, width in enumerate(widths)])))
    wo, q, k, v = late
    first = lax.axis_index("chan") == 0
    spread = []
    for p, rows in ((0, 2 * COLS), (1, 3 * COLS)):
        held, rest = parts[blocks + 2, p, 0:rows], jnp.zeros((T - rows, COLS), bf16)
        spread.append(jnp.where(first, jnp.concatenate([held, rest]), jnp.concatenate([rest, held])))
    low, high = spread
    pair = scatter(join([jnp.where(first, low, high), jnp.where(first, high, low)]))
    bias = lax.dynamic_slice(
        pair_bias, (lax.axis_index("rows") * pair.shape[0], lax.axis_index("chan") * (T // 2)), pair.shape
    )
    norms = lax.psum(out.o_norm, "rows")
    return (
        out.o_blk, out.o_tok.astype(f32), norms[0], norms[1], q, k, v, wo.T, norms[2], norms[3], up, down,
        pair * jnp.exp(bias),
    )


def on_device(
    tokens, segments, gain_in, shift_in, query_weight, key_weight, value_weight, out_weight,
    gain_mid, shift_mid, up_weight, down_weight, pair_bias, out_grad,
):
    T = segments.shape[1]
    D, FH = up_weight.shape
    R = lax.axis_size("rows")
    half = D // 2
    blocks = FH // COLS
    fused = R == 16 and D % (16 * R) == 0 and T % (16 * R) == 0
    nb = R if fused else 16
    nz = nb // 4
    sh, sp = D // nb, T // nb
    inputs = dict(
        tokens=tokens, segments=segments, gi=gain_in, si=shift_in, wq=query_weight, wk=key_weight, wv=value_weight,
        wo=out_weight, gm=gain_mid, sm=shift_mid, wu=up_weight, wd=down_weight, pair_bias=pair_bias,
        out_grad=out_grad,
    )
    near = ("segments", "gi", "si", "gm", "sm")
    outputs = dict(
        o_blk=(ANY, (2 * T, half), bf16), o_tok=(ANY, (2 * T, half), bf16), o_norm=(VMEM, (8, half), f32)
    )
    if fused:
        outputs |= dict(o_fin=(ANY, (blocks + 5, 2, sp, COLS), f32))
    else:
        outputs |= dict(GO=(ANY, (blocks + 5, 2, D, COLS), bf16))
    square, act, total = pltpu.VMEM((D, D), bf16), pltpu.VMEM((T, D), bf16), pltpu.VMEM((T, D), f32)
    small, halves = pltpu.VMEM((8, TILE), f32), pltpu.VMEM((8, half), f32)
    sems = pltpu.SemaphoreType.DMA
    scratch = dict(
        XB=act, OG=act, HN=act, G=act, Y=act, QQ=act, RT=act, RZ=act, T2=act,
        AB=pltpu.VMEM((T, 2 * D), bf16), MM=pltpu.VMEM((T, T), bf16), F1=total, F3=total,
        ST=pltpu.VMEM((T, TILE), f32), WQ=square, WK=square, WV=square, WO=square,
        WU=pltpu.VMEM((2 * D, FH), bf16), WD=pltpu.VMEM((2 * FH, D), bf16),
        SD=pltpu.VMEM((T, 4 * COLS), bf16), SC=pltpu.VMEM((T, TILE), bf16),
        NP=pltpu.VMEM((8, D), f32), NPS=halves, NPR=halves,
        PS=pltpu.VMEM((2, 2, D, COLS), bf16), PR=pltpu.VMEM((2, 2, D, COLS), bf16),
        S=pltpu.VMEM((SLOTS, 2, D, COLS), bf16),
        RX=pltpu.VMEM((SLOTS, 2, D, COLS), bf16) if fused else small,
        FIN=pltpu.VMEM((SLOTS, 2, sp, COLS), f32) if fused else small,
        NG=pltpu.VMEM((4, 8, D), f32), NV=pltpu.VMEM((8, D), f32), NR=pltpu.VMEM((5, 8, half), f32),
        NZS=pltpu.VMEM((nz, 8, half), f32), PBO=pltpu.VMEM((sp, T // 2), f32),
        local_sem=sems((16,)), entry_s=sems((16,)), entry_r=sems((16,)), end_l=sems((2,)), end_s=sems((2,)),
        end_r=sems((2,)), up_l=sems((blocks,)), up_s=sems((blocks,)), up_r=sems((blocks,)),
        down_l=sems((blocks,)), down_s=sems((blocks,)), down_r=sems((blocks,)),
        pair_s=sems((2, 5)), pair_r=sems((2, 5)), ring_s=sems((SLOTS, 2, 6)), ring_r=sems((SLOTS, 2, 6)),
        norm_s=sems((2 + nz,)), norm_r=sems((2 + nz,)), fin_sem=sems((blocks + 5, 2)),
    )
    results = pl.pallas_call(
        functools.partial(
            block_kernel, T, D, FH, R, fused, tuple(inputs) + tuple(outputs) + tuple(scratch)
        ),
        out_shape=tuple(jax.ShapeDtypeStruct(shape, kind) for _, shape, kind in outputs.values()),
        in_specs=[VMEM if name in near else ANY for name in inputs],
        out_specs=tuple(spec for spec, _, _ in outputs.values()),
        scratch_shapes=list(scratch.values()),
        compiler_params=pltpu.CompilerParams(
            collective_id=0, has_side_effects=True, vmem_limit_bytes=63 << 20
        ),
    )(*inputs.values())
    out = SimpleNamespace(**dict(zip(outputs, results)))
    if fused:
        return unpack(T, D, FH, sh, sp, out)
    return gather_parts(T, D, out, pair_bias)


def solution(mesh):
    split, first, second, vector = P("rows", "chan"), P("chan", None), P(None, "chan"), P("chan")
    return jax.shard_map(
        on_device,
        mesh=mesh,
        in_specs=(
            split, P("rows", None), vector, vector, second, second, second, first, vector, vector, second, first,
            P(), split,
        ),
        out_specs=(
            split, split, vector, vector, split, split, split, P("chan", "rows"), vector, vector, split,
            P("chan", "rows"), split,
        ),
        check_vma=False,
    )
```

```python
import functools
from types import SimpleNamespace

import jax
import jax.numpy as jnp
from jax import lax
from jax.experimental import pallas as pl
from jax.experimental.pallas import tpu as pltpu
from jax.sharding import PartitionSpec as P

MESH = pl.DeviceIdType.MESH
ANY, VMEM = pl.BlockSpec(memory_space=pl.ANY), pl.BlockSpec(memory_space=pltpu.VMEM)
WIN = 256
EPSILON = 1e-05
TILE = 128
COLS = 256
SLOTS = 5
FINALS = 6
STEP = 256
LAGS = (2, 3, 4)
LATE = (
    ((-3, 2), (-2, 1)), ((-4, 3),), ((-2, 2), (-1, 1)), ((-3, 3),), ((0, 1),), ((-1, 2),), ((-2, 3),), ((0, 2), (1, 1)),
    ((2, 1),), ((-1, 3), (1, 2)), ((0, 3), (2, 2)), (), ((3, 1), (1, 3)), ((4, 1), (3, 2)), ((2, 3), (4, 2)),
    ((3, 3), (4, 3)),
)
f32 = jnp.float32
bf16 = jnp.bfloat16


def dot(left, right, cl=1, cr=0):
    return lax.dot_general(left, right, (((cl,), (cr,)), ((), ())), preferred_element_type=f32)


def dot_nt(left, right):
    return dot(left, right, 1, 1)


def dot_tn(left, right):
    return dot(left, right, 0, 0)


def gelu_pair(p):
    phi = 0.5 * (1.0 + lax.erf(p * 0.7071067811865476))
    return p * phi, phi + p * (jnp.exp(-0.5 * p * p) * 0.3989422804014327)


def fold_rows(v):
    return jnp.sum(v.reshape(v.shape[0] // 8, 8, v.shape[1]), axis=0)


def widths_of(half, late):
    return (COLS, half - COLS) if late % 2 == 0 else (half - COLS, COLS)


def block_kernel(T, D, FH, R, fused, names, *all_refs):
    ref = SimpleNamespace(**dict(zip(names, all_refs)))
    half = D // 2
    blocks = FH // COLS
    nb = R if fused else 16
    nz = nb // 4
    sh, sp = D // nb, T // nb
    r = lax.axis_index("rows")
    c = lax.axis_index("chan")
    o = 1 - c
    mx, my, mz = lax.rem(r, 2), lax.rem(r // 2, 2), r // 4
    z0, z1 = lax.rem(mz, 2), mz // 2
    dev_c = (r, o)
    dev_x = (r + 1 - 2 * mx, c)
    dev_y = (r + 2 - 4 * my, c)
    z0, z1 = lax.rem(mz, 2), mz // 2
    dev_z = [(lax.rem(mz + j, nz) * 4 + lax.rem(r, 4), c) for j in range(1, nz)]
    dev_z0, dev_z1 = (r + 4 - 8 * z0, c), (r + 8 - 16 * z1, c)
    dev_z0 = (r + 4 - 8 * z0, c)
    dev_z1 = (r + 8 - 16 * z1, c)
    own_half = pl.ds(pl.multiple_of(c * half, TILE), half)
    other_half = pl.ds(pl.multiple_of(o * half, TILE), half)

    XB, OG, HN, G = ref.XB, ref.OG, ref.HN, ref.G
    Y, QQ, RT, RZ, T2 = ref.Y, ref.QQ, ref.RT, ref.RZ, ref.T2
    AB, MM, F1, F3, ST = ref.AB, ref.MM, ref.F1, ref.F3, ref.ST
    WQ, WK, WV, WO, WU, WD = ref.WQ, ref.WK, ref.WV, ref.WO, ref.WU, ref.WD
    SD, SC, NP, NPS, NPR = ref.SD, ref.SC, ref.NP, ref.NPS, ref.NPR
    PS, PR, S, RX, FIN = ref.PS, ref.PR, ref.S, ref.RX, ref.FIN
    NG, NV, NR, NZS = ref.NG, ref.NV, ref.NR, ref.NZS

    def remote(src, dst, send, recv, device):
        return pltpu.make_async_remote_copy(
            src_ref=src, dst_ref=dst, send_sem=send, recv_sem=recv, device_id=device, device_id_type=MESH
        )

    barrier = pltpu.get_barrier_semaphore()
    greeted = [dev_c] + ([dev_x, dev_y] + dev_z if fused else [])
    for device in greeted:
        pl.semaphore_signal(barrier, inc=1, device_id=device, device_id_type=MESH)

    my_rows, other_rows = pl.ds(c * T, T), pl.ds(o * T, T)
    h2 = T // 2
    local, cross = [], []

    def load(src, dst, away=None, there=None):
        at = len(local)
        local.append(pltpu.make_async_copy(src, dst, ref.local_sem.at[at]))
        cross.append(None if away is None else remote(away, there, ref.entry_s.at[at], ref.entry_r.at[at], dev_c))
        local[at].start()
        return at

    bias_at = [
        load(ref.pair_bias.at[0:h2, 0:D], F3.at[0:h2, :]),
        load(ref.pair_bias.at[h2:T, T - D : T], F3.at[h2:T, :]),
    ]
    tokens_at = load(
        ref.tokens.at[my_rows, :], XB.at[:, own_half], ref.tokens.at[other_rows, :], XB.at[:, own_half]
    )
    qkv_at = [
        load(src, dst.at[:, 0:half], src, dst.at[:, half:D]) for src, dst in ((ref.wk, WK), (ref.wv, WV), (ref.wq, WQ))
    ]
    wo_at = load(ref.wo, WO.at[0:half, :], ref.wo, WO.at[half:D, :])
    og_at = load(
        ref.out_grad.at[my_rows, :], OG.at[:, own_half], ref.out_grad.at[other_rows, :], OG.at[:, own_half]
    )
    wide, per_row = 2 * COLS, blocks // 2

    def up_block(i, at=0, width=wide):
        rows = pl.ds(pl.multiple_of(i // per_row * D, TILE), D)
        return rows, pl.ds(pl.multiple_of(lax.rem(i, per_row) * wide + at, COLS), width)

    def down_block(i, at=0, width=wide):
        return pl.ds(pl.multiple_of(i * wide + at, COLS), width)

    def hidden_copies(i):
        part = pl.ds(pl.multiple_of(i * COLS, COLS), COLS)
        up, down = ref.wu.at[:, part], ref.wd.at[part, :]
        return (
            pltpu.make_async_copy(up, WU.at[up_block(i, 0, COLS)], ref.up_l.at[i]),
            pltpu.make_async_copy(down, WD.at[down_block(i, 0, COLS), :], ref.down_l.at[i]),
            remote(up, WU.at[up_block(i, COLS, COLS)], ref.up_s.at[i], ref.up_r.at[i], dev_c),
            remote(down, WD.at[down_block(i, COLS, COLS), :], ref.down_s.at[i], ref.down_r.at[i], dev_c),
        )

    pbo_at = None
    if fused:
        pair_rows = pl.ds(pl.multiple_of(r * sp, 8), sp)
        pair_cols = pl.ds(pl.multiple_of(c * (T // 2), TILE), T // 2)
        pbo_at = load(ref.pair_bias.at[pair_rows, pair_cols], ref.PBO)

    NPS[...] = jnp.zeros(NPS.shape, f32)
    for i, vector in enumerate((ref.gi, ref.si, ref.gm, ref.sm)):
        NPS[i : i + 1, :] = vector[...].reshape(1, half)
    norms_cross = remote(NPS, NPR, ref.entry_s.at[15], ref.entry_r.at[15], dev_c)
    pl.semaphore_wait(barrier, len(greeted))
    cross[tokens_at].start()
    norms_cross.start()
    for at in qkv_at:
        cross[at].start()
    hidden_weights = [hidden_copies(jnp.int32(i)) for i in range(blocks)]
    for copies in hidden_weights:
        copies[0].start()
        copies[1].start()

    def ready(*chosen):
        for at in chosen:
            local[at].wait()
            if cross[at] is not None:
                cross[at].wait()

    seg = ref.segments[pl.ds(c, 1), :].astype(f32)
    SC[...] = jnp.broadcast_to(seg, (TILE, T)).T.astype(bf16)
    ready(*bias_at)
    row_id = lax.broadcasted_iota(jnp.int32, (TILE, TILE), 0)
    col_id = lax.broadcasted_iota(jnp.int32, (TILE, TILE), 1)
    for a in range(T // TILE):
        rows = slice(a * TILE, (a + 1) * TILE)
        shift = 0 if a * TILE < h2 else T - D
        for b in range(T // TILE):
            cols = slice(b * TILE, (b + 1) * TILE)
            far = abs(a - b) * TILE
            if far - TILE + 1 >= T // 2:
                MM[rows, cols] = jnp.zeros((TILE, TILE), bf16)
                continue
            same = SC[rows, :].astype(f32) == seg[:, cols]
            if far - TILE + 1 >= WIN:
                weight = jnp.ones((TILE, TILE), f32)
            else:
                weight = jnp.exp(F3[rows, b * TILE - shift : (b + 1) * TILE - shift])
                if far + TILE - 1 >= WIN:
                    inside = jnp.abs(row_id - col_id + (a - b) * TILE) < WIN
                    weight = jnp.where(inside, weight, 1.0)
            MM[rows, cols] = jnp.where(same, weight, 0.0).astype(bf16)

    norms_cross.wait()
    for i in range(4):
        NP[i : i + 1, own_half] = NPS[i : i + 1, :]
        NP[i : i + 1, other_half] = NPR[i : i + 1, :]
    ready(tokens_at)

    def norm_in(i, carry):
        rows = pl.ds(i * STEP, STEP)
        x = XB[rows, :].astype(f32)
        centred = x - jnp.mean(x, axis=1, keepdims=True)
        inv = lax.rsqrt(jnp.mean(centred * centred, axis=1, keepdims=True) + EPSILON)
        t = centred * inv
        F1[rows, :] = x
        XB[rows, :] = t.astype(bf16)
        HN[rows, :] = (t * NP[0:1, :] + NP[1:2, :]).astype(bf16)
        ST[rows, 0:1] = inv
        return carry

    lax.fori_loop(0, T // STEP, norm_in, 0, unroll=2)
    cross[wo_at].start()
    cross[og_at].start()
    for copies in hidden_weights:
        copies[2].start()
        copies[3].start()
    for at in qkv_at:
        local[at].wait()

    for j in range(D // COLS):
        if j * COLS <= half < (j + 1) * COLS:
            for at in qkv_at:
                cross[at].wait()
        cols = slice(j * COLS, (j + 1) * COLS)
        late = slice(D + j * COLS, D + (j + 1) * COLS)
        e = jnp.exp(dot(HN[...], WK[:, cols]))
        a = (e * dot(HN[...], WV[:, cols])).astype(bf16)
        AB[:, cols] = a
        AB[:, late] = e.astype(bf16)
        gate = jax.nn.sigmoid(dot(HN[...], WQ[:, cols]))
        inv = 1.0 / dot(MM[...], AB[:, late])
        ratio = dot(MM[...], AB[:, cols]) * inv
        y = gate * ratio
        Y[:, cols] = y.astype(bf16)
        QQ[:, cols] = (y * (1.0 - gate)).astype(bf16)
        RT[:, cols] = ratio.astype(bf16)
        RZ[:, cols] = (gate * inv).astype(bf16)

    ready(wo_at)
    for i in range(T // STEP):
        rows = slice(i * STEP, (i + 1) * STEP)
        x = F1[rows, :] + dot(Y[rows, :], WO[...])
        F1[rows, :] = x
        centred = x - jnp.mean(x, axis=1, keepdims=True)
        inv = lax.rsqrt(jnp.mean(centred * centred, axis=1, keepdims=True) + EPSILON)
        t = centred * inv
        T2[rows, :] = t.astype(bf16)
        G[rows, :] = (t * NP[2:3, :] + NP[3:4, :]).astype(bf16)
        ST[rows, 1:2] = inv
        F3[rows, :] = jnp.zeros((STEP, D), f32)
    ready(og_at)
    if fused:
        ready(pbo_at)

    ex, ey, ez0, ez1 = (mx, dev_x), (my, dev_y), (z0, dev_z0), (z1, dev_z1)
    halvings = (((ex, ey), (ey, ex)), ((ex, ez0, ez1, ey), (ey, ez0, ez1, ex)))

    def chunk(k, wind=(0, 0), widths=(COLS, COLS)):
        return SimpleNamespace(
            k=k, slot=lax.rem(k, SLOTS), wind=wind, widths=widths, height=sh, counts=(nz, nz),
            index=(lambda z: z, lambda z: z), valid=(None, None), late=False,
        )

    def late_chunk(late):
        widths = (COLS, COLS) if late == 2 else widths_of(half, late if late < 2 else late - 1)
        ch = chunk(jnp.int32(blocks + late), widths=widths)
        ch.late = True
        if late == 2:
            ch.height = sp
        if late == 2 and fused:
            ch.counts = (2, 3)
            ch.index = (lambda z: lax.rem(z, 2), lambda z: lax.rem(z + 3 - c, 3))
            ch.valid = (mz // 2 == c, mz != 3 * o)
        return ch

    def place(ch, b, part):
        if not fused:
            return b
        bx, by, bz = b % 2, (b // 2) % 2, b // 4
        outer, inner = (bx, by) if part == 0 else (by, bx)
        if ch.wind[part]:
            return ((outer * 2 + bz % 2) * 2 + bz // 2) * 2 + inner
        return (outer * 2 + inner) * ch.counts[part] + bz

    def form(ch, part, own, total_rows):
        width, height = ch.widths[part], ch.height
        for b in range(total_rows // height):
            rows = slice(b * height, (b + 1) * height)
            at = place(ch, b, part) * height
            S[ch.slot, part, at : at + height, 0:width] = (
                own[rows, :].astype(bf16) + PR[lax.rem(ch.k, 2), part, rows, 0:width]
            )

    def block_rows(ch, first, count):
        return pl.ds(pl.multiple_of(first * ch.height, 16), count * ch.height)

    def stages(ch, part):
        return 4 if ch.wind[part] else 3

    def span(ch, part, n):
        base, size = 0, nb if ch.wind[part] else 4 * ch.counts[part]
        for bit, _ in halvings[ch.wind[part]][part][: n - 1]:
            size //= 2
            base = base + bit * size
        return base, size

    def landing(ch, part, n):
        if ch.wind[part]:
            return (0, nb // 2, 3 * nb // 4, nb - 2)[n - 1]
        return (0, 2, 3)[n - 1] * ch.counts[part]

    def stage(ch, part, n):
        cols, copies = pl.ds(0, ch.widths[part]), []
        base, size = span(ch, part, n)
        plan = halvings[ch.wind[part]][part]
        if n <= len(plan):
            bit, device = plan[n - 1]
            moves = [(base + (1 - bit) * (size // 2), landing(ch, part, n), size // 2, device)]
        else:
            moves = [
                (base + ch.index[part](lax.rem(mz + j, nz)), landing(ch, part, n) + j - 1, 1, dev_z[j - 1])
                for j in range(1, nz)
            ]
        for i, (first, at, count, device) in enumerate(moves):
            copies.append(remote(
                S.at[ch.slot, part, block_rows(ch, first, count), cols],
                RX.at[ch.slot, part, block_rows(ch, at, count), cols],
                ref.ring_s.at[ch.slot, part, n - 1 + i], ref.ring_r.at[ch.slot, part, n - 1 + i], device,
            ))
        return copies

    def whole(ch):
        return pltpu.make_async_copy(S.at[ch.slot], ref.GO.at[ch.k], ref.ring_s.at[ch.slot, 0, 0])

    def fin_copy(ch, part):
        rows, cols = pl.ds(0, ch.height), pl.ds(0, ch.widths[part])
        return pltpu.make_async_copy(
            FIN.at[lax.rem(ch.k, FINALS), part, rows, cols], ref.o_fin.at[ch.k, part, rows, cols], ref.fin_sem.at[ch.k, part]
        )

    def launch(ch):
        if not fused:
            whole(ch).start()
            return
        for part in range(2):
            for copy in stage(ch, part, 1):
                copy.start()

    def advance(ch, n):
        if not fused:
            if n == 1:
                whole(ch).wait()
            return
        for part in range(2):
            last = stages(ch, part)
            if n > last:
                continue
            for copy in stage(ch, part, n):
                copy.wait()
            cols, at = slice(0, ch.widths[part]), landing(ch, part, n)
            base, size = span(ch, part, n + 1)
            if n < last:
                S[ch.slot, part, block_rows(ch, base, size), cols] += RX[ch.slot, part, block_rows(ch, at, size), cols]
                for copy in stage(ch, part, n + 1):
                    copy.start()
                continue
            mine = base if ch.wind[part] else base + ch.index[part](mz)
            total = S[ch.slot, part, block_rows(ch, mine, 1), cols].astype(f32)
            for j in range(1 if ch.wind[part] else nz - 1):
                total = total + RX[ch.slot, part, block_rows(ch, at + j, 1), cols].astype(f32)
            if ch.valid[part] is not None:
                bias = ref.PBO[:, pl.ds(pl.multiple_of(pair_part[part] * COLS, COLS), COLS)]
                total = jnp.where(ch.valid[part], total * jnp.exp(bias), 0.0)
            if ch.late:
                fin_copy(chunk(ch.k - FINALS), part).wait()
            FIN[lax.rem(ch.k, FINALS), part, 0 : ch.height, cols] = total
            fin_copy(ch, part).start()

    def pair_copy(slot):
        return remote(PS.at[slot], PR.at[slot], ref.pair_s.at[slot, 0], ref.pair_r.at[slot, 0], dev_c)

    def hidden_round(i, carry):
        for copy in hidden_copies(i):
            copy.wait()
        up_at, down_at = up_block(i), down_block(i)
        s, slope = gelu_pair(dot(G[...], WU[up_at]))
        SD[:, 0:wide] = s.astype(bf16)
        SD[:, wide:] = (dot_nt(OG[...], WD[down_at, :]) * slope).astype(bf16)
        for n, lag in enumerate(LAGS):
            pl.when(i >= lag)(functools.partial(advance, chunk(i - lag), n + 1))
        slot = lax.rem(i, 2)
        PS[slot, 0] = dot_tn(G[...], SD[:, wide + COLS :]).astype(bf16)
        PS[slot, 1] = dot_tn(OG[...], SD[:, COLS:wide]).astype(bf16)
        pair_copy(slot).start()
        F1[...] += dot(SD[:, 0:wide], WD[down_at, :])
        F3[...] += dot_nt(SD[:, wide:], WU[up_at])
        up = dot_tn(G[...], SD[:, wide : wide + COLS])
        down = dot_tn(OG[...], SD[:, 0:COLS])
        pair_copy(slot).wait()
        ch = chunk(i)
        form(ch, 0, up, D)
        form(ch, 1, down, D)
        launch(ch)
        return carry

    lax.fori_loop(0, blocks, hidden_round, 0)
    pair_part = (c, 1 - c)

    def pump(*steps):
        for late, n in steps:
            if late >= 0:
                advance(late_chunk(late), n)
            else:
                advance(chunk(jnp.int32(blocks + late)), n)

    NG[...] = jnp.zeros(NG.shape, f32)

    def norm_mid_back(i, carry):
        rows = pl.ds(i * STEP, STEP)
        G[rows, :] = F1[rows, :].astype(bf16)
        grad, t = F3[rows, :], T2[rows, :].astype(f32)
        w = grad * NP[2:3, :]
        mean_w = jnp.mean(w, axis=1, keepdims=True)
        mean_wt = jnp.mean(w * t, axis=1, keepdims=True)
        dx = OG[rows, :].astype(f32) + ST[rows, 1:2] * (w - mean_w - t * mean_wt)
        F3[rows, :] = dx
        T2[rows, :] = dx.astype(bf16)
        NG[2] += fold_rows(grad * t)
        NG[3] += fold_rows(grad)
        return carry

    lax.fori_loop(0, T // STEP, norm_mid_back, 0, unroll=2)
    blk_local = pltpu.make_async_copy(G.at[:, own_half], ref.o_blk.at[my_rows, :], ref.end_l.at[0])
    blk_cross = remote(G.at[:, other_half], ref.o_blk.at[my_rows, :], ref.end_s.at[0], ref.end_r.at[0], dev_c)
    blk_local.start()
    blk_cross.start()
    pump(*LATE[0])

    half_cols = (slice(0, half), slice(half, D))

    def late_copies(late, source):
        ch, copies, at = late_chunk(late), [], half
        for part, width in enumerate(ch.widths):
            copies.append(remote(
                source.at[pl.ds(0, D), pl.ds(at, width)], PR.at[late % 2, part, :, pl.ds(0, width)],
                ref.pair_s.at[late % 2, 1 + part], ref.pair_r.at[late % 2, 1 + part], dev_c,
            ))
            at += width
        for copy in copies:
            copy.start()
        return copies

    def late_form(late, source, copies):
        for copy in copies:
            copy.wait()
        ch, at = late_chunk(late), 0
        for part, width in enumerate(ch.widths):
            form(ch, part, source.at[pl.ds(0, D), pl.ds(at, width)], D)
            at += width
        launch(ch)

    NZ = WU

    def gate_back(j):
        cols = slice(j * COLS, (j + 1) * COLS)
        late = slice(D + j * COLS, D + (j + 1) * COLS)
        dm = dot_nt(T2[...], WO[cols, :])
        QQ[:, cols] = (dm * QQ[:, cols].astype(f32)).astype(bf16)
        dn = dm * RZ[:, cols].astype(f32)
        NZ[0:T, cols] = dn.astype(bf16)
        NZ[0:T, late] = (-dn * RT[:, cols].astype(f32)).astype(bf16)

    OG[0:D, :] = dot_tn(T2[...], Y[...]).astype(bf16)
    sent = late_copies(0, OG)
    gate_back(0)
    gate_back(1)
    pump(*LATE[1])
    late_form(0, OG, sent)
    gate_back(2)
    RZ[0:D, :] = dot_tn(HN[...], QQ[...]).astype(bf16)
    sent = late_copies(1, RZ)
    pump(*LATE[2])

    def mixer_grad(j):
        cols = slice(j * COLS, (j + 1) * COLS)
        low, high = max(0, (j - 1) * COLS), min(T, (j + 2) * COLS)
        target = PS.at[j // 2, j if j < 2 else 3 - j]
        grad = dot_nt(NZ[low:high, :], AB[cols, :])
        for t in range(COLS // TILE):
            at = j * COLS + t * TILE
            same = SC[low:high, :].astype(f32) == seg[:, at : at + TILE]
            gap = (
                lax.broadcasted_iota(jnp.int32, (high - low, TILE), 0)
                - lax.broadcasted_iota(jnp.int32, (high - low, TILE), 1)
                + (low - at)
            )
            kept = jnp.where(same & (jnp.abs(gap) < WIN), grad[:, t * TILE : (t + 1) * TILE], 0.0)
            target[0 : high - low, t * TILE : (t + 1) * TILE] = kept.astype(bf16)

    mixer_rows = (2 * COLS, 3 * COLS)
    mixer_grad(0)
    mixer_grad(1)
    pump(*LATE[3])
    late_form(1, RZ, sent)
    mixer_grad(2)
    mixer_grad(3)
    mixer_copies = [
        remote(
            PS.at[o, part, pl.ds(0, mixer_rows[part]), :], PR.at[0, part, pl.ds(0, mixer_rows[part]), :],
            ref.pair_s.at[0, 3 + part], ref.pair_r.at[0, 3 + part], dev_c,
        )
        for part in range(2)
    ]
    for copy in mixer_copies:
        copy.start()
    pump(*LATE[4])

    def mixing_back(j):
        cols = slice(j * COLS, (j + 1) * COLS)
        late = slice(D + j * COLS, D + (j + 1) * COLS)
        da = dot_tn(MM[...], NZ[0:T, cols])
        db = dot_tn(MM[...], NZ[0:T, late])
        e = AB[:, late].astype(f32)
        T2[:, cols] = (db * e + da * AB[:, cols].astype(f32)).astype(bf16)
        Y[:, cols] = (da * e).astype(bf16)

    mixing_back(0)
    pump(*LATE[5])
    for copy in mixer_copies:
        copy.wait()
    for part in range(2):
        form(late_chunk(2), part, PS.at[c, part], mixer_rows[part])
    launch(late_chunk(2))
    mixing_back(1)
    mixing_back(2)
    pump(*LATE[6])
    RT[0:D, :] = dot_tn(HN[...], T2[...]).astype(bf16)
    sent = late_copies(3, RT)
    pump(*LATE[7])
    AB[0:D, 0:D] = dot_tn(HN[...], Y[...]).astype(bf16)
    pump(*LATE[8])
    late_form(3, RT, sent)
    sent = late_copies(4, AB)

    def norm_in_grad(j):
        cols = slice(j * COLS, (j + 1) * COLS)
        F1[:, cols] = dot_nt(QQ[...], WQ[cols, :]) + dot_nt(T2[...], WK[cols, :]) + dot_nt(Y[...], WV[cols, :])

    norm_in_grad(0)
    pump(*LATE[9])
    late_form(4, AB, sent)
    norm_in_grad(1)
    pump(*LATE[10])
    norm_in_grad(2)
    pump(*LATE[11])

    def norm_in_back(i, carry):
        rows = pl.ds(i * STEP, STEP)
        grad, t = F1[rows, :], XB[rows, :].astype(f32)
        w = grad * NP[0:1, :]
        mean_w = jnp.mean(w, axis=1, keepdims=True)
        mean_wt = jnp.mean(w * t, axis=1, keepdims=True)
        HN[rows, :] = (F3[rows, :] + ST[rows, 0:1] * (w - mean_w - t * mean_wt)).astype(bf16)
        NG[0] += fold_rows(grad * t)
        NG[1] += fold_rows(grad)
        return carry

    lax.fori_loop(0, T // STEP, norm_in_back, 0, unroll=2)
    tok_local = pltpu.make_async_copy(HN.at[:, own_half], ref.o_tok.at[my_rows, :], ref.end_l.at[1])
    tok_cross = remote(HN.at[:, other_half], ref.o_tok.at[my_rows, :], ref.end_s.at[1], ref.end_r.at[1], dev_c)
    tok_local.start()
    tok_cross.start()

    NV[...] = jnp.zeros(NV.shape, f32)
    for i in range(4):
        NV[i : i + 1, :] = jnp.sum(NG[i], axis=0, keepdims=True)
    copy = remote(NV.at[:, other_half], NR.at[0], ref.norm_s.at[0], ref.norm_r.at[0], dev_c)
    copy.start()
    pump(*LATE[12])
    copy.wait()
    NR[1] = NV[:, own_half] + NR[0]
    if fused:
        copy = remote(NR.at[1], NR.at[2], ref.norm_s.at[1], ref.norm_r.at[1], dev_x)
        copy.start()
        pump(*LATE[13])
        copy.wait()
        NR[3] = NR[1] + NR[2]
        copy = remote(NR.at[3], NR.at[4], ref.norm_s.at[2], ref.norm_r.at[2], dev_y)
        copy.start()
        pump(*LATE[14])
        copy.wait()
        NZS[mz] = NR[3] + NR[4]
        copies = [
            remote(NZS.at[mz], NZS.at[mz], ref.norm_s.at[2 + j], ref.norm_r.at[2 + j], dev_z[j - 1])
            for j in range(1, nz)
        ]
        for copy in copies:
            copy.start()
    pump(*LATE[15])
    if fused:
        for copy in copies:
            copy.wait()
        total = NZS[0]
        for j in range(1, nz):
            total = total + NZS[j]
        ref.o_norm[...] = total
        for k in range(blocks + 5 - FINALS, blocks + 5):
            for part in range(2):
                fin_copy(late_chunk(k - blocks) if k >= blocks else chunk(jnp.int32(k)), part).wait()
    else:
        pump((4, 1))
        ref.o_norm[...] = NR[1]
    blk_local.wait()
    blk_cross.wait()
    tok_local.wait()
    tok_cross.wait()


def unpack_kernel(sh, blocks, half, count, names, *all_refs):
    ref = SimpleNamespace(**dict(zip(names, all_refs)))
    step = ref.tok_in.shape[0] // count
    loads, saves = [], []

    def save(src, dst):
        copy = pltpu.make_async_copy(src, dst, ref.save_sem.at[len(saves)])
        copy.start()
        saves.append(copy)

    def load(src, dst):
        copy = pltpu.make_async_copy(src, dst, ref.load_sem.at[len(loads)])
        copy.start()
        loads.append(copy)
        return copy

    parts = [slice(i * step, (i + 1) * step) for i in range(count)]
    load_t = [load(ref.o_tok.at[parts[0], :], ref.tok_in.at[parts[0], :])]
    load_f = load(ref.o_fin, ref.fin)
    load_n = load(ref.o_norm, ref.norm)
    load_b = load(ref.o_blk, ref.blk)
    load_t += [load(ref.o_tok.at[rows, :], ref.tok_in.at[rows, :]) for rows in parts[1:]]

    def widen(i):
        load_t[i].wait()
        ref.tok_out[parts[i], :] = ref.tok_in[parts[i], :].astype(f32)
        save(ref.tok_out.at[parts[i], :], ref.r_tok.at[parts[i], :])

    widen(0)
    load_f.wait()
    fin = ref.fin
    for k in range(blocks):
        cols = slice(k * COLS, (k + 1) * COLS)
        ref.up[:, cols] = fin[k, 0, 0:sh, :]
        ref.dn[:, cols] = fin[k, 1, 0:sh, :]
    save(ref.up, ref.r_up)
    save(ref.dn, ref.r_dn)
    low, high = fin[blocks + 2, 0], fin[blocks + 2, 1]
    first = lax.axis_index("chan") == 0
    ref.pair[:, 0:COLS] = jnp.where(first, low, high)
    ref.pair[:, COLS : 2 * COLS] = jnp.where(first, high, low)
    save(ref.pair, ref.r_pair)
    for i, (late, target) in enumerate(((0, ref.r_wo), (1, ref.r_q), (3, ref.r_k), (4, ref.r_v))):
        at = 0
        for part, width in enumerate(widths_of(half, i)):
            ref.square[i, :, at : at + width] = fin[blocks + late, part, 0:sh, 0:width]
            at += width
        save(ref.square.at[i], target)
    load_n.wait()
    for i, (vector, target) in enumerate(((ref.gi, ref.r_gi), (ref.si, ref.r_si), (ref.gm, ref.r_gm), (ref.sm, ref.r_sm))):
        vector[...] = ref.norm[i, :]
        save(vector, target)
    load_b.wait()
    save(ref.blk, ref.r_blk)
    for i in range(1, count):
        widen(i)
    for copy in saves:
        copy.wait()


def unpack(T, D, FH, sh, sp, out):
    half = D // 2
    blocks = FH // COLS
    count = 4
    inputs = dict(o_blk=out.o_blk, o_tok=out.o_tok, o_norm=out.o_norm, o_fin=out.o_fin)
    vector, square, wide = ((half,), f32), ((sh, half), f32), ((sh, FH), f32)
    results = dict(
        r_blk=((2 * T, half), bf16), r_tok=((2 * T, half), f32), r_gi=vector, r_si=vector, r_q=square, r_k=square,
        r_v=square, r_wo=square, r_gm=vector, r_sm=vector, r_up=wide, r_dn=wide, r_pair=((sp, T // 2), f32),
    )
    held = pltpu.VMEM((half,), f32)
    scratch = dict(
        blk=pltpu.VMEM((2 * T, half), bf16), tok_in=pltpu.VMEM((2 * T, half), bf16),
        tok_out=pltpu.VMEM((2 * T, half), f32), fin=pltpu.VMEM(out.o_fin.shape, f32),
        norm=pltpu.VMEM((8, half), f32), up=pltpu.VMEM((sh, FH), f32), dn=pltpu.VMEM((sh, FH), f32),
        pair=pltpu.VMEM((sp, T // 2), f32), square=pltpu.VMEM((4, sh, half), f32), gi=held, si=held, gm=held, sm=held,
        load_sem=pltpu.SemaphoreType.DMA((3 + count,)), save_sem=pltpu.SemaphoreType.DMA((len(results) - 1 + count,)),
    )
    values = pl.pallas_call(
        functools.partial(unpack_kernel, sh, blocks, half, count, tuple(inputs) + tuple(results) + tuple(scratch)),
        out_shape=tuple(jax.ShapeDtypeStruct(shape, kind) for shape, kind in results.values()),
        in_specs=[ANY] * len(inputs),
        out_specs=tuple(ANY for _ in results),
        scratch_shapes=list(scratch.values()),
        compiler_params=pltpu.CompilerParams(vmem_limit_bytes=63 << 20),
    )(*inputs.values())
    blk, tok, gi, si, q, k, v, wo, gm, sm, up, dn, pair = values
    return blk, tok, gi, si, q, k, v, wo.T, gm, sm, up, dn.T, pair


def gather_parts(T, D, out, pair_bias):
    half = D // 2
    parts = out.GO
    blocks = parts.shape[0] - 5
    join = lambda chosen: jnp.concatenate(chosen, 1).astype(f32)
    scatter = lambda v: lax.psum_scatter(v, "rows", scatter_dimension=0, tiled=True)
    up = scatter(join([parts[k, 0] for k in range(blocks)]))
    down = scatter(join([parts[k, 1] for k in range(blocks)])).T
    late = []
    for i in (0, 1, 3, 4):
        widths = widths_of(half, i if i < 2 else i - 1)
        late.append(scatter(join([parts[blocks + i, p, :, 0:width] for p, width in enumerate(widths)])))
    wo, q, k, v = late
    first = lax.axis_index("chan") == 0
    spread = []
    for p, rows in ((0, 2 * COLS), (1, 3 * COLS)):
        held, rest = parts[blocks + 2, p, 0:rows], jnp.zeros((T - rows, COLS), bf16)
        spread.append(jnp.where(first, jnp.concatenate([held, rest]), jnp.concatenate([rest, held])))
    low, high = spread
    pair = scatter(join([jnp.where(first, low, high), jnp.where(first, high, low)]))
    bias = lax.dynamic_slice(
        pair_bias, (lax.axis_index("rows") * pair.shape[0], lax.axis_index("chan") * (T // 2)), pair.shape
    )
    norms = lax.psum(out.o_norm, "rows")
    return (
        out.o_blk, out.o_tok.astype(f32), norms[0], norms[1], q, k, v, wo.T, norms[2], norms[3], up, down,
        pair * jnp.exp(bias),
    )


def on_device(
    tokens, segments, gain_in, shift_in, query_weight, key_weight, value_weight, out_weight,
    gain_mid, shift_mid, up_weight, down_weight, pair_bias, out_grad,
):
    T = segments.shape[1]
    D, FH = up_weight.shape
    R = lax.axis_size("rows")
    half = D // 2
    blocks = FH // COLS
    fused = R == 16 and D % (16 * R) == 0 and T % (16 * R) == 0
    nb = R if fused else 16
    nz = nb // 4
    sh, sp = D // nb, T // nb
    inputs = dict(
        tokens=tokens, segments=segments, gi=gain_in, si=shift_in, wq=query_weight, wk=key_weight, wv=value_weight,
        wo=out_weight, gm=gain_mid, sm=shift_mid, wu=up_weight, wd=down_weight, pair_bias=pair_bias,
        out_grad=out_grad,
    )
    near = ("segments", "gi", "si", "gm", "sm")
    outputs = dict(
        o_blk=(ANY, (2 * T, half), bf16), o_tok=(ANY, (2 * T, half), bf16), o_norm=(VMEM, (8, half), f32)
    )
    if fused:
        outputs |= dict(o_fin=(ANY, (blocks + 5, 2, sp, COLS), f32))
    else:
        outputs |= dict(GO=(ANY, (blocks + 5, 2, D, COLS), bf16))
    square, act, total = pltpu.VMEM((D, D), bf16), pltpu.VMEM((T, D), bf16), pltpu.VMEM((T, D), f32)
    small, halves = pltpu.VMEM((8, TILE), f32), pltpu.VMEM((8, half), f32)
    sems = pltpu.SemaphoreType.DMA
    scratch = dict(
        XB=act, OG=act, HN=act, G=act, Y=act, QQ=act, RT=act, RZ=act, T2=act,
        AB=pltpu.VMEM((T, 2 * D), bf16), MM=pltpu.VMEM((T, T), bf16), F1=total, F3=total,
        ST=pltpu.VMEM((T, TILE), f32), WQ=square, WK=square, WV=square, WO=square,
        WU=pltpu.VMEM((2 * D, FH), bf16), WD=pltpu.VMEM((2 * FH, D), bf16),
        SD=pltpu.VMEM((T, 4 * COLS), bf16), SC=pltpu.VMEM((T, TILE), bf16),
        NP=pltpu.VMEM((8, D), f32), NPS=halves, NPR=halves,
        PS=pltpu.VMEM((2, 2, D, COLS), bf16), PR=pltpu.VMEM((2, 2, D, COLS), bf16),
        S=pltpu.VMEM((SLOTS, 2, D, COLS), bf16),
        RX=pltpu.VMEM((SLOTS, 2, D, COLS), bf16) if fused else small,
        FIN=pltpu.VMEM((FINALS, 2, sp, COLS), f32) if fused else small,
        NG=pltpu.VMEM((4, 8, D), f32), NV=pltpu.VMEM((8, D), f32), NR=pltpu.VMEM((5, 8, half), f32),
        NZS=pltpu.VMEM((nz, 8, half), f32), PBO=pltpu.VMEM((sp, T // 2), f32),
        local_sem=sems((16,)), entry_s=sems((16,)), entry_r=sems((16,)), end_l=sems((2,)), end_s=sems((2,)),
        end_r=sems((2,)), up_l=sems((blocks,)), up_s=sems((blocks,)), up_r=sems((blocks,)),
        down_l=sems((blocks,)), down_s=sems((blocks,)), down_r=sems((blocks,)),
        pair_s=sems((2, 5)), pair_r=sems((2, 5)), ring_s=sems((SLOTS, 2, 6)), ring_r=sems((SLOTS, 2, 6)),
        norm_s=sems((2 + nz,)), norm_r=sems((2 + nz,)), fin_sem=sems((blocks + 5, 2)),
    )
    results = pl.pallas_call(
        functools.partial(
            block_kernel, T, D, FH, R, fused, tuple(inputs) + tuple(outputs) + tuple(scratch)
        ),
        out_shape=tuple(jax.ShapeDtypeStruct(shape, kind) for _, shape, kind in outputs.values()),
        in_specs=[VMEM if name in near else ANY for name in inputs],
        out_specs=tuple(spec for spec, _, _ in outputs.values()),
        scratch_shapes=list(scratch.values()),
        compiler_params=pltpu.CompilerParams(
            collective_id=0, has_side_effects=True, vmem_limit_bytes=63 << 20
        ),
    )(*inputs.values())
    out = SimpleNamespace(**dict(zip(outputs, results)))
    if fused:
        return unpack(T, D, FH, sh, sp, out)
    return gather_parts(T, D, out, pair_bias)


def solution(mesh):
    split, first, second, vector = P("rows", "chan"), P("chan", None), P(None, "chan"), P("chan")
    return jax.shard_map(
        on_device,
        mesh=mesh,
        in_specs=(
            split, P("rows", None), vector, vector, second, second, second, first, vector, vector, second, first,
            P(), split,
        ),
        out_specs=(
            split, split, vector, vector, split, split, split, P("chan", "rows"), vector, vector, split,
            P("chan", "rows"), split,
        ),
        check_vma=False,
    )
```

```python
import functools
from types import SimpleNamespace

import jax
import jax.numpy as jnp
from jax import lax
from jax.experimental import pallas as pl
from jax.experimental.pallas import tpu as pltpu
from jax.sharding import PartitionSpec as P

MESH = pl.DeviceIdType.MESH
ANY, VMEM = pl.BlockSpec(memory_space=pl.ANY), pl.BlockSpec(memory_space=pltpu.VMEM)
WIN = 256
EPSILON = 1e-05
TILE = 128
COLS = 256
SLOTS = 5
FINALS = 6
STEP = 256
LAGS = (2, 3, 4)
LATE = (
    ((-3, 2), (-2, 1)), ((-4, 3),), ((-2, 2), (-1, 1)), ((-3, 3),), ((0, 1),), ((-1, 2),), ((-2, 3),), ((0, 2), (1, 1)),
    ((2, 1),), ((-1, 3), (1, 2)), ((0, 3), (2, 2)), (), ((3, 1), (1, 3)), ((4, 1), (3, 2)), ((2, 3), (4, 2)),
    ((3, 3), (4, 3)),
)
f32 = jnp.float32
bf16 = jnp.bfloat16


def dot(left, right, cl=1, cr=0):
    return lax.dot_general(left, right, (((cl,), (cr,)), ((), ())), preferred_element_type=f32)


def dot_nt(left, right):
    return dot(left, right, 1, 1)


def dot_tn(left, right):
    return dot(left, right, 0, 0)


def gelu_pair(p):
    phi = 0.5 * (1.0 + lax.erf(p * 0.7071067811865476))
    return p * phi, phi + p * (jnp.exp(-0.5 * p * p) * 0.3989422804014327)


def fold_rows(v):
    return jnp.sum(v.reshape(v.shape[0] // 8, 8, v.shape[1]), axis=0)


def widths_of(half, late):
    return (COLS, half - COLS) if late % 2 == 0 else (half - COLS, COLS)


def block_kernel(T, D, FH, R, fused, names, *all_refs):
    ref = SimpleNamespace(**dict(zip(names, all_refs)))
    half = D // 2
    blocks = FH // COLS
    nb = R if fused else 16
    nz = nb // 4
    sh, sp = D // nb, T // nb
    r = lax.axis_index("rows")
    c = lax.axis_index("chan")
    o = 1 - c
    mx, my, mz = lax.rem(r, 2), lax.rem(r // 2, 2), r // 4
    z0, z1 = lax.rem(mz, 2), mz // 2
    dev_c = (r, o)
    dev_x = (r + 1 - 2 * mx, c)
    dev_y = (r + 2 - 4 * my, c)
    z0, z1 = lax.rem(mz, 2), mz // 2
    dev_z = [(lax.rem(mz + j, nz) * 4 + lax.rem(r, 4), c) for j in range(1, nz)]
    dev_z0, dev_z1 = (r + 4 - 8 * z0, c), (r + 8 - 16 * z1, c)
    dev_z0 = (r + 4 - 8 * z0, c)
    dev_z1 = (r + 8 - 16 * z1, c)
    own_half = pl.ds(pl.multiple_of(c * half, TILE), half)
    other_half = pl.ds(pl.multiple_of(o * half, TILE), half)

    XB, OG, HN, G = ref.XB, ref.OG, ref.HN, ref.G
    Y, QQ, RT, RZ, T2 = ref.Y, ref.QQ, ref.RT, ref.RZ, ref.T2
    AB, MM, F1, F3, ST = ref.AB, ref.MM, ref.F1, ref.F3, ref.ST
    WQ, WK, WV, WO, WU, WD = ref.WQ, ref.WK, ref.WV, ref.WO, ref.WU, ref.WD
    SD, SC, NP, NPS, NPR = ref.SD, ref.SC, ref.NP, ref.NPS, ref.NPR
    PS, PR, S, RX, FIN = ref.PS, ref.PR, ref.S, ref.RX, ref.FIN
    NG, NV, NR, NZS = ref.NG, ref.NV, ref.NR, ref.NZS

    def remote(src, dst, send, recv, device):
        return pltpu.make_async_remote_copy(
            src_ref=src, dst_ref=dst, send_sem=send, recv_sem=recv, device_id=device, device_id_type=MESH
        )

    barrier = pltpu.get_barrier_semaphore()
    greeted = [dev_c] + ([dev_x, dev_y] + dev_z if fused else [])
    for device in greeted:
        pl.semaphore_signal(barrier, inc=1, device_id=device, device_id_type=MESH)

    my_rows, other_rows = pl.ds(c * T, T), pl.ds(o * T, T)
    h2 = T // 2
    local, cross = [], []

    def load(src, dst, away=None, there=None):
        at = len(local)
        local.append(pltpu.make_async_copy(src, dst, ref.local_sem.at[at]))
        cross.append(None if away is None else remote(away, there, ref.entry_s.at[at], ref.entry_r.at[at], dev_c))
        local[at].start()
        return at

    bias_at = [
        load(ref.pair_bias.at[0:h2, 0:D], F3.at[0:h2, :]),
        load(ref.pair_bias.at[h2:T, T - D : T], F3.at[h2:T, :]),
    ]
    tokens_at = load(
        ref.tokens.at[my_rows, :], XB.at[:, own_half], ref.tokens.at[other_rows, :], XB.at[:, own_half]
    )
    qkv_at = [
        load(src, dst.at[:, 0:half], src, dst.at[:, half:D]) for src, dst in ((ref.wk, WK), (ref.wv, WV), (ref.wq, WQ))
    ]
    wo_at = load(ref.wo, WO.at[0:half, :], ref.wo, WO.at[half:D, :])
    og_at = load(
        ref.out_grad.at[my_rows, :], OG.at[:, own_half], ref.out_grad.at[other_rows, :], OG.at[:, own_half]
    )
    wide, per_row = 2 * COLS, blocks // 2

    def up_block(i, at=0, width=wide):
        rows = pl.ds(pl.multiple_of(i // per_row * D, TILE), D)
        return rows, pl.ds(pl.multiple_of(lax.rem(i, per_row) * wide + at, COLS), width)

    def down_block(i, at=0, width=wide):
        return pl.ds(pl.multiple_of(i * wide + at, COLS), width)

    def hidden_copies(i):
        part = pl.ds(pl.multiple_of(i * COLS, COLS), COLS)
        up, down = ref.wu.at[:, part], ref.wd.at[part, :]
        return (
            pltpu.make_async_copy(up, WU.at[up_block(i, 0, COLS)], ref.up_l.at[i]),
            pltpu.make_async_copy(down, WD.at[down_block(i, 0, COLS), :], ref.down_l.at[i]),
            remote(up, WU.at[up_block(i, COLS, COLS)], ref.up_s.at[i], ref.up_r.at[i], dev_c),
            remote(down, WD.at[down_block(i, COLS, COLS), :], ref.down_s.at[i], ref.down_r.at[i], dev_c),
        )

    pbo_at = None
    if fused:
        pair_rows = pl.ds(pl.multiple_of(r * sp, 8), sp)
        pair_cols = pl.ds(pl.multiple_of(c * (T // 2), TILE), T // 2)
        pbo_at = load(ref.pair_bias.at[pair_rows, pair_cols], ref.PBO)

    NPS[...] = jnp.zeros(NPS.shape, f32)
    for i, vector in enumerate((ref.gi, ref.si, ref.gm, ref.sm)):
        NPS[i : i + 1, :] = vector[...].reshape(1, half)
    norms_cross = remote(NPS, NPR, ref.entry_s.at[15], ref.entry_r.at[15], dev_c)
    pl.semaphore_wait(barrier, len(greeted))
    cross[tokens_at].start()
    norms_cross.start()
    for at in qkv_at:
        cross[at].start()
    hidden_weights = [hidden_copies(jnp.int32(i)) for i in range(blocks)]
    for copies in hidden_weights:
        copies[0].start()
        copies[1].start()

    def ready(*chosen):
        for at in chosen:
            local[at].wait()
            if cross[at] is not None:
                cross[at].wait()

    seg = ref.segments[pl.ds(c, 1), :].astype(f32)
    SC[...] = jnp.broadcast_to(seg, (TILE, T)).T.astype(bf16)
    ready(*bias_at)
    row_id = lax.broadcasted_iota(jnp.int32, (TILE, TILE), 0)
    col_id = lax.broadcasted_iota(jnp.int32, (TILE, TILE), 1)
    for a in range(T // TILE):
        rows = slice(a * TILE, (a + 1) * TILE)
        shift = 0 if a * TILE < h2 else T - D
        for b in range(T // TILE):
            cols = slice(b * TILE, (b + 1) * TILE)
            far = abs(a - b) * TILE
            if far - TILE + 1 >= T // 2:
                MM[rows, cols] = jnp.zeros((TILE, TILE), bf16)
                continue
            same = SC[rows, :].astype(f32) == seg[:, cols]
            if far - TILE + 1 >= WIN:
                weight = jnp.ones((TILE, TILE), f32)
            else:
                weight = jnp.exp(F3[rows, b * TILE - shift : (b + 1) * TILE - shift])
                if far + TILE - 1 >= WIN:
                    inside = jnp.abs(row_id - col_id + (a - b) * TILE) < WIN
                    weight = jnp.where(inside, weight, 1.0)
            MM[rows, cols] = jnp.where(same, weight, 0.0).astype(bf16)

    norms_cross.wait()
    for i in range(4):
        NP[i : i + 1, own_half] = NPS[i : i + 1, :]
        NP[i : i + 1, other_half] = NPR[i : i + 1, :]
    ready(tokens_at)

    def norm_in(i, carry):
        rows = pl.ds(i * STEP, STEP)
        x = XB[rows, :].astype(f32)
        centred = x - jnp.mean(x, axis=1, keepdims=True)
        inv = lax.rsqrt(jnp.mean(centred * centred, axis=1, keepdims=True) + EPSILON)
        t = centred * inv
        F1[rows, :] = x
        XB[rows, :] = t.astype(bf16)
        HN[rows, :] = (t * NP[0:1, :] + NP[1:2, :]).astype(bf16)
        ST[rows, 0:1] = inv
        return carry

    lax.fori_loop(0, T // STEP, norm_in, 0, unroll=2)
    cross[wo_at].start()
    cross[og_at].start()
    for copies in hidden_weights:
        copies[2].start()
        copies[3].start()
    for at in qkv_at:
        local[at].wait()

    for j in range(D // COLS):
        if j * COLS <= half < (j + 1) * COLS:
            for at in qkv_at:
                cross[at].wait()
        cols = slice(j * COLS, (j + 1) * COLS)
        late = slice(D + j * COLS, D + (j + 1) * COLS)
        e = jnp.exp(dot(HN[...], WK[:, cols]))
        a = (e * dot(HN[...], WV[:, cols])).astype(bf16)
        AB[:, cols] = a
        AB[:, late] = e.astype(bf16)
        gate = jax.nn.sigmoid(dot(HN[...], WQ[:, cols]))
        inv = 1.0 / dot(MM[...], AB[:, late])
        ratio = dot(MM[...], AB[:, cols]) * inv
        y = gate * ratio
        Y[:, cols] = y.astype(bf16)
        QQ[:, cols] = (y * (1.0 - gate)).astype(bf16)
        RT[:, cols] = ratio.astype(bf16)
        RZ[:, cols] = (gate * inv).astype(bf16)

    ready(wo_at)
    for i in range(T // STEP):
        rows = slice(i * STEP, (i + 1) * STEP)
        x = F1[rows, :] + dot(Y[rows, :], WO[...])
        F1[rows, :] = x
        centred = x - jnp.mean(x, axis=1, keepdims=True)
        inv = lax.rsqrt(jnp.mean(centred * centred, axis=1, keepdims=True) + EPSILON)
        t = centred * inv
        T2[rows, :] = t.astype(bf16)
        G[rows, :] = (t * NP[2:3, :] + NP[3:4, :]).astype(bf16)
        ST[rows, 1:2] = inv
        F3[rows, :] = jnp.zeros((STEP, D), f32)
    ready(og_at)
    if fused:
        ready(pbo_at)

    ex, ey, ez0, ez1 = (mx, dev_x), (my, dev_y), (z0, dev_z0), (z1, dev_z1)
    halvings = (((ex, ey), (ey, ex)), ((ex, ez0, ez1, ey), (ey, ez0, ez1, ex)))

    def chunk(k, wind=(0, 0), widths=(COLS, COLS)):
        return SimpleNamespace(
            k=k, slot=lax.rem(k, SLOTS), wind=wind, widths=widths, height=sh, counts=(nz, nz),
            index=(lambda z: z, lambda z: z), valid=(None, None), late=False,
        )

    def late_chunk(late):
        widths = (COLS, COLS) if late == 2 else widths_of(half, late if late < 2 else late - 1)
        ch = chunk(jnp.int32(blocks + late), widths=widths)
        ch.late = True
        if late == 2:
            ch.height = sp
        if late == 2 and fused:
            ch.counts = (2, 3)
            ch.index = (lambda z: lax.rem(z, 2), lambda z: lax.rem(z + 3 - c, 3))
            ch.valid = (mz // 2 == c, mz != 3 * o)
        return ch

    def place(ch, b, part):
        if not fused:
            return b
        bx, by, bz = b % 2, (b // 2) % 2, b // 4
        outer, inner = (bx, by) if part == 0 else (by, bx)
        if ch.wind[part]:
            return ((outer * 2 + bz % 2) * 2 + bz // 2) * 2 + inner
        return (outer * 2 + inner) * ch.counts[part] + bz

    def form(ch, part, own, total_rows):
        width, height = ch.widths[part], ch.height
        for b in range(total_rows // height):
            rows = slice(b * height, (b + 1) * height)
            at = place(ch, b, part) * height
            S[ch.slot, part, at : at + height, 0:width] = (
                own[rows, :].astype(bf16) + PR[lax.rem(ch.k, 2), part, rows, 0:width]
            )

    def block_rows(ch, first, count):
        return pl.ds(pl.multiple_of(first * ch.height, 16), count * ch.height)

    def stages(ch, part):
        return 4 if ch.wind[part] else 3

    def span(ch, part, n):
        base, size = 0, nb if ch.wind[part] else 4 * ch.counts[part]
        for bit, _ in halvings[ch.wind[part]][part][: n - 1]:
            size //= 2
            base = base + bit * size
        return base, size

    def landing(ch, part, n):
        if ch.wind[part]:
            return (0, nb // 2, 3 * nb // 4, nb - 2)[n - 1]
        return (0, 2, 3)[n - 1] * ch.counts[part]

    def stage(ch, part, n):
        cols, copies = pl.ds(0, ch.widths[part]), []
        base, size = span(ch, part, n)
        plan = halvings[ch.wind[part]][part]
        if n <= len(plan):
            bit, device = plan[n - 1]
            moves = [(base + (1 - bit) * (size // 2), landing(ch, part, n), size // 2, device)]
        else:
            moves = [
                (base + ch.index[part](lax.rem(mz + j, nz)), landing(ch, part, n) + j - 1, 1, dev_z[j - 1])
                for j in range(1, nz)
            ]
        for i, (first, at, count, device) in enumerate(moves):
            copies.append(remote(
                S.at[ch.slot, part, block_rows(ch, first, count), cols],
                RX.at[ch.slot, part, block_rows(ch, at, count), cols],
                ref.ring_s.at[ch.slot, part, n - 1 + i], ref.ring_r.at[ch.slot, part, n - 1 + i], device,
            ))
        return copies

    def whole(ch):
        return pltpu.make_async_copy(S.at[ch.slot], ref.GO.at[ch.k], ref.ring_s.at[ch.slot, 0, 0])

    def fin_copy(ch, part):
        rows, cols = pl.ds(0, ch.height), pl.ds(0, ch.widths[part])
        return pltpu.make_async_copy(
            FIN.at[lax.rem(ch.k, FINALS), part, rows, cols], ref.o_fin.at[ch.k, part, rows, cols], ref.fin_sem.at[ch.k, part]
        )

    def launch(ch):
        if not fused:
            whole(ch).start()
            return
        for part in range(2):
            for copy in stage(ch, part, 1):
                copy.start()

    def advance(ch, n):
        if not fused:
            if n == 1:
                whole(ch).wait()
            return
        for part in range(2):
            last = stages(ch, part)
            if n > last:
                continue
            for copy in stage(ch, part, n):
                copy.wait()
            cols, at = slice(0, ch.widths[part]), landing(ch, part, n)
            base, size = span(ch, part, n + 1)
            if n < last:
                S[ch.slot, part, block_rows(ch, base, size), cols] += RX[ch.slot, part, block_rows(ch, at, size), cols]
                for copy in stage(ch, part, n + 1):
                    copy.start()
                continue
            mine = base if ch.wind[part] else base + ch.index[part](mz)
            total = S[ch.slot, part, block_rows(ch, mine, 1), cols].astype(f32)
            for j in range(1 if ch.wind[part] else nz - 1):
                total = total + RX[ch.slot, part, block_rows(ch, at + j, 1), cols].astype(f32)
            if ch.valid[part] is not None:
                bias = ref.PBO[:, pl.ds(pl.multiple_of(pair_part[part] * COLS, COLS), COLS)]
                total = jnp.where(ch.valid[part], total * jnp.exp(bias), 0.0)
            if ch.late:
                fin_copy(chunk(ch.k - FINALS), part).wait()
            FIN[lax.rem(ch.k, FINALS), part, 0 : ch.height, cols] = total
            fin_copy(ch, part).start()

    def pair_copy(slot):
        return remote(PS.at[slot], PR.at[slot], ref.pair_s.at[slot, 0], ref.pair_r.at[slot, 0], dev_c)

    def hidden_round(i, carry):
        for copy in hidden_copies(i):
            copy.wait()
        up_at, down_at = up_block(i), down_block(i)
        s, slope = gelu_pair(dot(G[...], WU[up_at]))
        SD[:, 0:wide] = s.astype(bf16)
        SD[:, wide:] = (dot_nt(OG[...], WD[down_at, :]) * slope).astype(bf16)
        for n, lag in enumerate(LAGS):
            pl.when(i >= lag)(functools.partial(advance, chunk(i - lag), n + 1))
        slot = lax.rem(i, 2)
        PS[slot, 0] = dot_tn(G[...], SD[:, wide + COLS :]).astype(bf16)
        PS[slot, 1] = dot_tn(OG[...], SD[:, COLS:wide]).astype(bf16)
        pair_copy(slot).start()
        F1[...] += dot(SD[:, 0:wide], WD[down_at, :])
        F3[...] += dot_nt(SD[:, wide:], WU[up_at])
        up = dot_tn(G[...], SD[:, wide : wide + COLS])
        down = dot_tn(OG[...], SD[:, 0:COLS])
        pair_copy(slot).wait()
        ch = chunk(i)
        form(ch, 0, up, D)
        form(ch, 1, down, D)
        launch(ch)
        return carry

    lax.fori_loop(0, blocks, hidden_round, 0)
    pair_part = (c, 1 - c)

    def pump(*steps):
        for late, n in steps:
            if late >= 0:
                advance(late_chunk(late), n)
            else:
                advance(chunk(jnp.int32(blocks + late)), n)

    NG[...] = jnp.zeros(NG.shape, f32)

    def norm_mid_back(i, carry):
        rows = pl.ds(i * STEP, STEP)
        G[rows, :] = F1[rows, :].astype(bf16)
        grad, t = F3[rows, :], T2[rows, :].astype(f32)
        w = grad * NP[2:3, :]
        mean_w = jnp.mean(w, axis=1, keepdims=True)
        mean_wt = jnp.mean(w * t, axis=1, keepdims=True)
        dx = OG[rows, :].astype(f32) + ST[rows, 1:2] * (w - mean_w - t * mean_wt)
        F3[rows, :] = dx
        T2[rows, :] = dx.astype(bf16)
        NG[2] += fold_rows(grad * t)
        NG[3] += fold_rows(grad)
        return carry

    lax.fori_loop(0, T // STEP, norm_mid_back, 0, unroll=2)
    blk_local = pltpu.make_async_copy(G.at[:, own_half], ref.o_blk.at[my_rows, :], ref.end_l.at[0])
    blk_cross = remote(G.at[:, other_half], ref.o_blk.at[my_rows, :], ref.end_s.at[0], ref.end_r.at[0], dev_c)
    blk_local.start()
    blk_cross.start()
    pump(*LATE[0])

    half_cols = (slice(0, half), slice(half, D))

    def late_copies(late, source):
        ch, copies, at = late_chunk(late), [], half
        for part, width in enumerate(ch.widths):
            copies.append(remote(
                source.at[pl.ds(0, D), pl.ds(at, width)], PR.at[late % 2, part, :, pl.ds(0, width)],
                ref.pair_s.at[late % 2, 1 + part], ref.pair_r.at[late % 2, 1 + part], dev_c,
            ))
            at += width
        for copy in copies:
            copy.start()
        return copies

    def late_form(late, source, copies):
        for copy in copies:
            copy.wait()
        ch, at = late_chunk(late), 0
        for part, width in enumerate(ch.widths):
            form(ch, part, source.at[pl.ds(0, D), pl.ds(at, width)], D)
            at += width
        launch(ch)

    NZ = WU

    def gate_back(j):
        cols = slice(j * COLS, (j + 1) * COLS)
        late = slice(D + j * COLS, D + (j + 1) * COLS)
        dm = dot_nt(T2[...], WO[cols, :])
        QQ[:, cols] = (dm * QQ[:, cols].astype(f32)).astype(bf16)
        dn = dm * RZ[:, cols].astype(f32)
        NZ[0:T, cols] = dn.astype(bf16)
        NZ[0:T, late] = (-dn * RT[:, cols].astype(f32)).astype(bf16)

    OG[0:D, :] = dot_tn(T2[...], Y[...]).astype(bf16)
    sent = late_copies(0, OG)
    gate_back(0)
    gate_back(1)
    pump(*LATE[1])
    late_form(0, OG, sent)
    gate_back(2)
    RZ[0:D, :] = dot_tn(HN[...], QQ[...]).astype(bf16)
    sent = late_copies(1, RZ)
    pump(*LATE[2])

    def mixer_grad(j):
        cols = slice(j * COLS, (j + 1) * COLS)
        low, high = max(0, (j - 1) * COLS), min(T, (j + 2) * COLS)
        target = PS.at[j // 2, j if j < 2 else 3 - j]
        grad = dot_nt(NZ[low:high, :], AB[cols, :])
        for t in range(COLS // TILE):
            at = j * COLS + t * TILE
            same = SC[low:high, :].astype(f32) == seg[:, at : at + TILE]
            gap = (
                lax.broadcasted_iota(jnp.int32, (high - low, TILE), 0)
                - lax.broadcasted_iota(jnp.int32, (high - low, TILE), 1)
                + (low - at)
            )
            kept = jnp.where(same & (jnp.abs(gap) < WIN), grad[:, t * TILE : (t + 1) * TILE], 0.0)
            target[0 : high - low, t * TILE : (t + 1) * TILE] = kept.astype(bf16)

    mixer_rows = (2 * COLS, 3 * COLS)
    mixer_grad(0)
    mixer_grad(1)
    pump(*LATE[3])
    late_form(1, RZ, sent)
    mixer_grad(2)
    mixer_grad(3)
    mixer_copies = [
        remote(
            PS.at[o, part, pl.ds(0, mixer_rows[part]), :], PR.at[0, part, pl.ds(0, mixer_rows[part]), :],
            ref.pair_s.at[0, 3 + part], ref.pair_r.at[0, 3 + part], dev_c,
        )
        for part in range(2)
    ]
    for copy in mixer_copies:
        copy.start()
    pump(*LATE[4])

    def mixing_back(j):
        cols = slice(j * COLS, (j + 1) * COLS)
        late = slice(D + j * COLS, D + (j + 1) * COLS)
        da = dot_tn(MM[...], NZ[0:T, cols])
        db = dot_tn(MM[...], NZ[0:T, late])
        e = AB[:, late].astype(f32)
        T2[:, cols] = (db * e + da * AB[:, cols].astype(f32)).astype(bf16)
        Y[:, cols] = (da * e).astype(bf16)

    mixing_back(0)
    pump(*LATE[5])
    for copy in mixer_copies:
        copy.wait()
    for part in range(2):
        form(late_chunk(2), part, PS.at[c, part], mixer_rows[part])
    launch(late_chunk(2))
    mixing_back(1)
    mixing_back(2)
    pump(*LATE[6])
    RT[0:D, :] = dot_tn(HN[...], T2[...]).astype(bf16)
    sent = late_copies(3, RT)
    pump(*LATE[7])
    AB[0:D, 0:D] = dot_tn(HN[...], Y[...]).astype(bf16)
    pump(*LATE[8])
    late_form(3, RT, sent)
    sent = late_copies(4, AB)

    def norm_in_grad(j):
        cols = slice(j * COLS, (j + 1) * COLS)
        F1[:, cols] = dot_nt(QQ[...], WQ[cols, :]) + dot_nt(T2[...], WK[cols, :]) + dot_nt(Y[...], WV[cols, :])

    norm_in_grad(0)
    pump(*LATE[9])
    late_form(4, AB, sent)
    norm_in_grad(1)
    pump(*LATE[10])
    norm_in_grad(2)
    pump(*LATE[11])

    def norm_in_back(i, carry):
        rows = pl.ds(i * STEP, STEP)
        grad, t = F1[rows, :], XB[rows, :].astype(f32)
        w = grad * NP[0:1, :]
        mean_w = jnp.mean(w, axis=1, keepdims=True)
        mean_wt = jnp.mean(w * t, axis=1, keepdims=True)
        HN[rows, :] = (F3[rows, :] + ST[rows, 0:1] * (w - mean_w - t * mean_wt)).astype(bf16)
        NG[0] += fold_rows(grad * t)
        NG[1] += fold_rows(grad)
        return carry

    lax.fori_loop(0, T // STEP, norm_in_back, 0, unroll=2)
    tok_local = pltpu.make_async_copy(HN.at[:, own_half], ref.o_tok.at[my_rows, :], ref.end_l.at[1])
    tok_cross = remote(HN.at[:, other_half], ref.o_tok.at[my_rows, :], ref.end_s.at[1], ref.end_r.at[1], dev_c)
    tok_local.start()
    tok_cross.start()

    NV[...] = jnp.zeros(NV.shape, f32)
    for i in range(4):
        NV[i : i + 1, :] = jnp.sum(NG[i], axis=0, keepdims=True)
    copy = remote(NV.at[:, other_half], NR.at[0], ref.norm_s.at[0], ref.norm_r.at[0], dev_c)
    copy.start()
    pump(*LATE[12])
    copy.wait()
    NR[1] = NV[:, own_half] + NR[0]
    if fused:
        copy = remote(NR.at[1], NR.at[2], ref.norm_s.at[1], ref.norm_r.at[1], dev_x)
        copy.start()
        pump(*LATE[13])
        copy.wait()
        NR[3] = NR[1] + NR[2]
        copy = remote(NR.at[3], NR.at[4], ref.norm_s.at[2], ref.norm_r.at[2], dev_y)
        copy.start()
        pump(*LATE[14])
        copy.wait()
        NZS[mz] = NR[3] + NR[4]
        copies = [
            remote(NZS.at[mz], NZS.at[mz], ref.norm_s.at[2 + j], ref.norm_r.at[2 + j], dev_z[j - 1])
            for j in range(1, nz)
        ]
        for copy in copies:
            copy.start()
    pump(*LATE[15])
    if fused:
        for copy in copies:
            copy.wait()
        total = NZS[0]
        for j in range(1, nz):
            total = total + NZS[j]
        ref.o_norm[...] = total
        for k in range(blocks + 5 - FINALS, blocks + 5):
            for part in range(2):
                fin_copy(late_chunk(k - blocks) if k >= blocks else chunk(jnp.int32(k)), part).wait()
    else:
        pump((4, 1))
        ref.o_norm[...] = NR[1]
    blk_local.wait()
    blk_cross.wait()
    tok_local.wait()
    tok_cross.wait()


def unpack_kernel(sh, blocks, half, count, names, *all_refs):
    ref = SimpleNamespace(**dict(zip(names, all_refs)))
    step = ref.tok_in.shape[0] // count
    loads, saves = [], []

    def save(src, dst):
        copy = pltpu.make_async_copy(src, dst, ref.save_sem.at[len(saves)])
        copy.start()
        saves.append(copy)

    def load(src, dst):
        copy = pltpu.make_async_copy(src, dst, ref.load_sem.at[len(loads)])
        copy.start()
        loads.append(copy)
        return copy

    parts = [slice(i * step, (i + 1) * step) for i in range(count)]
    load_t = [load(ref.o_tok.at[parts[0], :], ref.tok_in.at[parts[0], :])]
    load_f = load(ref.o_fin, ref.fin)
    load_n = load(ref.o_norm, ref.norm)
    rows_b = [slice(i * step * count // 2, (i + 1) * step * count // 2) for i in range(2)]
    load_b = [load(ref.o_blk.at[rows, :], ref.blk.at[rows, :]) for rows in rows_b]
    load_t += [load(ref.o_tok.at[rows, :], ref.tok_in.at[rows, :]) for rows in parts[1:]]

    def widen(i):
        load_t[i].wait()
        ref.tok_out[parts[i], :] = ref.tok_in[parts[i], :].astype(f32)
        save(ref.tok_out.at[parts[i], :], ref.r_tok.at[parts[i], :])

    widen(0)
    load_f.wait()
    fin = ref.fin
    for k in range(blocks):
        cols = slice(k * COLS, (k + 1) * COLS)
        ref.up[:, cols] = fin[k, 0, 0:sh, :]
        ref.dn[:, cols] = fin[k, 1, 0:sh, :]
    save(ref.up, ref.r_up)
    save(ref.dn, ref.r_dn)
    low, high = fin[blocks + 2, 0], fin[blocks + 2, 1]
    first = lax.axis_index("chan") == 0
    ref.pair[:, 0:COLS] = jnp.where(first, low, high)
    ref.pair[:, COLS : 2 * COLS] = jnp.where(first, high, low)
    save(ref.pair, ref.r_pair)
    for i, (late, target) in enumerate(((0, ref.r_wo), (1, ref.r_q), (3, ref.r_k), (4, ref.r_v))):
        at = 0
        for part, width in enumerate(widths_of(half, i)):
            ref.square[i, :, at : at + width] = fin[blocks + late, part, 0:sh, 0:width]
            at += width
        save(ref.square.at[i], target)
    load_n.wait()
    for i, (vector, target) in enumerate(((ref.gi, ref.r_gi), (ref.si, ref.r_si), (ref.gm, ref.r_gm), (ref.sm, ref.r_sm))):
        vector[...] = ref.norm[i, :]
        save(vector, target)
    for copy, rows in zip(load_b, rows_b):
        copy.wait()
        save(ref.blk.at[rows, :], ref.r_blk.at[rows, :])
    for i in range(1, count):
        widen(i)
    for copy in saves:
        copy.wait()


def unpack(T, D, FH, sh, sp, out):
    half = D // 2
    blocks = FH // COLS
    count = 8
    inputs = dict(o_blk=out.o_blk, o_tok=out.o_tok, o_norm=out.o_norm, o_fin=out.o_fin)
    vector, square, wide = ((half,), f32), ((sh, half), f32), ((sh, FH), f32)
    results = dict(
        r_blk=((2 * T, half), bf16), r_tok=((2 * T, half), f32), r_gi=vector, r_si=vector, r_q=square, r_k=square,
        r_v=square, r_wo=square, r_gm=vector, r_sm=vector, r_up=wide, r_dn=wide, r_pair=((sp, T // 2), f32),
    )
    held = pltpu.VMEM((half,), f32)
    scratch = dict(
        blk=pltpu.VMEM((2 * T, half), bf16), tok_in=pltpu.VMEM((2 * T, half), bf16),
        tok_out=pltpu.VMEM((2 * T, half), f32), fin=pltpu.VMEM(out.o_fin.shape, f32),
        norm=pltpu.VMEM((8, half), f32), up=pltpu.VMEM((sh, FH), f32), dn=pltpu.VMEM((sh, FH), f32),
        pair=pltpu.VMEM((sp, T // 2), f32), square=pltpu.VMEM((4, sh, half), f32), gi=held, si=held, gm=held, sm=held,
        load_sem=pltpu.SemaphoreType.DMA((4 + count,)), save_sem=pltpu.SemaphoreType.DMA((len(results) + count,)),
    )
    values = pl.pallas_call(
        functools.partial(unpack_kernel, sh, blocks, half, count, tuple(inputs) + tuple(results) + tuple(scratch)),
        out_shape=tuple(jax.ShapeDtypeStruct(shape, kind) for shape, kind in results.values()),
        in_specs=[ANY] * len(inputs),
        out_specs=tuple(ANY for _ in results),
        scratch_shapes=list(scratch.values()),
        compiler_params=pltpu.CompilerParams(vmem_limit_bytes=63 << 20),
    )(*inputs.values())
    blk, tok, gi, si, q, k, v, wo, gm, sm, up, dn, pair = values
    return blk, tok, gi, si, q, k, v, wo.T, gm, sm, up, dn.T, pair


def gather_parts(T, D, out, pair_bias):
    half = D // 2
    parts = out.GO
    blocks = parts.shape[0] - 5
    join = lambda chosen: jnp.concatenate(chosen, 1).astype(f32)
    scatter = lambda v: lax.psum_scatter(v, "rows", scatter_dimension=0, tiled=True)
    up = scatter(join([parts[k, 0] for k in range(blocks)]))
    down = scatter(join([parts[k, 1] for k in range(blocks)])).T
    late = []
    for i in (0, 1, 3, 4):
        widths = widths_of(half, i if i < 2 else i - 1)
        late.append(scatter(join([parts[blocks + i, p, :, 0:width] for p, width in enumerate(widths)])))
    wo, q, k, v = late
    first = lax.axis_index("chan") == 0
    spread = []
    for p, rows in ((0, 2 * COLS), (1, 3 * COLS)):
        held, rest = parts[blocks + 2, p, 0:rows], jnp.zeros((T - rows, COLS), bf16)
        spread.append(jnp.where(first, jnp.concatenate([held, rest]), jnp.concatenate([rest, held])))
    low, high = spread
    pair = scatter(join([jnp.where(first, low, high), jnp.where(first, high, low)]))
    bias = lax.dynamic_slice(
        pair_bias, (lax.axis_index("rows") * pair.shape[0], lax.axis_index("chan") * (T // 2)), pair.shape
    )
    norms = lax.psum(out.o_norm, "rows")
    return (
        out.o_blk, out.o_tok.astype(f32), norms[0], norms[1], q, k, v, wo.T, norms[2], norms[3], up, down,
        pair * jnp.exp(bias),
    )


def on_device(
    tokens, segments, gain_in, shift_in, query_weight, key_weight, value_weight, out_weight,
    gain_mid, shift_mid, up_weight, down_weight, pair_bias, out_grad,
):
    T = segments.shape[1]
    D, FH = up_weight.shape
    R = lax.axis_size("rows")
    half = D // 2
    blocks = FH // COLS
    fused = R == 16 and D % (16 * R) == 0 and T % (16 * R) == 0
    nb = R if fused else 16
    nz = nb // 4
    sh, sp = D // nb, T // nb
    inputs = dict(
        tokens=tokens, segments=segments, gi=gain_in, si=shift_in, wq=query_weight, wk=key_weight, wv=value_weight,
        wo=out_weight, gm=gain_mid, sm=shift_mid, wu=up_weight, wd=down_weight, pair_bias=pair_bias,
        out_grad=out_grad,
    )
    near = ("segments", "gi", "si", "gm", "sm")
    outputs = dict(
        o_blk=(ANY, (2 * T, half), bf16), o_tok=(ANY, (2 * T, half), bf16), o_norm=(VMEM, (8, half), f32)
    )
    if fused:
        outputs |= dict(o_fin=(ANY, (blocks + 5, 2, sp, COLS), f32))
    else:
        outputs |= dict(GO=(ANY, (blocks + 5, 2, D, COLS), bf16))
    square, act, total = pltpu.VMEM((D, D), bf16), pltpu.VMEM((T, D), bf16), pltpu.VMEM((T, D), f32)
    small, halves = pltpu.VMEM((8, TILE), f32), pltpu.VMEM((8, half), f32)
    sems = pltpu.SemaphoreType.DMA
    scratch = dict(
        XB=act, OG=act, HN=act, G=act, Y=act, QQ=act, RT=act, RZ=act, T2=act,
        AB=pltpu.VMEM((T, 2 * D), bf16), MM=pltpu.VMEM((T, T), bf16), F1=total, F3=total,
        ST=pltpu.VMEM((T, TILE), f32), WQ=square, WK=square, WV=square, WO=square,
        WU=pltpu.VMEM((2 * D, FH), bf16), WD=pltpu.VMEM((2 * FH, D), bf16),
        SD=pltpu.VMEM((T, 4 * COLS), bf16), SC=pltpu.VMEM((T, TILE), bf16),
        NP=pltpu.VMEM((8, D), f32), NPS=halves, NPR=halves,
        PS=pltpu.VMEM((2, 2, D, COLS), bf16), PR=pltpu.VMEM((2, 2, D, COLS), bf16),
        S=pltpu.VMEM((SLOTS, 2, D, COLS), bf16),
        RX=pltpu.VMEM((SLOTS, 2, D, COLS), bf16) if fused else small,
        FIN=pltpu.VMEM((FINALS, 2, sp, COLS), f32) if fused else small,
        NG=pltpu.VMEM((4, 8, D), f32), NV=pltpu.VMEM((8, D), f32), NR=pltpu.VMEM((5, 8, half), f32),
        NZS=pltpu.VMEM((nz, 8, half), f32), PBO=pltpu.VMEM((sp, T // 2), f32),
        local_sem=sems((16,)), entry_s=sems((16,)), entry_r=sems((16,)), end_l=sems((2,)), end_s=sems((2,)),
        end_r=sems((2,)), up_l=sems((blocks,)), up_s=sems((blocks,)), up_r=sems((blocks,)),
        down_l=sems((blocks,)), down_s=sems((blocks,)), down_r=sems((blocks,)),
        pair_s=sems((2, 5)), pair_r=sems((2, 5)), ring_s=sems((SLOTS, 2, 6)), ring_r=sems((SLOTS, 2, 6)),
        norm_s=sems((2 + nz,)), norm_r=sems((2 + nz,)), fin_sem=sems((blocks + 5, 2)),
    )
    results = pl.pallas_call(
        functools.partial(
            block_kernel, T, D, FH, R, fused, tuple(inputs) + tuple(outputs) + tuple(scratch)
        ),
        out_shape=tuple(jax.ShapeDtypeStruct(shape, kind) for _, shape, kind in outputs.values()),
        in_specs=[VMEM if name in near else ANY for name in inputs],
        out_specs=tuple(spec for spec, _, _ in outputs.values()),
        scratch_shapes=list(scratch.values()),
        compiler_params=pltpu.CompilerParams(
            collective_id=0, has_side_effects=True, vmem_limit_bytes=63 << 20
        ),
    )(*inputs.values())
    out = SimpleNamespace(**dict(zip(outputs, results)))
    if fused:
        return unpack(T, D, FH, sh, sp, out)
    return gather_parts(T, D, out, pair_bias)


def solution(mesh):
    split, first, second, vector = P("rows", "chan"), P("chan", None), P(None, "chan"), P("chan")
    return jax.shard_map(
        on_device,
        mesh=mesh,
        in_specs=(
            split, P("rows", None), vector, vector, second, second, second, first, vector, vector, second, first,
            P(), split,
        ),
        out_specs=(
            split, split, vector, vector, split, split, split, P("chan", "rows"), vector, vector, split,
            P("chan", "rows"), split,
        ),
        check_vma=False,
    )
```
